256 devices in a mesh: sec: 32 (over x, z), term: 8 (over y, core).
Axes of the slice: x: 4, y: 4, z: 8, core: 2. Of those that a mesh axis runs over, the one named last changes fastest.
Arguments:
- psi: bfloat16 [256, 384, 384], P('sec'), may hold values from -1.5 to 1.5
- left_ops: bfloat16 [16, 256, 384, 384], P('term', 'sec'), may hold values from -0.3125 to 0.3125
- right_ops: bfloat16 [16, 256, 384, 384], P('term', 'sec'), may hold values from -0.3125 to 0.3125
- pair_src: int32 [16, 256], P('term'), may hold values from 0 to 255, each once within a row
- widths: int32 [2, 256], P(None, 'sec'), may hold values from 64 to 384, as said below
Outputs:
- sigma: float32 [256, 384, 384], P('sec', None, 'term')
The draws below stay inside these ranges and needn't reach their ends.
Inputs may be any that keep to these rules, and one draw needn't show every extreme that they name: Each entry lies between 64 and 384; in every draw all sectors of some one index of sec have both widths equal to 384. `pair_src`: each row is a permutation of the 256 sectors.
All inputs are finite; a program needn't handle non-finite values.
Results may differ from the reference program's by a relative error of at most 0.015.
Values may be sent and summed in bfloat16 or wider, within the bound.
A program may use at most 64 MiB of HBM per device.

```python
import jax
import jax.numpy as jnp
from jax import lax

M = 384
S_DEV = 8
G_DEV = 2
SECTORS = 256
TERMS = 16
N_SEC = 32
N_TERM = 8


def draw_widths(key, part):
    key = jax.random.fold_in(key, 5)
    first, second = jax.random.split(key)
    drawn = jax.random.randint(first, (2, SECTORS), M // 6, M + 1, dtype=jnp.int32)
    chosen = jax.random.randint(second, (), 0, N_SEC, dtype=jnp.int32)
    owner = jnp.arange(SECTORS, dtype=jnp.int32) // S_DEV
    return jnp.where((owner == chosen)[None, :], jnp.int32(M), drawn)


def steps_of(key, dims, shards, smallest, top_value):
    def one(dim, blocks):
        heights = jax.random.uniform(jax.random.fold_in(jax.random.fold_in(key, 6), dim), (blocks,), jnp.float32, smallest / len(shards), top_value / len(shards))
        return jnp.repeat(jnp.exp(heights), dims[dim] // blocks).reshape((-1,) + (1,) * (len(dims) - dim - 1))

    factor_of = one(*shards[0])
    for cut in shards[1:]:
        factor_of = factor_of * one(*cut)
    return factor_of


def normal_values(rng, extent, width, most, shards=(), held_as=jnp.bfloat16):
    values = jax.random.normal(rng, extent, jnp.float32) * width
    if len(shards) > 0:
        values = steps_of(rng, extent, shards, -0.22, 0.18) * values
    return jnp.clip(values, min=-most, max=most).astype(held_as)


def setup_inputs(seed: int = 0) -> dict:
    arg_keys = jax.random.split(jax.random.key(seed), 6)
    psi = normal_values(arg_keys[0], (SECTORS, M, M), 0.25, 1.5, ((0, 32),))
    left_ops = normal_values(arg_keys[1], (TERMS, SECTORS, M, M), M ** -0.5, 0.3125, ((0, 8), (1, 32)))
    right_ops = normal_values(arg_keys[2], (TERMS, SECTORS, M, M), M ** -0.5, 0.3125, ((0, 8), (1, 32)))
    pair_src = jax.vmap(lambda own: jax.random.permutation(own, SECTORS))(jax.random.split(arg_keys[3], TERMS)).reshape((TERMS, SECTORS)).astype(jnp.int32)
    widths = draw_widths(jax.random.fold_in(arg_keys[5], 71), 0)
    return dict(psi=psi, left_ops=left_ops, right_ops=right_ops, pair_src=pair_src, widths=widths)


def block_mask(widths, size):
    line = jnp.arange(size, dtype=jnp.int32)
    return (line[None, :, None] < widths[0][:, None, None]) & (line[None, None, :] < widths[1][:, None, None])


def reference(psi, left_ops, right_ops, pair_src, widths):
    size = psi.shape[1]
    keep = block_mask(widths, size)
    masked = jnp.where(keep, psi, jnp.zeros_like(psi))

    def window_sum(window, total):
        acc = jnp.zeros(psi.shape, jnp.float32)
        for inner in range(G_DEV):
            group = (window * G_DEV + inner).astype(jnp.int32)
            lop = lax.dynamic_index_in_dim(left_ops, group, 0, keepdims=False)
            rop = lax.dynamic_index_in_dim(right_ops, group, 0, keepdims=False)
            order = lax.dynamic_index_in_dim(pair_src, group, 0, keepdims=False)
            half = jnp.einsum("kij,kjl->kil", lop.astype(jnp.float32), masked.astype(jnp.float32)).astype(jnp.bfloat16)
            half = lax.optimization_barrier(half)
            image = jnp.einsum("kil,kml->kim", half.astype(jnp.float32), rop.astype(jnp.float32)).astype(jnp.bfloat16)
            image = lax.optimization_barrier(image)
            acc = acc + jnp.take(image, order, axis=0).astype(jnp.float32)
        part = lax.optimization_barrier(acc.astype(jnp.bfloat16))
        return total + part.astype(jnp.float32)

    total = lax.fori_loop(0, N_TERM, window_sum, jnp.zeros(psi.shape, jnp.float32))
    return jnp.where(keep, total, jnp.zeros_like(total))
```

```python
import functools

import jax
import jax.numpy as jnp
from jax import lax
from jax.experimental import pallas as pl
from jax.experimental.pallas import tpu as pltpu
from jax.sharding import PartitionSpec as P

NX, NY, NZ, NC = 4, 4, 8, 2
PIECES = 3
HALVES = 2
SLOTS = NX * NY
SECTORS_HERE = 8
PER_HALF = SECTORS_HERE // HALVES
X_PART = NX // NC
STEPS = NZ // 2
EMPTY = SLOTS * SECTORS_HERE
MESH = pl.DeviceIdType.MESH


def device(x, y, z, c):
    return (x * NZ + z, y * NC + c)


def rows_of(ref, index, start, count):
    low = start // 16 * 16
    high = min(-(-(start + count) // 16) * 16, ref.shape[-2])
    value = ref[index + (slice(low, high), slice(None))].astype(jnp.float32)
    return value[start - low : start - low + count]


def kernel(
    slot_in, widths, psi, left, right, out,
    psi_v, left_v, right_v, sends, got0, got1, got2, slot_v, slot_s,
    give, take, own, up_out, up_in, down_out, down_in, done, final,
    load_sem, slot_sem, slot_send, spread_send, spread_recv, core_send, core_recv,
    up_send, up_recv, down_send, down_recv, final_send, final_recv,
):
    got = (got0, got1, got2)[:PIECES]
    sec, term = lax.axis_index("sec"), lax.axis_index("term")
    x, z = lax.div(sec, NZ), lax.rem(sec, NZ)
    y, c = lax.div(term, NC), lax.rem(term, NC)
    me = y * NX + x
    size = psi_v.shape[-1]
    rows = size // SLOTS
    lanes = size // PIECES
    moves = [(dx, dy) for dx in range(NX) for dy in range(NY) if (dx, dy) != (0, 0)]
    moves.sort(key=lambda m: -(min(m[0], NX - m[0]) + min(m[1], NY - m[1])))

    def shifted(value, by, count):
        return lax.rem(value + (by % count), count)

    barrier = pltpu.get_barrier_semaphore()
    others = [device(shifted(x, dx, NX), shifted(y, dy, NY), z, c) for dx, dy in moves]
    others += [device(shifted(x, dx, NX), y, z, 1 - c) for dx in range(NX)]
    others += [device(x, y, shifted(z, 1, NZ), c), device(x, y, shifted(z, -1, NZ), c)]
    for other in others:
        pl.semaphore_signal(barrier, inc=1, device_id=other, device_id_type=MESH)

    def loads(k):
        return (
            pltpu.make_async_copy(psi.at[k], psi_v.at[k], load_sem.at[0, k]),
            pltpu.make_async_copy(right.at[:, k], right_v.at[:, k], load_sem.at[1, k]),
            pltpu.make_async_copy(left.at[:, k], left_v.at[:, k], load_sem.at[2, k]),
        )

    for k in range(SECTORS_HERE):
        for copy in loads(k):
            copy.start()
    for piece in range(PIECES):
        got[piece][EMPTY] = jnp.zeros(got[piece].shape[1:], got[piece].dtype)

    def images(piece, half):
        def one(inner, _):
            k = half * PER_HALF + inner
            if piece == 0:
                for copy in loads(k):
                    copy.wait()
                keep = (lax.broadcasted_iota(jnp.int32, (size, size), 0) < widths[0, k]) & (
                    lax.broadcasted_iota(jnp.int32, (size, size), 1) < widths[1, k]
                )
                psi_v[k] = jnp.where(keep, psi_v[k].astype(jnp.float32), 0.0).astype(jnp.bfloat16)
            block = []
            for group in range(2):
                part = jnp.dot(
                    left_v[group, k, piece * lanes : (piece + 1) * lanes, :],
                    psi_v[k],
                    preferred_element_type=jnp.float32,
                ).astype(jnp.bfloat16)
                block.append(
                    lax.dot_general(
                        right_v[group, k], part, (((1,), (1,)), ((), ())),
                        preferred_element_type=jnp.float32,
                    )
                )
            for slot in range(SLOTS):
                at = slice(slot * rows, (slot + 1) * rows)
                sends[piece, slot, k] = jnp.concatenate([block[0][at], block[1][at]], 0).astype(
                    jnp.bfloat16
                )
            return 0

        lax.fori_loop(0, PER_HALF, one, 0)

    def spread(piece, half):
        first = half * PER_HALF
        place = pl.ds(half * (SLOTS * PER_HALF) + me * PER_HALF, PER_HALF)
        for dx, dy in moves:
            xd, yd = shifted(x, dx, NX), shifted(y, dy, NY)
            pltpu.make_async_remote_copy(
                src_ref=sends.at[piece, yd * NX + xd, first : first + PER_HALF],
                dst_ref=got[piece].at[place],
                send_sem=spread_send.at[piece],
                recv_sem=spread_recv.at[piece],
                device_id=device(xd, yd, z, c),
                device_id_type=MESH,
            ).start()
        pltpu.make_async_copy(
            sends.at[piece, me, first : first + PER_HALF], got[piece].at[place], spread_recv.at[piece]
        ).start()

    def slot_copy(dy):
        return pltpu.make_async_remote_copy(
            src_ref=slot_in,
            dst_ref=slot_v.at[y],
            send_sem=slot_send.at[dy],
            recv_sem=slot_sem.at[0],
            device_id=device(x, shifted(y, dy, NY), z, c),
            device_id_type=MESH,
        )

    def gather(piece, part, to):
        first = part * (to.shape[1] * 2)

        def pair(p, _):
            both = []
            for which in range(2):
                total = jnp.zeros((rows, lanes), jnp.float32)
                for yy in range(NY):
                    for group in range(2):
                        slot = slot_s[yy, group, first + 2 * p + which]
                        total = total + rows_of(got[piece], (slot,), group * rows, rows)
                both.append(total)
            to[piece, p] = jnp.concatenate(both, 0).astype(to.dtype)
            return 0

        lax.fori_loop(0, to.shape[1], pair, 0)

    def core_copy(piece):
        return pltpu.make_async_remote_copy(
            src_ref=give.at[piece],
            dst_ref=take.at[piece],
            send_sem=core_send.at[piece],
            recv_sem=core_recv.at[piece],
            device_id=device(x, y, z, 1 - c),
            device_id_type=MESH,
        )

    def held(piece, part, zd):
        at = pl.ds(part * (NZ * PER_HALF) + zd * PER_HALF, PER_HALF)
        return own[piece, at] + take[piece, at].astype(jnp.float32)

    def z_copy(piece, step, way):
        source, target = (up_out, up_in) if way > 0 else (down_out, down_in)
        out_sem, in_sem = (up_send, up_recv) if way > 0 else (down_send, down_recv)
        at = (piece, step) if step > 0 else (piece, step, 0 if way > 0 else 1)
        return pltpu.make_async_remote_copy(
            src_ref=source.at[at],
            dst_ref=target.at[at],
            send_sem=out_sem.at[piece, step],
            recv_sem=in_sem.at[piece, step],
            device_id=device(x, y, shifted(z, way, NZ), c),
            device_id_type=MESH,
        )

    def parts_at(step, way):
        return range(X_PART) if step > 0 else ((0,) if way > 0 else (1,))

    def chain(piece):
        for step in range(STEPS):
            for way in (1, -1):
                source, target = (up_out, up_in) if way > 0 else (down_out, down_in)
                if step > 0:
                    z_copy(piece, step - 1, way).wait_recv()
                zd = shifted(z, way * (STEPS - step), NZ)
                for part in parts_at(step, way):
                    value = held(piece, part, zd)
                    if step > 0 and part in parts_at(step - 1, way):
                        value = value + target[piece, step - 1, part].astype(jnp.float32)
                    source[piece, step, part] = value.astype(jnp.bfloat16)
                z_copy(piece, step, way).start()

    def final_copies(piece, part):
        xd = c * X_PART + part
        place = final.at[piece, lax.rem(x, X_PART)]
        there = pltpu.make_async_remote_copy(
            src_ref=done.at[piece, part],
            dst_ref=place,
            send_sem=final_send.at[piece, part],
            recv_sem=final_recv.at[piece],
            device_id=device(xd, y, z, lax.div(x, X_PART)),
            device_id_type=MESH,
        )
        here = pltpu.make_async_copy(done.at[piece, part], place, final_recv.at[piece])
        return xd, there, here

    def finish(piece):
        last = STEPS - 1
        for way in (1, -1):
            z_copy(piece, last, way).wait_recv()
        for part in range(X_PART):
            value = held(piece, part, z)
            if part in parts_at(last, 1):
                value = value + up_in[piece, last, part].astype(jnp.float32)
            if part in parts_at(last, -1):
                value = value + down_in[piece, last, part].astype(jnp.float32)
            done[piece, part] = value.astype(jnp.bfloat16)
            xd, there, here = final_copies(piece, part)

            @pl.when(xd != x)
            def _():
                there.start()

            @pl.when(xd == x)
            def _():
                here.start()

    def reduce_piece(piece):
        pltpu.make_async_copy(
            got[piece].at[0:EMPTY], got[piece].at[0:EMPTY], spread_recv.at[piece]
        ).wait()
        gather(piece, 1 - c, give)
        core_copy(piece).start()
        gather(piece, c, own)
        core_copy(piece).wait_recv()
        chain(piece)
        finish(piece)

    images(0, 0)
    pl.semaphore_wait(barrier, len(others))
    for dy in range(1, NY):
        slot_copy(dy).start()
    pltpu.make_async_copy(slot_in, slot_v.at[y], slot_sem.at[0]).start()
    units = [(piece, half) for piece in range(PIECES) for half in range(HALVES)]
    for unit, following in zip(units, units[1:] + [None]):
        spread(*unit)
        if following is not None:
            images(*following)
    pltpu.make_async_copy(slot_v, slot_v, slot_sem.at[0]).wait()
    to_scalar = pltpu.make_async_copy(slot_v, slot_s, slot_sem.at[1])
    to_scalar.start()
    to_scalar.wait()
    for piece in range(PIECES):
        reduce_piece(piece)
    for piece in range(PIECES):
        pltpu.make_async_copy(final.at[piece], final.at[piece], final_recv.at[piece]).wait()
        for sector in range(SECTORS_HERE):
            for part in range(X_PART):
                out[
                    sector, part * rows : (part + 1) * rows, piece * lanes : (piece + 1) * lanes
                ] = rows_of(final, (piece, part, sector // 2), sector % 2 * rows, rows)

    for dy in range(1, NY):
        slot_copy(dy).wait_send()
    for piece in range(PIECES):
        sent = sends.at[piece, 0 : SLOTS - 1]
        pltpu.make_async_copy(sent, sent, spread_send.at[piece]).wait()
        core_copy(piece).wait_send()
        for step in range(STEPS):
            for way in (1, -1):
                z_copy(piece, step, way).wait_send()
        for part in range(X_PART):
            xd, there, _ = final_copies(piece, part)

            @pl.when(xd != x)
            def _():
                there.wait_send()


def shards(psi, left_ops, right_ops, pair_src, widths):
    size = psi.shape[1]
    targets = pair_src.shape[1]
    rows, lanes = size // SLOTS, size // PIECES
    sec, term = lax.axis_index("sec"), lax.axis_index("term")
    z, y = sec % NZ, term // NC
    here = pair_src // SECTORS_HERE % NZ == z
    x_from, inner = pair_src // (SECTORS_HERE * NZ), pair_src % SECTORS_HERE
    slot = (inner // PER_HALF) * (SLOTS * PER_HALF) + (y * NX + x_from) * PER_HALF + inner % PER_HALF
    slot = jnp.pad(jnp.where(here, slot, EMPTY).astype(jnp.int32), ((0, 6), (0, 0)))

    bf, block = jnp.bfloat16, (2 * rows, lanes)
    half_targets = targets // NC // 2
    ring = pltpu.VMEM((PIECES, STEPS, X_PART, PER_HALF) + block, bf)
    scratch = [
        pltpu.VMEM(psi.shape, bf),
        pltpu.VMEM(left_ops.shape, bf),
        pltpu.VMEM(right_ops.shape, bf),
        pltpu.VMEM((PIECES, SLOTS, SECTORS_HERE) + block, bf),
        *[pltpu.VMEM((EMPTY + 1,) + block, bf) for _ in range(3)],
        pltpu.VMEM((NY,) + slot.shape, jnp.int32),
        pltpu.SMEM((NY,) + slot.shape, jnp.int32),
        pltpu.VMEM((PIECES, half_targets) + block, bf),
        pltpu.VMEM((PIECES, half_targets) + block, bf),
        pltpu.VMEM((PIECES, half_targets) + block, jnp.float32),
        ring, ring, ring, ring,
        pltpu.VMEM((PIECES, X_PART, PER_HALF) + block, bf),
        pltpu.VMEM((PIECES, X_PART, PER_HALF) + block, bf),
    ]
    dma = pltpu.SemaphoreType.DMA
    scratch += [
        dma((3, SECTORS_HERE)), dma((2,)), dma((NY,)), dma((PIECES,)), dma((PIECES,)),
        dma((PIECES,)), dma((PIECES,)),
        dma((PIECES, STEPS)), dma((PIECES, STEPS)), dma((PIECES, STEPS)), dma((PIECES, STEPS)),
        dma((PIECES, X_PART)), dma((PIECES,)),
    ]
    summed = pl.pallas_call(
        kernel,
        out_shape=jax.ShapeDtypeStruct((SECTORS_HERE, X_PART * rows, size), jnp.float32),
        in_specs=[
            pl.BlockSpec(memory_space=pltpu.VMEM),
            pl.BlockSpec(memory_space=pltpu.SMEM),
            pl.BlockSpec(memory_space=pl.ANY),
            pl.BlockSpec(memory_space=pl.ANY),
            pl.BlockSpec(memory_space=pl.ANY),
        ],
        out_specs=pl.BlockSpec(memory_space=pltpu.VMEM),
        scratch_shapes=scratch,
        compiler_params=pltpu.CompilerParams(
            collective_id=0, has_side_effects=True, vmem_limit_bytes=56 * 1024 * 1024
        ),
        cost_estimate=pl.CostEstimate(
            flops=64 * size**3, bytes_accessed=40 * size * size * 2, transcendentals=0
        ),
    )(slot, widths, psi, left_ops, right_ops)

    summed = jnp.swapaxes(summed, 1, 2)
    line = jnp.arange(size, dtype=jnp.int32)
    columns = term * (X_PART * rows) + jnp.arange(X_PART * rows, dtype=jnp.int32)
    keep = (line[None, :, None] < widths[0][:, None, None]) & (
        columns[None, None, :] < widths[1][:, None, None]
    )
    return jnp.where(keep, summed, jnp.zeros_like(summed))


def solution(mesh):
    return jax.shard_map(
        shards,
        mesh=mesh,
        in_specs=(
            P("sec", None, None),
            P("term", "sec", None, None),
            P("term", "sec", None, None),
            P("term", None),
            P(None, "sec"),
        ),
        out_specs=P("sec", None, "term"),
        check_vma=False,
    )
```

```python
import jax
import jax.numpy as jnp
from jax import lax
from jax.experimental import pallas as pl
from jax.experimental.pallas import tpu as pltpu
from jax.sharding import PartitionSpec as P

NX, NY, NZ, NC = 4, 4, 8, 2
CHUNKS = 3
PIECES = ((0, 0, 3), (1, 0, 3), (2, 0, 2), (2, 2, 1))
SLOTS = NX * NY
GROUPS_HERE = 2
SECTORS_HERE = 8
TILE = GROUPS_HERE * SECTORS_HERE
SOURCES = SLOTS * TILE
X_PART = NX // NC
STEPS = NZ // 2
MESH = pl.DeviceIdType.MESH
BUFFERS = 11


def routes(sign):
    direct, relayed = [], []
    for dx in range(NX):
        for dy in range(NY):
            far_x, far_y = NX > 2 and dx == NX // 2, NY > 2 and dy == NY // 2
            if far_x or far_y:
                via = (sign if far_x else 0, sign if far_y else 0)
                relayed.append(((dx, dy), via, (dx - via[0], dy - via[1])))
            elif (dx, dy) != (0, 0):
                direct.append((dx, dy))
    return direct, relayed


RELAYS = len(routes(1)[1])


def device(x, y, z, c):
    return (x * NZ + z, y * NC + c)


def ones_where(condition):
    return jnp.where(condition, 1.0, 0.0).astype(jnp.bfloat16)


def tile_at(index):
    return pl.ds(pl.multiple_of(index * TILE, TILE), TILE)


def kernel(pair_src, widths, psi, left, right, out, *rest):
    psi_v, left_v, right_v, orders_own, orders, image, swap, pick, *rest = rest
    sends, rest = rest[:CHUNKS], rest[CHUNKS:]
    buffers = [rest[i * BUFFERS : (i + 1) * BUFFERS] for i in range(len(PIECES))]
    (
        load_sem, order_sem, order_send, spread_send, spread_recv, relay_recv, relay_send, core_send, core_recv,
        up_send, up_recv, down_send, down_recv, final_send, final_recv,
    ) = rest[len(PIECES) * BUFFERS :]
    got, relay, give, take, own, up_out, up_in, down_out, down_in, done, final = zip(*buffers)
    sec, term = lax.axis_index("sec"), lax.axis_index("term")
    x, z = lax.div(sec, NZ), lax.rem(sec, NZ)
    y, c = lax.div(term, NC), lax.rem(term, NC)
    size = psi_v.shape[-1]
    rows = size // SLOTS
    lanes = size // CHUNKS
    targets = pair_src.shape[1]
    pieces = range(len(PIECES))
    first_row = [rows * at // 3 for _, at, _ in PIECES]
    piece_rows = [rows * count // 3 for _, _, count in PIECES]

    def shifted(value, by, count):
        return lax.rem(value + (by % count), count)

    barrier = pltpu.get_barrier_semaphore()
    others = [
        device(shifted(x, dx, NX), shifted(y, dy, NY), z, c)
        for dx in range(NX)
        for dy in range(NY)
        if (dx, dy) != (0, 0)
    ]
    others += [device(shifted(x, dx, NX), y, z, 1 - c) for dx in range(NX)]
    others += [device(x, y, shifted(z, 1, NZ), c), device(x, y, shifted(z, -1, NZ), c)]
    for other in others:
        pl.semaphore_signal(barrier, inc=1, device_id=other, device_id_type=MESH)

    def loads(k):
        return (
            pltpu.make_async_copy(psi.at[k], psi_v.at[k], load_sem.at[0, k]),
            pltpu.make_async_copy(left.at[:, k], left_v.at[:, k], load_sem.at[1, k]),
            pltpu.make_async_copy(right.at[:, k], right_v.at[:, k], load_sem.at[2, k]),
        )

    for k in range(SECTORS_HERE):
        for copy in loads(k):
            copy.start()

    row = lax.broadcasted_iota(jnp.int32, swap.shape, 0)
    column = lax.broadcasted_iota(jnp.int32, swap.shape, 1)
    swap[...] = ones_where(row == (column & (TILE - 1)) * TILE + lax.shift_right_logical(column, 4))
    orders_own[...] = jnp.concatenate([pair_src[...], jnp.zeros((6, targets), jnp.int32)], 0)

    def images(chunk):
        def one(k, _):
            if chunk == 0:
                for copy in loads(k)[:2]:
                    copy.wait()
                keep = (lax.broadcasted_iota(jnp.int32, (size, size), 0) < widths[0, k]) & (
                    lax.broadcasted_iota(jnp.int32, (size, size), 1) < widths[1, k]
                )
                psi_v[k] = jnp.where(keep, psi_v[k].astype(jnp.float32), 0.0).astype(jnp.bfloat16)
            here = left_v[:, k, chunk * lanes : (chunk + 1) * lanes, :].reshape(2 * lanes, size)
            part = jnp.dot(here, psi_v[k], preferred_element_type=jnp.float32).astype(jnp.bfloat16)
            if chunk == 0:
                loads(k)[2].wait()
            for group in range(GROUPS_HERE):
                image[group * SECTORS_HERE + k] = lax.dot_general(
                    right_v[group, k],
                    part[group * lanes : (group + 1) * lanes],
                    (((1,), (1,)), ((), ())),
                    preferred_element_type=jnp.float32,
                ).astype(jnp.bfloat16)
            return 0

        lax.fori_loop(0, SECTORS_HERE, one, 0)

        def turn(step, _):
            for inner in range(2):
                low = step * (4 * TILE) + inner * (2 * TILE)
                both = [
                    image[:, pl.ds(pl.multiple_of(low + part * TILE, TILE), TILE), :].reshape(
                        TILE * TILE, lanes
                    )
                    for part in range(2)
                ]
                turned = jnp.dot(
                    swap[...], jnp.concatenate(both, 1), preferred_element_type=jnp.float32
                ).astype(jnp.bfloat16)
                for part in range(2):
                    sends[chunk][pl.ds(low + part * TILE, TILE)] = turned[
                        :, part * lanes : (part + 1) * lanes
                    ].reshape(TILE, TILE, lanes)
            return 0

        lax.fori_loop(0, size // (4 * TILE), turn, 0)

    def halves(piece):
        count = piece_rows[piece] // 2
        return ((0, 1, 0, count), (1, -1, count, count))

    def block_for(piece, x_to, y_to, low, count):
        start = (y_to * NX + x_to) * rows + first_row[piece] + low
        return sends[PIECES[piece][0]].at[pl.ds(start, count)]

    def place(piece, x_from, y_from, low, count):
        return got[piece].at[low : low + count, tile_at(y_from * NX + x_from)]

    def spread(piece):
        for half, sign, low, count in halves(piece):
            for j, ((dx, dy), (vx, vy), _) in enumerate(routes(sign)[1]):
                pltpu.make_async_remote_copy(
                    src_ref=block_for(piece, shifted(x, dx, NX), shifted(y, dy, NY), low, count),
                    dst_ref=relay[piece].at[half, j],
                    send_sem=spread_send.at[piece],
                    recv_sem=relay_recv.at[piece, half],
                    device_id=device(shifted(x, vx, NX), shifted(y, vy, NY), z, c),
                    device_id_type=MESH,
                ).start()
        count = piece_rows[piece]
        for dx, dy in routes(1)[0]:
            xd, yd = shifted(x, dx, NX), shifted(y, dy, NY)
            pltpu.make_async_remote_copy(
                src_ref=block_for(piece, xd, yd, 0, count),
                dst_ref=place(piece, x, y, 0, count),
                send_sem=spread_send.at[piece],
                recv_sem=spread_recv.at[piece],
                device_id=device(xd, yd, z, c),
                device_id_type=MESH,
            ).start()
        pltpu.make_async_copy(
            block_for(piece, x, y, 0, count), place(piece, x, y, 0, count), spread_recv.at[piece]
        ).start()

    def forward(piece):
        if RELAYS == 0:
            return
        for half, sign, low, count in halves(piece):
            arrived = relay[piece].at[half]
            pltpu.make_async_copy(arrived, arrived, relay_recv.at[piece, half]).wait()
            for j, (_, (vx, vy), (fx, fy)) in enumerate(routes(sign)[1]):
                pltpu.make_async_remote_copy(
                    src_ref=relay[piece].at[half, j],
                    dst_ref=place(piece, shifted(x, -vx, NX), shifted(y, -vy, NY), low, count),
                    send_sem=relay_send.at[piece],
                    recv_sem=spread_recv.at[piece],
                    device_id=device(shifted(x, fx, NX), shifted(y, fy, NY), z, c),
                    device_id_type=MESH,
                ).start()

    def order_copy(dy):
        return pltpu.make_async_remote_copy(
            src_ref=orders_own,
            dst_ref=orders.at[y],
            send_sem=order_send.at[dy],
            recv_sem=order_sem.at[0],
            device_id=device(x, shifted(y, dy, NY), z, c),
            device_id_type=MESH,
        )

    def make_pick():
        pltpu.make_async_copy(orders, orders, order_sem.at[0]).wait()
        line = lax.broadcasted_iota(jnp.int32, (SECTORS_HERE, targets), 0)
        blocks = []
        for yy in range(NY):
            for xx in range(NX):
                for group in range(GROUPS_HERE):
                    wanted = orders[yy, group : group + 1, :]
                    first = (xx * NZ + z) * SECTORS_HERE
                    blocks.append(jnp.where(wanted == line + first, 1.0, 0.0))
        table = jnp.concatenate(blocks, 0).T
        blocks = []
        for xh in range(NC):
            for zz in range(NZ):
                for part in range(X_PART):
                    low = ((xh * X_PART + part) * NZ + zz) * SECTORS_HERE
                    blocks.append(table[low : low + SECTORS_HERE])
        pick[...] = jnp.concatenate(blocks, 0).astype(jnp.bfloat16)

    def gather(piece, part, to):
        half = targets // NC
        chosen = pick[pl.ds(pl.multiple_of(part * half, half), half), :]

        def some(step, _):
            for inner in range(2):
                m = step * 4 + inner * 2
                both = jnp.concatenate([got[piece][m], got[piece][m + 1]], 1)
                value = jnp.dot(chosen, both, preferred_element_type=jnp.float32).astype(to.dtype)
                for zz in range(NZ):
                    for next_m in range(2):
                        to[zz, m + next_m] = value[
                            zz * TILE : (zz + 1) * TILE, next_m * lanes : (next_m + 1) * lanes
                        ]
            return 0

        lax.fori_loop(0, piece_rows[piece] // 4, some, 0)

    def core_copy(piece):
        return pltpu.make_async_remote_copy(
            src_ref=give[piece],
            dst_ref=take[piece],
            send_sem=core_send.at[piece],
            recv_sem=core_recv.at[piece],
            device_id=device(x, y, z, 1 - c),
            device_id_type=MESH,
        )

    def give_half(piece):
        pltpu.make_async_copy(got[piece], got[piece], spread_recv.at[piece]).wait()
        gather(piece, 1 - c, give[piece])
        core_copy(piece).start()

    def keep_half(piece):
        gather(piece, c, own[piece])

    def held(piece, zd, low, count):
        at = slice(low, low + count)
        return own[piece][zd, at] + take[piece][zd, at].astype(jnp.float32)

    def z_buffers(piece, way):
        return (up_out[piece], up_in[piece]) if way > 0 else (down_out[piece], down_in[piece])

    def z_copy(piece, step, way):
        source, target = z_buffers(piece, way)
        out_sem, in_sem = (up_send, up_recv) if way > 0 else (down_send, down_recv)
        at = (step,)
        if step == 0:
            _, _, low, count = halves(piece)[0 if way > 0 else 1]
            at = (step, slice(low, low + count))
        return pltpu.make_async_remote_copy(
            src_ref=source.at[at],
            dst_ref=target.at[at],
            send_sem=out_sem.at[piece, step],
            recv_sem=in_sem.at[piece, step],
            device_id=device(x, y, shifted(z, way, NZ), c),
            device_id_type=MESH,
        )

    def carried(step, way, sign):
        return step > 0 or way == sign

    def chain(piece, step):
        if step >= STEPS:
            return
        if step == 0:
            core_copy(piece).wait_recv()
        for way in (1, -1):
            source, target = z_buffers(piece, way)
            if step > 0:
                z_copy(piece, step - 1, way).wait_recv()
            zd = shifted(z, way * (STEPS - step), NZ)
            for _, sign, low, count in halves(piece):
                if carried(step, way, sign):
                    at = slice(low, low + count)
                    value = held(piece, zd, low, count)
                    if step > 0 and carried(step - 1, way, sign):
                        value = value + target[step - 1, at].astype(jnp.float32)
                    source[step, at] = value.astype(jnp.bfloat16)
            z_copy(piece, step, way).start()

    def final_copies(piece, part):
        xd = c * X_PART + part
        spot_there = final[piece].at[lax.rem(x, X_PART)]
        there = dict(
            src_ref=done[piece].at[part],
            dst_ref=spot_there,
            send_sem=final_send.at[piece, part],
            recv_sem=final_recv.at[piece],
            device_id=device(xd, y, z, lax.div(x, X_PART)),
            device_id_type=MESH,
        )
        here = (done[piece].at[part], spot_there, final_recv.at[piece])
        return xd, there, here

    def finish(piece):
        last = STEPS - 1
        for way in (1, -1):
            z_copy(piece, last, way).wait_recv()
        for _, sign, low, count in halves(piece):
            value = held(piece, z, low, count)
            for way in (1, -1):
                if carried(last, way, sign):
                    value = value + z_buffers(piece, way)[1][last, low : low + count].astype(jnp.float32)
            for part in range(X_PART):
                at = slice(part * SECTORS_HERE, (part + 1) * SECTORS_HERE)
                done[piece][part, low // 2 : (low + count) // 2] = (
                    value[:, at, :].reshape(count // 2, TILE, lanes).astype(jnp.bfloat16)
                )
        for part in range(X_PART):
            xd, there, here = final_copies(piece, part)

            @pl.when(xd != x)
            def _():
                pltpu.make_async_remote_copy(**there).start()

            @pl.when(xd == x)
            def _():
                pltpu.make_async_copy(*here).start()

    def put(piece):
        pltpu.make_async_copy(final[piece], final[piece], final_recv.at[piece]).wait()
        chunk, count = PIECES[piece][0], piece_rows[piece]
        total = X_PART * count * SECTORS_HERE
        row = lax.broadcasted_iota(jnp.int32, (total, total), 0)
        column = lax.broadcasted_iota(jnp.int32, (total, total), 1)
        sector = column & (SECTORS_HERE - 1)
        line = lax.shift_right_logical(column, 3)
        value = jnp.dot(
            ones_where(row == sector * (X_PART * count) + line),
            final[piece][...].reshape(total, lanes),
            preferred_element_type=jnp.float32,
        )
        for sector in range(SECTORS_HERE):
            for part in range(X_PART):
                low = part * rows + first_row[piece]
                start = (sector * X_PART + part) * count
                out[sector, low : low + count, chunk * lanes : (chunk + 1) * lanes] = value[
                    start : start + count
                ]

    images(0)
    pl.semaphore_wait(barrier, len(others))
    spread(0)
    for dy in range(1, NY):
        order_copy(dy).start()
    pltpu.make_async_copy(orders_own, orders.at[y], order_sem.at[0]).start()
    images(1)
    forward(0)
    spread(1)
    make_pick()
    images(2)
    give_half(0)
    keep_half(0)
    chain(0, 0)
    forward(1)
    spread(2)
    chain(0, 1)
    chain(0, 2)
    spread(3)
    chain(0, 3)
    finish(0)
    give_half(1)
    keep_half(1)
    chain(1, 0)
    forward(2)
    put(0)
    chain(1, 1)
    forward(3)
    chain(1, 2)
    chain(1, 3)
    finish(1)
    give_half(2)
    keep_half(2)
    chain(2, 0)
    give_half(3)
    chain(2, 1)
    keep_half(3)
    chain(3, 0)
    put(1)
    chain(2, 2)
    chain(3, 1)
    chain(2, 3)
    chain(3, 2)
    finish(2)
    chain(3, 3)
    put(2)
    finish(3)
    put(3)

    for dy in range(1, NY):
        order_copy(dy).wait_send()
    for piece in pieces:
        sent = sends[PIECES[piece][0]].at[0 : (SLOTS - 1) * piece_rows[piece]]
        pltpu.make_async_copy(sent, sent, spread_send.at[piece]).wait()
        if RELAYS:
            pltpu.make_async_copy(relay[piece], relay[piece], relay_send.at[piece]).wait()
        core_copy(piece).wait_send()
        for step in range(STEPS):
            for way in (1, -1):
                z_copy(piece, step, way).wait_send()
        for part in range(X_PART):
            xd, there, _ = final_copies(piece, part)

            @pl.when(xd != x)
            def _():
                pltpu.make_async_remote_copy(**there).wait_send()


def shards(psi, left_ops, right_ops, pair_src, widths):
    size = psi.shape[1]
    targets = pair_src.shape[1]
    rows, lanes = size // SLOTS, size // CHUNKS
    term = lax.axis_index("term")
    bf, count = jnp.bfloat16, len(PIECES)
    tile = (TILE, lanes)
    scratch = [
        pltpu.VMEM(psi.shape, bf),
        pltpu.VMEM(left_ops.shape, bf),
        pltpu.VMEM(right_ops.shape, bf),
        pltpu.VMEM((8, targets), jnp.int32),
        pltpu.VMEM((NY, 8, targets), jnp.int32),
        pltpu.VMEM((TILE, size, lanes), bf),
        pltpu.VMEM((TILE * TILE, TILE * TILE), bf),
        pltpu.VMEM((targets, SOURCES), bf),
        *[pltpu.VMEM((size,) + tile, bf) for _ in range(CHUNKS)],
    ]
    for _, _, thirds in PIECES:
        here = rows * thirds // 3
        ring = pltpu.VMEM((STEPS, here) + tile, bf)
        scratch += [
            pltpu.VMEM((here, SOURCES, lanes), bf),
            pltpu.VMEM((2, max(RELAYS, 1), here // 2) + tile, bf),
            pltpu.VMEM((NZ, here) + tile, bf),
            pltpu.VMEM((NZ, here) + tile, bf),
            pltpu.VMEM((NZ, here) + tile, jnp.float32),
            ring, ring, ring, ring,
            pltpu.VMEM((X_PART, here // 2) + tile, bf),
            pltpu.VMEM((X_PART, here // 2) + tile, bf),
        ]
    dma = pltpu.SemaphoreType.DMA
    scratch += [
        dma((3, SECTORS_HERE)), dma((1,)), dma((NY,)), dma((count,)), dma((count,)),
        dma((count, 2)), dma((count,)), dma((count,)), dma((count,)),
        dma((count, STEPS)), dma((count, STEPS)), dma((count, STEPS)), dma((count, STEPS)),
        dma((count, X_PART)), dma((count,)),
    ]
    summed = pl.pallas_call(
        kernel,
        out_shape=jax.ShapeDtypeStruct((SECTORS_HERE, X_PART * rows, size), jnp.float32),
        in_specs=[
            pl.BlockSpec(memory_space=pltpu.VMEM),
            pl.BlockSpec(memory_space=pltpu.SMEM),
            pl.BlockSpec(memory_space=pl.ANY),
            pl.BlockSpec(memory_space=pl.ANY),
            pl.BlockSpec(memory_space=pl.ANY),
        ],
        out_specs=pl.BlockSpec(memory_space=pltpu.VMEM),
        scratch_shapes=scratch,
        compiler_params=pltpu.CompilerParams(
            collective_id=0, has_side_effects=True, vmem_limit_bytes=56 * 1024 * 1024
        ),
        cost_estimate=pl.CostEstimate(
            flops=64 * size**3, bytes_accessed=40 * size * size * 2, transcendentals=0
        ),
    )(pair_src, widths, psi, left_ops, right_ops)

    summed = jnp.swapaxes(summed, 1, 2)
    line = jnp.arange(size, dtype=jnp.int32)
    columns = term * (X_PART * rows) + jnp.arange(X_PART * rows, dtype=jnp.int32)
    keep = (line[None, :, None] < widths[0][:, None, None]) & (
        columns[None, None, :] < widths[1][:, None, None]
    )
    return jnp.where(keep, summed, jnp.zeros_like(summed))


def solution(mesh):
    return jax.shard_map(
        shards,
        mesh=mesh,
        in_specs=(
            P("sec", None, None),
            P("term", "sec", None, None),
            P("term", "sec", None, None),
            P("term", None),
            P(None, "sec"),
        ),
        out_specs=P("sec", None, "term"),
        check_vma=False,
    )
```

```python
import jax
import jax.numpy as jnp
from jax import lax
from jax.experimental import pallas as pl
from jax.experimental.pallas import tpu as pltpu
from jax.sharding import PartitionSpec as P

NX, NY, NZ, NC = 4, 4, 8, 2
CHUNKS = 3
PIECES = ((0, 0, 3), (1, 0, 3), (2, 0, 2), (2, 2, 1))
SLOTS = NX * NY
GROUPS_HERE = 2
SECTORS_HERE = 8
TILE = GROUPS_HERE * SECTORS_HERE
SOURCES = SLOTS * TILE
X_PART = NX // NC
STEPS = NZ // 2
MESH = pl.DeviceIdType.MESH
BUFFERS = 11


def routes(sign):
    direct, relayed = [], []
    for dx in range(NX):
        for dy in range(NY):
            far_x, far_y = NX > 2 and dx == NX // 2, NY > 2 and dy == NY // 2
            if far_x or far_y:
                via = (sign if far_x else 0, sign if far_y else 0)
                relayed.append(((dx, dy), via, (dx - via[0], dy - via[1])))
            elif (dx, dy) != (0, 0):
                direct.append((dx, dy))
    return direct, relayed


RELAYS = len(routes(1)[1])


def device(x, y, z, c):
    return (x * NZ + z, y * NC + c)


def ones_where(condition):
    return jnp.where(condition, 1.0, 0.0).astype(jnp.bfloat16)


def tile_at(index):
    return pl.ds(pl.multiple_of(index * TILE, TILE), TILE)


def kernel(pair_src, widths, psi, left, right, out, *rest):
    psi_v, left_v, right_v, orders_own, orders, parts, image, swap, pick, *rest = rest
    sends, rest = rest[:CHUNKS], rest[CHUNKS:]
    buffers = [rest[i * BUFFERS : (i + 1) * BUFFERS] for i in range(len(PIECES))]
    (
        load_sem, order_sem, order_send, spread_send, spread_recv, relay_recv, relay_send, core_send, core_recv,
        up_send, up_recv, down_send, down_recv, final_send, final_recv,
    ) = rest[len(PIECES) * BUFFERS :]
    got, relay, give, take, own, up_out, up_in, down_out, down_in, done, final = zip(*buffers)
    sec, term = lax.axis_index("sec"), lax.axis_index("term")
    x, z = lax.div(sec, NZ), lax.rem(sec, NZ)
    y, c = lax.div(term, NC), lax.rem(term, NC)
    size = psi_v.shape[-1]
    rows = size // SLOTS
    lanes = size // CHUNKS
    targets = pair_src.shape[1]
    pieces = range(len(PIECES))
    y_order = sorted(range(NY), key=lambda dy: -min(dy, NY - dy))
    first_row = [rows * at // 3 for _, at, _ in PIECES]
    piece_rows = [rows * count // 3 for _, _, count in PIECES]

    def shifted(value, by, count):
        return lax.rem(value + (by % count), count)

    barrier = pltpu.get_barrier_semaphore()
    others = [
        device(shifted(x, dx, NX), shifted(y, dy, NY), z, c)
        for dx in range(NX)
        for dy in range(NY)
        if (dx, dy) != (0, 0)
    ]
    others += [device(shifted(x, dx, NX), y, z, 1 - c) for dx in range(NX)]
    others += [device(x, y, shifted(z, 1, NZ), c), device(x, y, shifted(z, -1, NZ), c)]
    for other in others:
        pl.semaphore_signal(barrier, inc=1, device_id=other, device_id_type=MESH)

    def loads(k):
        return (
            pltpu.make_async_copy(psi.at[k], psi_v.at[k], load_sem.at[0, k]),
            pltpu.make_async_copy(left.at[:, k], left_v.at[:, k], load_sem.at[1, k]),
            pltpu.make_async_copy(right.at[:, k], right_v.at[:, k], load_sem.at[2, k]),
        )

    for which in ((0, 1), (2,)):
        for k in range(SECTORS_HERE):
            for copy in which:
                loads(k)[copy].start()

    row = lax.broadcasted_iota(jnp.int32, swap.shape, 0)
    column = lax.broadcasted_iota(jnp.int32, swap.shape, 1)
    swap[...] = ones_where(row == (column & (TILE - 1)) * TILE + lax.shift_right_logical(column, 4))
    orders_own[...] = jnp.concatenate([pair_src[...], jnp.zeros((6, targets), jnp.int32)], 0)

    def part_of(k, chunk):
        here = left_v[:, k, chunk * lanes : (chunk + 1) * lanes, :].reshape(2 * lanes, size)
        return jnp.dot(here, psi_v[k], preferred_element_type=jnp.float32).astype(jnp.bfloat16)

    def image_of(k, group, at, part):
        return lax.dot_general(
            right_v[group, k, at, :], part, (((1,), (1,)), ((), ())), preferred_element_type=jnp.float32
        ).astype(jnp.bfloat16)

    def turn(chunk, low, start):
        both = [
            image[:, pl.ds(pl.multiple_of(low + part * TILE, TILE), TILE), :].reshape(TILE * TILE, lanes)
            for part in range(2)
        ]
        turned = jnp.dot(
            swap[...], jnp.concatenate(both, 1), preferred_element_type=jnp.float32
        ).astype(jnp.bfloat16)
        for part in range(2):
            sends[chunk][pl.ds(start + part * TILE, TILE)] = turned[
                :, part * lanes : (part + 1) * lanes
            ].reshape(TILE, TILE, lanes)

    def first_parts():
        def one(k, _):
            for copy in loads(k)[:2]:
                copy.wait()
            keep = (lax.broadcasted_iota(jnp.int32, (size, size), 0) < widths[0, k]) & (
                lax.broadcasted_iota(jnp.int32, (size, size), 1) < widths[1, k]
            )
            psi_v[k] = jnp.where(keep, psi_v[k].astype(jnp.float32), 0.0).astype(jnp.bfloat16)
            parts[k] = part_of(k, 0)
            return 0

        lax.fori_loop(0, SECTORS_HERE, one, 0)

    def first_images(dy):
        count = size // NY
        start = shifted(y, dy, NY) * count
        at = pl.ds(pl.multiple_of(start, 2 * TILE), count)

        def one(k, _):
            if dy == y_order[0]:
                loads(k)[2].wait()
            for group in range(GROUPS_HERE):
                part = parts[k, group * lanes : (group + 1) * lanes, :]
                image[group * SECTORS_HERE + k, 0:count, :] = image_of(k, group, at, part)
            return 0

        lax.fori_loop(0, SECTORS_HERE, one, 0)
        for low in range(0, count, 2 * TILE):
            turn(0, low, start + low)

    def images(chunk):
        def one(k, _):
            part = part_of(k, chunk)
            for group in range(GROUPS_HERE):
                image[group * SECTORS_HERE + k] = image_of(
                    k, group, slice(None), part[group * lanes : (group + 1) * lanes]
                )
            return 0

        lax.fori_loop(0, SECTORS_HERE, one, 0)

        def some(step, _):
            for inner in range(2):
                low = step * (4 * TILE) + inner * (2 * TILE)
                turn(chunk, low, low)
            return 0

        lax.fori_loop(0, size // (4 * TILE), some, 0)

    def halves(piece):
        count = piece_rows[piece] // 2
        return ((0, 1, 0, count), (1, -1, count, count))

    def block_for(piece, x_to, y_to, low, count):
        start = (y_to * NX + x_to) * rows + first_row[piece] + low
        return sends[PIECES[piece][0]].at[pl.ds(start, count)]

    def place(piece, x_from, y_from, low, count):
        return got[piece].at[low : low + count, tile_at(y_from * NX + x_from)]

    def spread(piece, rings=range(NY)):
        for half, sign, low, count in halves(piece):
            for j, ((dx, dy), (vx, vy), _) in enumerate(routes(sign)[1]):
                if dy in rings:
                    pltpu.make_async_remote_copy(
                        src_ref=block_for(piece, shifted(x, dx, NX), shifted(y, dy, NY), low, count),
                        dst_ref=relay[piece].at[half, j],
                        send_sem=spread_send.at[piece],
                        recv_sem=relay_recv.at[piece, half],
                        device_id=device(shifted(x, vx, NX), shifted(y, vy, NY), z, c),
                        device_id_type=MESH,
                    ).start()
        count = piece_rows[piece]
        for dx, dy in routes(1)[0]:
            if dy in rings:
                xd, yd = shifted(x, dx, NX), shifted(y, dy, NY)
                pltpu.make_async_remote_copy(
                    src_ref=block_for(piece, xd, yd, 0, count),
                    dst_ref=place(piece, x, y, 0, count),
                    send_sem=spread_send.at[piece],
                    recv_sem=spread_recv.at[piece],
                    device_id=device(xd, yd, z, c),
                    device_id_type=MESH,
                ).start()
        if 0 in rings:
            pltpu.make_async_copy(
                block_for(piece, x, y, 0, count), place(piece, x, y, 0, count), spread_recv.at[piece]
            ).start()

    def forward(piece):
        if RELAYS == 0:
            return
        for half, sign, low, count in halves(piece):
            arrived = relay[piece].at[half]
            pltpu.make_async_copy(arrived, arrived, relay_recv.at[piece, half]).wait()
            for j, (_, (vx, vy), (fx, fy)) in enumerate(routes(sign)[1]):
                pltpu.make_async_remote_copy(
                    src_ref=relay[piece].at[half, j],
                    dst_ref=place(piece, shifted(x, -vx, NX), shifted(y, -vy, NY), low, count),
                    send_sem=relay_send.at[piece],
                    recv_sem=spread_recv.at[piece],
                    device_id=device(shifted(x, fx, NX), shifted(y, fy, NY), z, c),
                    device_id_type=MESH,
                ).start()

    def order_copy(dy):
        return pltpu.make_async_remote_copy(
            src_ref=orders_own,
            dst_ref=orders.at[y],
            send_sem=order_send.at[dy],
            recv_sem=order_sem.at[0],
            device_id=device(x, shifted(y, dy, NY), z, c),
            device_id_type=MESH,
        )

    def make_pick():
        pltpu.make_async_copy(orders, orders, order_sem.at[0]).wait()
        line = lax.broadcasted_iota(jnp.int32, (SECTORS_HERE, targets), 0)
        blocks = []
        for yy in range(NY):
            for xx in range(NX):
                for group in range(GROUPS_HERE):
                    wanted = orders[yy, group : group + 1, :]
                    first = (xx * NZ + z) * SECTORS_HERE
                    blocks.append(jnp.where(wanted == line + first, 1.0, 0.0))
        table = jnp.concatenate(blocks, 0).T
        blocks = []
        for xh in range(NC):
            for zz in range(NZ):
                for part in range(X_PART):
                    low = ((xh * X_PART + part) * NZ + zz) * SECTORS_HERE
                    blocks.append(table[low : low + SECTORS_HERE])
        pick[...] = jnp.concatenate(blocks, 0).astype(jnp.bfloat16)

    def gather(piece, part, to):
        half = targets // NC
        chosen = pick[pl.ds(pl.multiple_of(part * half, half), half), :]

        def some(step, _):
            for inner in range(2):
                m = step * 4 + inner * 2
                both = jnp.concatenate([got[piece][m], got[piece][m + 1]], 1)
                value = jnp.dot(chosen, both, preferred_element_type=jnp.float32).astype(to.dtype)
                for zz in range(NZ):
                    for next_m in range(2):
                        to[zz, m + next_m] = value[
                            zz * TILE : (zz + 1) * TILE, next_m * lanes : (next_m + 1) * lanes
                        ]
            return 0

        lax.fori_loop(0, piece_rows[piece] // 4, some, 0)

    def core_copy(piece):
        return pltpu.make_async_remote_copy(
            src_ref=give[piece],
            dst_ref=take[piece],
            send_sem=core_send.at[piece],
            recv_sem=core_recv.at[piece],
            device_id=device(x, y, z, 1 - c),
            device_id_type=MESH,
        )

    def give_half(piece):
        pltpu.make_async_copy(got[piece], got[piece], spread_recv.at[piece]).wait()
        gather(piece, 1 - c, give[piece])
        core_copy(piece).start()

    def keep_half(piece):
        gather(piece, c, own[piece])

    def held(piece, zd, low, count):
        at = slice(low, low + count)
        return own[piece][zd, at] + take[piece][zd, at].astype(jnp.float32)

    def z_buffers(piece, way):
        return (up_out[piece], up_in[piece]) if way > 0 else (down_out[piece], down_in[piece])

    def z_copy(piece, step, way):
        source, target = z_buffers(piece, way)
        out_sem, in_sem = (up_send, up_recv) if way > 0 else (down_send, down_recv)
        at = (step,)
        if step == 0:
            _, _, low, count = halves(piece)[0 if way > 0 else 1]
            at = (step, slice(low, low + count))
        return pltpu.make_async_remote_copy(
            src_ref=source.at[at],
            dst_ref=target.at[at],
            send_sem=out_sem.at[piece, step],
            recv_sem=in_sem.at[piece, step],
            device_id=device(x, y, shifted(z, way, NZ), c),
            device_id_type=MESH,
        )

    def carried(step, way, sign):
        return step > 0 or way == sign

    def chain(piece, step):
        if step >= STEPS:
            return
        if step == 0:
            core_copy(piece).wait_recv()
        for way in (1, -1):
            source, target = z_buffers(piece, way)
            if step > 0:
                z_copy(piece, step - 1, way).wait_recv()
            zd = shifted(z, way * (STEPS - step), NZ)
            for _, sign, low, count in halves(piece):
                if carried(step, way, sign):
                    at = slice(low, low + count)
                    value = held(piece, zd, low, count)
                    if step > 0 and carried(step - 1, way, sign):
                        value = value + target[step - 1, at].astype(jnp.float32)
                    source[step, at] = value.astype(jnp.bfloat16)
            z_copy(piece, step, way).start()

    def final_copies(piece, part):
        xd = c * X_PART + part
        spot_there = final[piece].at[lax.rem(x, X_PART)]
        there = dict(
            src_ref=done[piece].at[part],
            dst_ref=spot_there,
            send_sem=final_send.at[piece, part],
            recv_sem=final_recv.at[piece],
            device_id=device(xd, y, z, lax.div(x, X_PART)),
            device_id_type=MESH,
        )
        here = (done[piece].at[part], spot_there, final_recv.at[piece])
        return xd, there, here

    def finish(piece):
        last = STEPS - 1
        for way in (1, -1):
            z_copy(piece, last, way).wait_recv()
        for _, sign, low, count in halves(piece):
            value = held(piece, z, low, count)
            for way in (1, -1):
                if carried(last, way, sign):
                    value = value + z_buffers(piece, way)[1][last, low : low + count].astype(jnp.float32)
            for part in range(X_PART):
                at = slice(part * SECTORS_HERE, (part + 1) * SECTORS_HERE)
                done[piece][part, low // 2 : (low + count) // 2] = (
                    value[:, at, :].reshape(count // 2, TILE, lanes).astype(jnp.bfloat16)
                )
        for part in range(X_PART):
            xd, there, here = final_copies(piece, part)

            @pl.when(xd != x)
            def _():
                pltpu.make_async_remote_copy(**there).start()

            @pl.when(xd == x)
            def _():
                pltpu.make_async_copy(*here).start()

    def put(piece):
        pltpu.make_async_copy(final[piece], final[piece], final_recv.at[piece]).wait()
        chunk, count = PIECES[piece][0], piece_rows[piece]
        total = X_PART * count * SECTORS_HERE
        row = lax.broadcasted_iota(jnp.int32, (total, total), 0)
        column = lax.broadcasted_iota(jnp.int32, (total, total), 1)
        sector = column & (SECTORS_HERE - 1)
        line = lax.shift_right_logical(column, 3)
        value = jnp.dot(
            ones_where(row == sector * (X_PART * count) + line),
            final[piece][...].reshape(total, lanes),
            preferred_element_type=jnp.float32,
        )
        for sector in range(SECTORS_HERE):
            for part in range(X_PART):
                low = part * rows + first_row[piece]
                start = (sector * X_PART + part) * count
                out[sector, low : low + count, chunk * lanes : (chunk + 1) * lanes] = value[
                    start : start + count
                ]

    first_parts()
    for dy in y_order:
        first_images(dy)
        if dy == y_order[0]:
            pl.semaphore_wait(barrier, len(others))
        spread(0, (dy,))
    for dy in range(1, NY):
        order_copy(dy).start()
    pltpu.make_async_copy(orders_own, orders.at[y], order_sem.at[0]).start()
    images(1)
    forward(0)
    spread(1)
    make_pick()
    images(2)
    give_half(0)
    keep_half(0)
    forward(1)
    spread(2)
    chain(0, 0)
    spread(3)
    chain(0, 1)
    chain(0, 2)
    give_half(1)
    keep_half(1)
    chain(0, 3)
    forward(2)
    chain(1, 0)
    finish(0)
    chain(1, 1)
    forward(3)
    put(0)
    chain(1, 2)
    give_half(2)
    keep_half(2)
    chain(1, 3)
    chain(2, 0)
    give_half(3)
    keep_half(3)
    chain(3, 0)
    finish(1)
    chain(2, 1)
    chain(3, 1)
    put(1)
    chain(2, 2)
    chain(3, 2)
    chain(2, 3)
    chain(3, 3)
    finish(2)
    finish(3)
    put(2)
    put(3)

    for dy in range(1, NY):
        order_copy(dy).wait_send()
    for piece in pieces:
        sent = sends[PIECES[piece][0]].at[0 : (SLOTS - 1) * piece_rows[piece]]
        pltpu.make_async_copy(sent, sent, spread_send.at[piece]).wait()
        if RELAYS:
            pltpu.make_async_copy(relay[piece], relay[piece], relay_send.at[piece]).wait()
        core_copy(piece).wait_send()
        for step in range(STEPS):
            for way in (1, -1):
                z_copy(piece, step, way).wait_send()
        for part in range(X_PART):
            xd, there, _ = final_copies(piece, part)

            @pl.when(xd != x)
            def _():
                pltpu.make_async_remote_copy(**there).wait_send()


def shards(psi, left_ops, right_ops, pair_src, widths):
    size = psi.shape[1]
    targets = pair_src.shape[1]
    rows, lanes = size // SLOTS, size // CHUNKS
    term = lax.axis_index("term")
    bf, count = jnp.bfloat16, len(PIECES)
    tile = (TILE, lanes)
    scratch = [
        pltpu.VMEM(psi.shape, bf),
        pltpu.VMEM(left_ops.shape, bf),
        pltpu.VMEM(right_ops.shape, bf),
        pltpu.VMEM((8, targets), jnp.int32),
        pltpu.VMEM((NY, 8, targets), jnp.int32),
        pltpu.VMEM((SECTORS_HERE, 2 * lanes, size), bf),
        pltpu.VMEM((TILE, size, lanes), bf),
        pltpu.VMEM((TILE * TILE, TILE * TILE), bf),
        pltpu.VMEM((targets, SOURCES), bf),
        *[pltpu.VMEM((size,) + tile, bf) for _ in range(CHUNKS)],
    ]
    for _, _, thirds in PIECES:
        here = rows * thirds // 3
        ring = pltpu.VMEM((STEPS, here) + tile, bf)
        scratch += [
            pltpu.VMEM((here, SOURCES, lanes), bf),
            pltpu.VMEM((2, max(RELAYS, 1), here // 2) + tile, bf),
            pltpu.VMEM((NZ, here) + tile, bf),
            pltpu.VMEM((NZ, here) + tile, bf),
            pltpu.VMEM((NZ, here) + tile, jnp.float32),
            ring, ring, ring, ring,
            pltpu.VMEM((X_PART, here // 2) + tile, bf),
            pltpu.VMEM((X_PART, here // 2) + tile, bf),
        ]
    dma = pltpu.SemaphoreType.DMA
    scratch += [
        dma((3, SECTORS_HERE)), dma((1,)), dma((NY,)), dma((count,)), dma((count,)),
        dma((count, 2)), dma((count,)), dma((count,)), dma((count,)),
        dma((count, STEPS)), dma((count, STEPS)), dma((count, STEPS)), dma((count, STEPS)),
        dma((count, X_PART)), dma((count,)),
    ]
    summed = pl.pallas_call(
        kernel,
        out_shape=jax.ShapeDtypeStruct((SECTORS_HERE, X_PART * rows, size), jnp.float32),
        in_specs=[
            pl.BlockSpec(memory_space=pltpu.VMEM),
            pl.BlockSpec(memory_space=pltpu.SMEM),
            pl.BlockSpec(memory_space=pl.ANY),
            pl.BlockSpec(memory_space=pl.ANY),
            pl.BlockSpec(memory_space=pl.ANY),
        ],
        out_specs=pl.BlockSpec(memory_space=pltpu.VMEM),
        scratch_shapes=scratch,
        compiler_params=pltpu.CompilerParams(
            collective_id=0, has_side_effects=True, vmem_limit_bytes=56 * 1024 * 1024
        ),
        cost_estimate=pl.CostEstimate(
            flops=64 * size**3, bytes_accessed=40 * size * size * 2, transcendentals=0
        ),
    )(pair_src, widths, psi, left_ops, right_ops)

    summed = jnp.swapaxes(summed, 1, 2)
    line = jnp.arange(size, dtype=jnp.int32)
    columns = term * (X_PART * rows) + jnp.arange(X_PART * rows, dtype=jnp.int32)
    keep = (line[None, :, None] < widths[0][:, None, None]) & (
        columns[None, None, :] < widths[1][:, None, None]
    )
    return jnp.where(keep, summed, jnp.zeros_like(summed))


def solution(mesh):
    return jax.shard_map(
        shards,
        mesh=mesh,
        in_specs=(
            P("sec", None, None),
            P("term", "sec", None, None),
            P("term", "sec", None, None),
            P("term", None),
            P(None, "sec"),
        ),
        out_specs=P("sec", None, "term"),
        check_vma=False,
    )
```

```python
import jax
import jax.numpy as jnp
from jax import lax
from jax.experimental import pallas as pl
from jax.experimental.pallas import tpu as pltpu
from jax.sharding import PartitionSpec as P

NX, NY, NZ, NC = 4, 4, 8, 2
CHUNKS = 3
PIECES = ((0, 0, 3), (1, 0, 3), (2, 0, 2), (2, 2, 1))
SLOTS = NX * NY
GROUPS_HERE = 2
SECTORS_HERE = 8
TILE = GROUPS_HERE * SECTORS_HERE
SOURCES = SLOTS * TILE
X_PART = NX // NC
STEPS = NZ // 2
MESH = pl.DeviceIdType.MESH
BUFFERS = 11


def routes(sign):
    direct, relayed = [], []
    for dx in range(NX):
        for dy in range(NY):
            far_x, far_y = NX > 2 and dx == NX // 2, NY > 2 and dy == NY // 2
            if far_x or far_y:
                via = (sign if far_x else 0, sign if far_y else 0)
                relayed.append(((dx, dy), via, (dx - via[0], dy - via[1])))
            elif (dx, dy) != (0, 0):
                direct.append((dx, dy))
    return direct, relayed


RELAYS = len(routes(1)[1])


def device(x, y, z, c):
    return (x * NZ + z, y * NC + c)


def ones_where(condition):
    return jnp.where(condition, 1.0, 0.0).astype(jnp.bfloat16)


def tile_at(index):
    return pl.ds(pl.multiple_of(index * TILE, TILE), TILE)


def kernel(pair_src, widths, psi, left, right, out, *rest):
    psi_v, left_v, right_v, orders_own, orders, parts, image, swap, pick, *rest = rest
    sends, rest = rest[:CHUNKS], rest[CHUNKS:]
    buffers = [rest[i * BUFFERS : (i + 1) * BUFFERS] for i in range(len(PIECES))]
    (
        load_sem, order_sem, order_send, spread_send, spread_recv, relay_recv, relay_send, core_send, core_recv,
        up_send, up_recv, down_send, down_recv, final_send, final_recv,
    ) = rest[len(PIECES) * BUFFERS :]
    got, relay, give, take, own, up_out, up_in, down_out, down_in, done, final = zip(*buffers)
    sec, term = lax.axis_index("sec"), lax.axis_index("term")
    x, z = lax.div(sec, NZ), lax.rem(sec, NZ)
    y, c = lax.div(term, NC), lax.rem(term, NC)
    size = psi_v.shape[-1]
    rows = size // SLOTS
    lanes = size // CHUNKS
    targets = pair_src.shape[1]
    pieces = range(len(PIECES))
    y_order = sorted(range(NY), key=lambda dy: -min(dy, NY - dy))
    first_row = [rows * at // 3 for _, at, _ in PIECES]
    piece_rows = [rows * count // 3 for _, _, count in PIECES]

    def shifted(value, by, count):
        return lax.rem(value + (by % count), count)

    barrier = pltpu.get_barrier_semaphore()
    others = [
        device(shifted(x, dx, NX), shifted(y, dy, NY), z, c)
        for dx in range(NX)
        for dy in range(NY)
        if (dx, dy) != (0, 0)
    ]
    others += [device(shifted(x, dx, NX), y, z, 1 - c) for dx in range(NX)]
    others += [device(x, y, shifted(z, 1, NZ), c), device(x, y, shifted(z, -1, NZ), c)]
    for other in others:
        pl.semaphore_signal(barrier, inc=1, device_id=other, device_id_type=MESH)

    def loads(k):
        return (
            pltpu.make_async_copy(psi.at[k], psi_v.at[k], load_sem.at[0, k]),
            pltpu.make_async_copy(left.at[:, k], left_v.at[:, k], load_sem.at[1, k]),
            pltpu.make_async_copy(right.at[:, k], right_v.at[:, k], load_sem.at[2, k]),
        )

    for which in ((0, 1), (2,)):
        for k in range(SECTORS_HERE):
            for copy in which:
                loads(k)[copy].start()

    row = lax.broadcasted_iota(jnp.int32, swap.shape, 0)
    column = lax.broadcasted_iota(jnp.int32, swap.shape, 1)
    swap[...] = ones_where(row == (column & (TILE - 1)) * TILE + lax.shift_right_logical(column, 4))
    orders_own[...] = jnp.concatenate([pair_src[...], jnp.zeros((6, targets), jnp.int32)], 0)

    def image_of(right_block, part):
        return lax.dot_general(
            right_block, part, (((1,), (1,)), ((), ())), preferred_element_type=jnp.float32
        ).astype(jnp.bfloat16)

    def turned(block):
        return jnp.dot(swap[...], block, preferred_element_type=jnp.float32).astype(jnp.bfloat16)

    def each_sector(body):
        def some(step, _):
            for inner in range(2):
                body(step * 2 + inner)
            return 0

        lax.fori_loop(0, SECTORS_HERE // 2, some, 0)

    def first_parts():
        def one(k):
            for copy in loads(k)[:2]:
                copy.wait()
            keep = (lax.broadcasted_iota(jnp.int32, (size, size), 0) < widths[0, k]) & (
                lax.broadcasted_iota(jnp.int32, (size, size), 1) < widths[1, k]
            )
            masked = jnp.where(keep, psi_v[k].astype(jnp.float32), 0.0).astype(jnp.bfloat16)
            psi_v[k] = masked
            here = left_v[:, k, 0:lanes, :].reshape(GROUPS_HERE * lanes, size)
            parts[k, 0 : GROUPS_HERE * lanes] = jnp.dot(
                here, masked, preferred_element_type=jnp.float32
            ).astype(jnp.bfloat16)

        each_sector(one)

    def first_images(rings, first):
        count = size // NY
        starts = [pl.multiple_of(shifted(y, dy, NY) * count, 2 * TILE) for dy in rings]

        def one(k):
            if first:
                loads(k)[2].wait()
            for group in range(GROUPS_HERE):
                chosen = jnp.concatenate([right_v[group, k, pl.ds(start, count), :] for start in starts], 0)
                image[group * SECTORS_HERE + k, 0 : count * len(starts), 0:lanes] = image_of(
                    chosen, parts[k, group * lanes : (group + 1) * lanes, :]
                )

        each_sector(one)
        for low in range(0, count * len(starts), 2 * TILE):
            both = turned(
                jnp.concatenate(
                    [
                        image[:, at : at + TILE, 0:lanes].reshape(TILE * TILE, lanes)
                        for at in (low, low + TILE)
                    ],
                    1,
                )
            )
            for part in range(2):
                at = starts[low // count] + low % count + part * TILE
                sends[0][pl.ds(at, TILE)] = both[:, part * lanes : (part + 1) * lanes].reshape(
                    TILE, TILE, lanes
                )

    later = size - lanes

    def later_parts():
        def one(k):
            here = left_v[:, k, lanes:, :].reshape(GROUPS_HERE * later, size)
            parts[k] = jnp.dot(here, psi_v[k], preferred_element_type=jnp.float32).astype(jnp.bfloat16)

        each_sector(one)

    def later_images():
        def one(k):
            for group in range(GROUPS_HERE):
                image[group * SECTORS_HERE + k] = image_of(
                    right_v[group, k], parts[k, group * later : (group + 1) * later, :]
                )

        each_sector(one)

        def some(step, _):
            for inner in range(4):
                at = pl.multiple_of((step * 4 + inner) * TILE, TILE)
                value = turned(image[:, pl.ds(at, TILE), :].reshape(TILE * TILE, later))
                for chunk in range(1, CHUNKS):
                    sends[chunk][pl.ds(at, TILE)] = value[
                        :, (chunk - 1) * lanes : chunk * lanes
                    ].reshape(TILE, TILE, lanes)
            return 0

        lax.fori_loop(0, size // (4 * TILE), some, 0)

    def halves(piece):
        count = piece_rows[piece] // 2
        return ((0, 1, 0, count), (1, -1, count, count))

    def block_for(piece, x_to, y_to, low, count):
        start = (y_to * NX + x_to) * rows + first_row[piece] + low
        return sends[PIECES[piece][0]].at[pl.ds(start, count)]

    def place(piece, x_from, y_from, low, count):
        return got[piece].at[low : low + count, tile_at(y_from * NX + x_from)]

    def spread(piece, rings=range(NY)):
        for half, sign, low, count in halves(piece):
            for j, ((dx, dy), (vx, vy), _) in enumerate(routes(sign)[1]):
                if dy in rings:
                    pltpu.make_async_remote_copy(
                        src_ref=block_for(piece, shifted(x, dx, NX), shifted(y, dy, NY), low, count),
                        dst_ref=relay[piece].at[half, j],
                        send_sem=spread_send.at[piece],
                        recv_sem=relay_recv.at[piece, half],
                        device_id=device(shifted(x, vx, NX), shifted(y, vy, NY), z, c),
                        device_id_type=MESH,
                    ).start()
        count = piece_rows[piece]
        for dx, dy in routes(1)[0]:
            if dy in rings:
                xd, yd = shifted(x, dx, NX), shifted(y, dy, NY)
                pltpu.make_async_remote_copy(
                    src_ref=block_for(piece, xd, yd, 0, count),
                    dst_ref=place(piece, x, y, 0, count),
                    send_sem=spread_send.at[piece],
                    recv_sem=spread_recv.at[piece],
                    device_id=device(xd, yd, z, c),
                    device_id_type=MESH,
                ).start()
        if 0 in rings:
            pltpu.make_async_copy(
                block_for(piece, x, y, 0, count), place(piece, x, y, 0, count), spread_recv.at[piece]
            ).start()

    def forward(piece):
        if RELAYS == 0:
            return
        for half, sign, low, count in halves(piece):
            arrived = relay[piece].at[half]
            pltpu.make_async_copy(arrived, arrived, relay_recv.at[piece, half]).wait()
            for j, (_, (vx, vy), (fx, fy)) in enumerate(routes(sign)[1]):
                pltpu.make_async_remote_copy(
                    src_ref=relay[piece].at[half, j],
                    dst_ref=place(piece, shifted(x, -vx, NX), shifted(y, -vy, NY), low, count),
                    send_sem=relay_send.at[piece],
                    recv_sem=spread_recv.at[piece],
                    device_id=device(shifted(x, fx, NX), shifted(y, fy, NY), z, c),
                    device_id_type=MESH,
                ).start()

    def order_copy(dy):
        return pltpu.make_async_remote_copy(
            src_ref=orders_own,
            dst_ref=orders.at[y],
            send_sem=order_send.at[dy],
            recv_sem=order_sem.at[0],
            device_id=device(x, shifted(y, dy, NY), z, c),
            device_id_type=MESH,
        )

    def make_pick():
        pltpu.make_async_copy(orders, orders, order_sem.at[0]).wait()
        line = lax.broadcasted_iota(jnp.int32, (SECTORS_HERE, targets), 0)
        blocks = []
        for yy in range(NY):
            for xx in range(NX):
                for group in range(GROUPS_HERE):
                    wanted = orders[yy, group : group + 1, :]
                    first = (xx * NZ + z) * SECTORS_HERE
                    blocks.append(jnp.where(wanted == line + first, 1.0, 0.0))
        table = jnp.concatenate(blocks, 0).T
        half = targets // NC
        for xh in range(NC):
            blocks = []
            for zz in range(NZ):
                for part in range(X_PART):
                    low = ((xh * X_PART + part) * NZ + zz) * SECTORS_HERE
                    blocks.append(table[low : low + SECTORS_HERE])
            start = pl.multiple_of((1 - c if xh == 0 else c) * half, half)
            pick[pl.ds(start, half), :] = jnp.concatenate(blocks, 0).astype(jnp.bfloat16)

    def gather(piece):
        pltpu.make_async_copy(got[piece], got[piece], spread_recv.at[piece]).wait()
        half = targets // NC

        def some(step, _):
            for inner in range(4):
                m = step * 8 + inner * 2
                both = jnp.concatenate([got[piece][m], got[piece][m + 1]], 1)
                value = jnp.dot(pick[...], both, preferred_element_type=jnp.float32)
                for part, to in ((0, give[piece]), (1, own[piece])):
                    for zz in range(NZ):
                        low = part * half + zz * TILE
                        for next_m in range(2):
                            to[zz, m + next_m] = value[
                                low : low + TILE, next_m * lanes : (next_m + 1) * lanes
                            ].astype(to.dtype)
            return 0

        lax.fori_loop(0, piece_rows[piece] // 8, some, 0)
        core_copy(piece).start()

    def core_copy(piece):
        return pltpu.make_async_remote_copy(
            src_ref=give[piece],
            dst_ref=take[piece],
            send_sem=core_send.at[piece],
            recv_sem=core_recv.at[piece],
            device_id=device(x, y, z, 1 - c),
            device_id_type=MESH,
        )

    def held(piece, zd, low, count):
        at = slice(low, low + count)
        return own[piece][zd, at] + take[piece][zd, at].astype(jnp.float32)

    def z_buffers(piece, way):
        return (up_out[piece], up_in[piece]) if way > 0 else (down_out[piece], down_in[piece])

    def z_copy(piece, step, way):
        source, target = z_buffers(piece, way)
        out_sem, in_sem = (up_send, up_recv) if way > 0 else (down_send, down_recv)
        at = (step,)
        if step == 0:
            _, _, low, count = halves(piece)[0 if way > 0 else 1]
            at = (step, slice(low, low + count))
        return pltpu.make_async_remote_copy(
            src_ref=source.at[at],
            dst_ref=target.at[at],
            send_sem=out_sem.at[piece, step],
            recv_sem=in_sem.at[piece, step],
            device_id=device(x, y, shifted(z, way, NZ), c),
            device_id_type=MESH,
        )

    def carried(step, way, sign):
        return step > 0 or way == sign

    def chain(piece, step):
        if step >= STEPS:
            return
        if step == 0:
            core_copy(piece).wait_recv()
        for way in (1, -1):
            source, target = z_buffers(piece, way)
            if step > 0:
                z_copy(piece, step - 1, way).wait_recv()
            zd = shifted(z, way * (STEPS - step), NZ)
            for _, sign, low, count in halves(piece):
                if carried(step, way, sign):
                    at = slice(low, low + count)
                    value = held(piece, zd, low, count)
                    if step > 0 and carried(step - 1, way, sign):
                        value = value + target[step - 1, at].astype(jnp.float32)
                    source[step, at] = value.astype(jnp.bfloat16)
            z_copy(piece, step, way).start()

    def final_copies(piece, part):
        xd = c * X_PART + part
        spot_there = final[piece].at[lax.rem(x, X_PART)]
        there = dict(
            src_ref=done[piece].at[part],
            dst_ref=spot_there,
            send_sem=final_send.at[piece, part],
            recv_sem=final_recv.at[piece],
            device_id=device(xd, y, z, lax.div(x, X_PART)),
            device_id_type=MESH,
        )
        here = (done[piece].at[part], spot_there, final_recv.at[piece])
        return xd, there, here

    def finish(piece):
        last = STEPS - 1
        for way in (1, -1):
            z_copy(piece, last, way).wait_recv()
        for _, sign, low, count in halves(piece):
            value = held(piece, z, low, count)
            for way in (1, -1):
                if carried(last, way, sign):
                    value = value + z_buffers(piece, way)[1][last, low : low + count].astype(jnp.float32)
            for part in range(X_PART):
                at = slice(part * SECTORS_HERE, (part + 1) * SECTORS_HERE)
                done[piece][part, low // 2 : (low + count) // 2] = (
                    value[:, at, :].reshape(count // 2, TILE, lanes).astype(jnp.bfloat16)
                )
        for part in range(X_PART):
            xd, there, here = final_copies(piece, part)

            @pl.when(xd != x)
            def _():
                pltpu.make_async_remote_copy(**there).start()

            @pl.when(xd == x)
            def _():
                pltpu.make_async_copy(*here).start()

    def put(piece):
        pltpu.make_async_copy(final[piece], final[piece], final_recv.at[piece]).wait()
        chunk, count = PIECES[piece][0], piece_rows[piece]
        total = X_PART * count * SECTORS_HERE
        row = lax.broadcasted_iota(jnp.int32, (total, total), 0)
        column = lax.broadcasted_iota(jnp.int32, (total, total), 1)
        sector = column & (SECTORS_HERE - 1)
        line = lax.shift_right_logical(column, 3)
        value = jnp.dot(
            ones_where(row == sector * (X_PART * count) + line),
            final[piece][...].reshape(total, lanes),
            preferred_element_type=jnp.float32,
        )
        for sector in range(SECTORS_HERE):
            for part in range(X_PART):
                low = part * rows + first_row[piece]
                start = (sector * X_PART + part) * count
                out[sector, low : low + count, chunk * lanes : (chunk + 1) * lanes] = value[
                    start : start + count
                ]

    first_parts()
    for part in range(2):
        rings = y_order[part * NY // 2 : (part + 1) * NY // 2]
        first_images(rings, part == 0)
        if part == 0:
            pl.semaphore_wait(barrier, len(others))
        spread(0, rings)
    for dy in range(1, NY):
        order_copy(dy).start()
    pltpu.make_async_copy(orders_own, orders.at[y], order_sem.at[0]).start()
    later_parts()
    forward(0)
    later_images()
    spread(1)
    make_pick()
    gather(0)
    forward(1)
    spread(2)
    chain(0, 0)
    spread(3)
    chain(0, 1)
    chain(0, 2)
    gather(1)
    chain(0, 3)
    forward(2)
    chain(1, 0)
    finish(0)
    chain(1, 1)
    forward(3)
    put(0)
    chain(1, 2)
    gather(2)
    chain(1, 3)
    chain(2, 0)
    gather(3)
    finish(1)
    chain(3, 0)
    chain(2, 1)
    chain(3, 1)
    put(1)
    chain(2, 2)
    chain(3, 2)
    chain(2, 3)
    chain(3, 3)
    finish(2)
    finish(3)
    put(2)
    put(3)

    for dy in range(1, NY):
        order_copy(dy).wait_send()
    for piece in pieces:
        sent = sends[PIECES[piece][0]].at[0 : (SLOTS - 1) * piece_rows[piece]]
        pltpu.make_async_copy(sent, sent, spread_send.at[piece]).wait()
        if RELAYS:
            pltpu.make_async_copy(relay[piece], relay[piece], relay_send.at[piece]).wait()
        core_copy(piece).wait_send()
        for step in range(STEPS):
            for way in (1, -1):
                z_copy(piece, step, way).wait_send()
        for part in range(X_PART):
            xd, there, _ = final_copies(piece, part)

            @pl.when(xd != x)
            def _():
                pltpu.make_async_remote_copy(**there).wait_send()


def shards(psi, left_ops, right_ops, pair_src, widths):
    size = psi.shape[1]
    targets = pair_src.shape[1]
    rows, lanes = size // SLOTS, size // CHUNKS
    term = lax.axis_index("term")
    bf, count = jnp.bfloat16, len(PIECES)
    tile = (TILE, lanes)
    scratch = [
        pltpu.VMEM(psi.shape, bf),
        pltpu.VMEM(left_ops.shape, bf),
        pltpu.VMEM(right_ops.shape, bf),
        pltpu.VMEM((8, targets), jnp.int32),
        pltpu.VMEM((NY, 8, targets), jnp.int32),
        pltpu.VMEM((SECTORS_HERE, GROUPS_HERE * (size - lanes), size), bf),
        pltpu.VMEM((TILE, size, size - lanes), bf),
        pltpu.VMEM((TILE * TILE, TILE * TILE), bf),
        pltpu.VMEM((targets, SOURCES), bf),
        *[pltpu.VMEM((size,) + tile, bf) for _ in range(CHUNKS)],
    ]
    for _, _, thirds in PIECES:
        here = rows * thirds // 3
        ring = pltpu.VMEM((STEPS, here) + tile, bf)
        scratch += [
            pltpu.VMEM((here, SOURCES, lanes), bf),
            pltpu.VMEM((2, max(RELAYS, 1), here // 2) + tile, bf),
            pltpu.VMEM((NZ, here) + tile, bf),
            pltpu.VMEM((NZ, here) + tile, bf),
            pltpu.VMEM((NZ, here) + tile, jnp.float32),
            ring, ring, ring, ring,
            pltpu.VMEM((X_PART, here // 2) + tile, bf),
            pltpu.VMEM((X_PART, here // 2) + tile, bf),
        ]
    dma = pltpu.SemaphoreType.DMA
    scratch += [
        dma((3, SECTORS_HERE)), dma((1,)), dma((NY,)), dma((count,)), dma((count,)),
        dma((count, 2)), dma((count,)), dma((count,)), dma((count,)),
        dma((count, STEPS)), dma((count, STEPS)), dma((count, STEPS)), dma((count, STEPS)),
        dma((count, X_PART)), dma((count,)),
    ]
    summed = pl.pallas_call(
        kernel,
        out_shape=jax.ShapeDtypeStruct((SECTORS_HERE, X_PART * rows, size), jnp.float32),
        in_specs=[
            pl.BlockSpec(memory_space=pltpu.VMEM),
            pl.BlockSpec(memory_space=pltpu.SMEM),
            pl.BlockSpec(memory_space=pl.ANY),
            pl.BlockSpec(memory_space=pl.ANY),
            pl.BlockSpec(memory_space=pl.ANY),
        ],
        out_specs=pl.BlockSpec(memory_space=pltpu.VMEM),
        scratch_shapes=scratch,
        compiler_params=pltpu.CompilerParams(
            collective_id=0, has_side_effects=True, vmem_limit_bytes=56 * 1024 * 1024
        ),
        cost_estimate=pl.CostEstimate(
            flops=64 * size**3, bytes_accessed=40 * size * size * 2, transcendentals=0
        ),
    )(pair_src, widths, psi, left_ops, right_ops)

    summed = jnp.swapaxes(summed, 1, 2)
    line = jnp.arange(size, dtype=jnp.int32)
    columns = term * (X_PART * rows) + jnp.arange(X_PART * rows, dtype=jnp.int32)
    keep = (line[None, :, None] < widths[0][:, None, None]) & (
        columns[None, None, :] < widths[1][:, None, None]
    )
    return jnp.where(keep, summed, jnp.zeros_like(summed))


def solution(mesh):
    return jax.shard_map(
        shards,
        mesh=mesh,
        in_specs=(
            P("sec", None, None),
            P("term", "sec", None, None),
            P("term", "sec", None, None),
            P("term", None),
            P(None, "sec"),
        ),
        out_specs=P("sec", None, "term"),
        check_vma=False,
    )
```

```python
import jax
import jax.numpy as jnp
from jax import lax
from jax.experimental import pallas as pl
from jax.experimental.pallas import tpu as pltpu
from jax.sharding import PartitionSpec as P

NX, NY, NZ, NC = 4, 4, 8, 2
CHUNKS = 3
PIECES = ((0, 0, 3), (1, 0, 3), (2, 0, 2), (2, 2, 1))
SLOTS = NX * NY
GROUPS_HERE = 2
SECTORS_HERE = 8
TILE = GROUPS_HERE * SECTORS_HERE
SOURCES = SLOTS * TILE
X_PART = NX // NC
STEPS = NZ // 2
MESH = pl.DeviceIdType.MESH
LANES = 128
BUFFERS = 12


def routes(sign):
    direct, relayed = [], []
    for dx, dy in sorted(
        [(dx, dy) for dx in range(NX) for dy in range(NY)],
        key=lambda move: (min(move[0], NX - move[0]) + min(move[1], NY - move[1]), move[0] == 0, move),
    ):
        far_x, far_y = NX > 2 and dx == NX // 2, NY > 2 and dy == NY // 2
        if far_x or far_y:
            via = (sign if far_x else 0, sign if far_y else 0)
            relayed.append(((dx, dy), via, (dx - via[0], dy - via[1])))
        elif (dx, dy) != (0, 0):
            direct.append((dx, dy))
    by_x = [route for route in relayed if route[1][0] != 0]
    by_y = [route for route in relayed if route[1][0] == 0]
    relayed = [route for pair in zip(by_x, by_y) for route in pair]
    relayed += by_x[len(by_y) :] + by_y[len(by_x) :]
    return direct, relayed


RELAYS = len(routes(1)[1])


def device(x, y, z, c):
    return (x * NZ + z, y * NC + c)


def ones_where(condition):
    return jnp.where(condition, 1.0, 0.0).astype(jnp.bfloat16)


def tile_at(index):
    return pl.ds(pl.multiple_of(index * TILE, TILE), TILE)


def kernel(pair_src, widths, psi, left, right, out, *rest):
    psi_v, left_v, right_v, orders_own, orders, parts, image, swap, pick, *rest = rest
    sends, rest = rest[:CHUNKS], rest[CHUNKS:]
    buffers = [rest[i * BUFFERS : (i + 1) * BUFFERS] for i in range(len(PIECES))]
    (
        load_sem, order_sem, order_send, spread_send, spread_recv, relay_recv, relay_send, core_send, core_recv,
        up_send, up_recv, down_send, down_recv, final_send, final_recv,
    ) = rest[len(PIECES) * BUFFERS :]
    got, relay, give, take, own, up_out, up_in, down_out, down_in, done, final, spots = zip(*buffers)
    sec, term = lax.axis_index("sec"), lax.axis_index("term")
    x, z = lax.div(sec, NZ), lax.rem(sec, NZ)
    y, c = lax.div(term, NC), lax.rem(term, NC)
    size = psi_v.shape[-1]
    rows = size // SLOTS
    lanes = size // CHUNKS
    targets = pair_src.shape[1]
    pieces = range(len(PIECES))
    y_order = sorted(range(NY), key=lambda dy: -min(dy, NY - dy))
    first_row = [rows * at // 3 for _, at, _ in PIECES]
    piece_rows = [rows * count // 3 for _, _, count in PIECES]

    def shifted(value, by, count):
        return lax.rem(value + (by % count), count)

    barrier = pltpu.get_barrier_semaphore()
    others = [
        device(shifted(x, dx, NX), shifted(y, dy, NY), z, c)
        for dx in range(NX)
        for dy in range(NY)
        if (dx, dy) != (0, 0)
    ]
    others += [device(shifted(x, dx, NX), y, z, 1 - c) for dx in range(NX)]
    others += [device(x, y, shifted(z, 1, NZ), c), device(x, y, shifted(z, -1, NZ), c)]
    for other in others:
        pl.semaphore_signal(barrier, inc=1, device_id=other, device_id_type=MESH)

    def loads(k):
        return (
            pltpu.make_async_copy(psi.at[k], psi_v.at[k], load_sem.at[0, k]),
            pltpu.make_async_copy(left.at[:, k], left_v.at[:, k], load_sem.at[1, k]),
            pltpu.make_async_copy(right.at[:, k], right_v.at[:, k], load_sem.at[2, k]),
        )

    for which in ((0, 1), (2,)):
        for k in range(SECTORS_HERE):
            for copy in which:
                loads(k)[copy].start()

    row = lax.broadcasted_iota(jnp.int32, swap.shape, 0)
    column = lax.broadcasted_iota(jnp.int32, swap.shape, 1)
    swap[...] = ones_where(row == (column & (TILE - 1)) * TILE + lax.shift_right_logical(column, 4))
    orders_own[...] = jnp.concatenate([pair_src[...], jnp.zeros((6, targets), jnp.int32)], 0)

    def image_of(right_block, part):
        return lax.dot_general(
            right_block, part, (((1,), (1,)), ((), ())), preferred_element_type=jnp.float32
        ).astype(jnp.bfloat16)

    def turned(block):
        return jnp.dot(swap[...], block, preferred_element_type=jnp.float32).astype(jnp.bfloat16)

    def each_sector(body):
        def some(step, _):
            for inner in range(2):
                body(step * 2 + inner)
            return 0

        lax.fori_loop(0, SECTORS_HERE // 2, some, 0)

    def first_parts():
        def one(k):
            for copy in loads(k)[:2]:
                copy.wait()
            keep = (lax.broadcasted_iota(jnp.int32, (size, size), 0) < widths[0, k]) & (
                lax.broadcasted_iota(jnp.int32, (size, size), 1) < widths[1, k]
            )
            masked = jnp.where(keep, psi_v[k].astype(jnp.float32), 0.0).astype(jnp.bfloat16)
            psi_v[k] = masked
            here = left_v[:, k, 0:lanes, :].reshape(GROUPS_HERE * lanes, size)
            parts[k, 0 : GROUPS_HERE * lanes] = jnp.dot(
                here, masked, preferred_element_type=jnp.float32
            ).astype(jnp.bfloat16)

        each_sector(one)

    def first_images(rings, first):
        count = size // NY
        starts = [pl.multiple_of(shifted(y, dy, NY) * count, 2 * TILE) for dy in rings]

        def one(k):
            if first:
                loads(k)[2].wait()
            for group in range(GROUPS_HERE):
                chosen = jnp.concatenate([right_v[group, k, pl.ds(start, count), :] for start in starts], 0)
                image[group * SECTORS_HERE + k, 0 : count * len(starts), 0:lanes] = image_of(
                    chosen, parts[k, group * lanes : (group + 1) * lanes, :]
                )

        each_sector(one)
        for low in range(0, count * len(starts), 2 * TILE):
            both = turned(
                jnp.concatenate(
                    [
                        image[:, at : at + TILE, 0:lanes].reshape(TILE * TILE, lanes)
                        for at in (low, low + TILE)
                    ],
                    1,
                )
            )
            for part in range(2):
                at = starts[low // count] + low % count + part * TILE
                sends[0][pl.ds(at, TILE)] = both[:, part * lanes : (part + 1) * lanes].reshape(
                    TILE, TILE, lanes
                )

    later = size - lanes

    def later_parts():
        def one(k):
            here = left_v[:, k, lanes:, :].reshape(GROUPS_HERE * later, size)
            parts[k] = jnp.dot(here, psi_v[k], preferred_element_type=jnp.float32).astype(jnp.bfloat16)

        each_sector(one)

    def later_images():
        def one(k):
            for group in range(GROUPS_HERE):
                image[group * SECTORS_HERE + k] = image_of(
                    right_v[group, k], parts[k, group * later : (group + 1) * later, :]
                )

        each_sector(one)

        def some(step, _):
            for inner in range(4):
                at = pl.multiple_of((step * 4 + inner) * TILE, TILE)
                value = turned(image[:, pl.ds(at, TILE), :].reshape(TILE * TILE, later))
                for chunk in range(1, CHUNKS):
                    sends[chunk][pl.ds(at, TILE)] = value[
                        :, (chunk - 1) * lanes : chunk * lanes
                    ].reshape(TILE, TILE, lanes)
            return 0

        lax.fori_loop(0, size // (4 * TILE), some, 0)

    def halves(piece):
        count = piece_rows[piece] // 2
        return ((0, 1, 0, count), (1, -1, count, count))

    def block_for(piece, x_to, y_to, low, count):
        start = (y_to * NX + x_to) * rows + first_row[piece] + low
        return sends[PIECES[piece][0]].at[pl.ds(start, count)]

    def place(piece, x_from, y_from, low, count):
        return got[piece].at[low : low + count, tile_at(y_from * NX + x_from)]

    def spread(piece, rings=range(NY)):
        for j in range(RELAYS):
            for half, sign, low, count in halves(piece):
                (dx, dy), (vx, vy), _ = routes(sign)[1][j]
                if dy in rings:
                    pltpu.make_async_remote_copy(
                        src_ref=block_for(piece, shifted(x, dx, NX), shifted(y, dy, NY), low, count),
                        dst_ref=relay[piece].at[half, j],
                        send_sem=spread_send.at[piece],
                        recv_sem=relay_recv.at[piece, half],
                        device_id=device(shifted(x, vx, NX), shifted(y, vy, NY), z, c),
                        device_id_type=MESH,
                    ).start()
        count = piece_rows[piece]
        for dx, dy in routes(1)[0]:
            if dy in rings:
                xd, yd = shifted(x, dx, NX), shifted(y, dy, NY)
                pltpu.make_async_remote_copy(
                    src_ref=block_for(piece, xd, yd, 0, count),
                    dst_ref=place(piece, x, y, 0, count),
                    send_sem=spread_send.at[piece],
                    recv_sem=spread_recv.at[piece],
                    device_id=device(xd, yd, z, c),
                    device_id_type=MESH,
                ).start()
        if 0 in rings:
            pltpu.make_async_copy(
                block_for(piece, x, y, 0, count), place(piece, x, y, 0, count), spread_recv.at[piece]
            ).start()

    def forward(piece):
        if RELAYS == 0:
            return
        for half in range(2):
            arrived = relay[piece].at[half]
            pltpu.make_async_copy(arrived, arrived, relay_recv.at[piece, half]).wait()
        for j in range(RELAYS):
            for half, sign, low, count in halves(piece):
                _, (vx, vy), (fx, fy) = routes(sign)[1][j]
                pltpu.make_async_remote_copy(
                    src_ref=relay[piece].at[half, j],
                    dst_ref=place(piece, shifted(x, -vx, NX), shifted(y, -vy, NY), low, count),
                    send_sem=relay_send.at[piece],
                    recv_sem=spread_recv.at[piece],
                    device_id=device(shifted(x, fx, NX), shifted(y, fy, NY), z, c),
                    device_id_type=MESH,
                ).start()

    def order_copy(dy):
        return pltpu.make_async_remote_copy(
            src_ref=orders_own,
            dst_ref=orders.at[y],
            send_sem=order_send.at[dy],
            recv_sem=order_sem.at[0],
            device_id=device(x, shifted(y, dy, NY), z, c),
            device_id_type=MESH,
        )

    def make_pick():
        pltpu.make_async_copy(orders, orders, order_sem.at[0]).wait()
        line = lax.broadcasted_iota(jnp.int32, (SECTORS_HERE, targets), 0)
        blocks = []
        for yy in range(NY):
            for xx in range(NX):
                for group in range(GROUPS_HERE):
                    wanted = orders[yy, group : group + 1, :]
                    first = (xx * NZ + z) * SECTORS_HERE
                    blocks.append(jnp.where(wanted == line + first, 1.0, 0.0))
        table = jnp.concatenate(blocks, 0).T
        half = targets // NC
        for xh in range(NC):
            blocks = []
            for zz in range(NZ):
                for part in range(X_PART):
                    low = ((xh * X_PART + part) * NZ + zz) * SECTORS_HERE
                    blocks.append(table[low : low + SECTORS_HERE])
            start = pl.multiple_of((1 - c if xh == 0 else c) * half, half)
            pick[pl.ds(start, half), :] = jnp.concatenate(blocks, 0).astype(jnp.bfloat16)

    def gather(piece):
        pltpu.make_async_copy(got[piece], got[piece], spread_recv.at[piece]).wait()
        half = targets // NC

        def some(step, _):
            for inner in range(4):
                m = step * 8 + inner * 2
                both = jnp.concatenate([got[piece][m], got[piece][m + 1]], 1)
                value = jnp.dot(pick[...], both, preferred_element_type=jnp.float32)
                for part, to in ((0, give[piece]), (1, own[piece])):
                    for zz in range(NZ):
                        low = part * half + zz * TILE
                        for next_m in range(2):
                            to[zz, m + next_m] = value[
                                low : low + TILE, next_m * lanes : (next_m + 1) * lanes
                            ].astype(to.dtype)
            return 0

        lax.fori_loop(0, piece_rows[piece] // 8, some, 0)
        core_copy(piece).start()

    def core_copy(piece):
        return pltpu.make_async_remote_copy(
            src_ref=give[piece],
            dst_ref=take[piece],
            send_sem=core_send.at[piece],
            recv_sem=core_recv.at[piece],
            device_id=device(x, y, z, 1 - c),
            device_id_type=MESH,
        )

    def held(piece, zd, low, count):
        at = slice(low, low + count)
        return own[piece][zd, at] + take[piece][zd, at].astype(jnp.float32)

    def z_buffers(piece, way):
        return (up_out[piece], up_in[piece]) if way > 0 else (down_out[piece], down_in[piece])

    def z_copy(piece, step, way):
        source, target = z_buffers(piece, way)
        out_sem, in_sem = (up_send, up_recv) if way > 0 else (down_send, down_recv)
        at = (step,)
        if step == 0:
            _, _, low, count = halves(piece)[0 if way > 0 else 1]
            at = (step, slice(low, low + count))
        return pltpu.make_async_remote_copy(
            src_ref=source.at[at],
            dst_ref=target.at[at],
            send_sem=out_sem.at[piece, step],
            recv_sem=in_sem.at[piece, step],
            device_id=device(x, y, shifted(z, way, NZ), c),
            device_id_type=MESH,
        )

    def carried(step, way, sign):
        return step > 0 or way == sign

    def chain(piece, step):
        if step >= STEPS:
            return
        if step == 0:
            core_copy(piece).wait_recv()
        for way in (1, -1):
            source, target = z_buffers(piece, way)
            if step > 0:
                z_copy(piece, step - 1, way).wait_recv()
            zd = shifted(z, way * (STEPS - step), NZ)
            for _, sign, low, count in halves(piece):
                if carried(step, way, sign):
                    at = slice(low, low + count)
                    value = held(piece, zd, low, count)
                    if step > 0 and carried(step - 1, way, sign):
                        value = value + target[step - 1, at].astype(jnp.float32)
                    source[step, at] = value.astype(jnp.bfloat16)
            z_copy(piece, step, way).start()

    def final_copies(piece, part):
        xd = c * X_PART + part
        spot_there = final[piece].at[lax.rem(x, X_PART)]
        there = dict(
            src_ref=done[piece].at[part],
            dst_ref=spot_there,
            send_sem=final_send.at[piece, part],
            recv_sem=final_recv.at[piece],
            device_id=device(xd, y, z, lax.div(x, X_PART)),
            device_id_type=MESH,
        )
        here = (done[piece].at[part], spot_there, final_recv.at[piece])
        return xd, there, here

    def finish(piece):
        last = STEPS - 1
        for way in (1, -1):
            z_copy(piece, last, way).wait_recv()
        for _, sign, low, count in halves(piece):
            value = held(piece, z, low, count)
            for way in (1, -1):
                if carried(last, way, sign):
                    value = value + z_buffers(piece, way)[1][last, low : low + count].astype(jnp.float32)
            for part in range(X_PART):
                at = slice(part * SECTORS_HERE, (part + 1) * SECTORS_HERE)
                done[piece][part, low // 2 : (low + count) // 2] = (
                    value[:, at, :].reshape(count // 2, TILE, lanes).astype(jnp.bfloat16)
                )
        for part in range(X_PART):
            xd, there, here = final_copies(piece, part)

            @pl.when(xd != x)
            def _():
                pltpu.make_async_remote_copy(**there).start()

            @pl.when(xd == x)
            def _():
                pltpu.make_async_copy(*here).start()

    def make_spots():
        for piece in pieces:
            total, columns = spots[piece].shape
            count = piece_rows[piece]
            row = lax.broadcasted_iota(jnp.int32, (total, 1), 0)
            line = lax.shift_right_logical(row, 3)
            line = line + jnp.where(line < count, 0, rows - count) + first_row[piece]
            spot = (row & (SECTORS_HERE - 1)) * LANES + line
            spots[piece][...] = ones_where(
                lax.broadcasted_iota(jnp.int32, (total, columns), 1) == spot
            )

    def put(chunk):
        value = None
        for piece in pieces:
            if PIECES[piece][0] == chunk:
                pltpu.make_async_copy(final[piece], final[piece], final_recv.at[piece]).wait()
                here = lax.dot_general(
                    final[piece][...].reshape(spots[piece].shape[0], lanes),
                    spots[piece][...],
                    (((0,), (0,)), ((), ())),
                    preferred_element_type=jnp.float32,
                )
                value = here if value is None else value + here
        width = X_PART * rows
        row = chunk * lanes + lax.broadcasted_iota(jnp.int32, (lanes, width), 0)
        column = term * width + lax.broadcasted_iota(jnp.int32, (lanes, width), 1)
        for sector in range(SECTORS_HERE):
            keep = (row < widths[0, sector]) & (column < widths[1, sector])
            block = value[:, sector * LANES : sector * LANES + width]
            out[sector, chunk * lanes : (chunk + 1) * lanes, :] = jnp.where(keep, block, 0.0)

    first_parts()
    for part in range(2):
        rings = y_order[part * NY // 2 : (part + 1) * NY // 2]
        first_images(rings, part == 0)
        if part == 0:
            pl.semaphore_wait(barrier, len(others))
        spread(0, rings)
    for dy in range(1, NY):
        order_copy(dy).start()
    pltpu.make_async_copy(orders_own, orders.at[y], order_sem.at[0]).start()
    later_parts()
    forward(0)
    later_images()
    spread(1)
    make_pick()
    gather(0)
    forward(1)
    spread(2)
    chain(0, 0)
    spread(3)
    make_spots()
    chain(0, 1)
    chain(0, 2)
    gather(1)
    chain(0, 3)
    forward(2)
    chain(1, 0)
    forward(3)
    finish(0)
    chain(1, 1)
    chain(1, 2)
    gather(2)
    chain(2, 0)
    chain(1, 3)
    put(0)
    gather(3)
    chain(2, 1)
    chain(3, 0)
    chain(2, 2)
    chain(3, 1)
    finish(1)
    chain(3, 2)
    chain(2, 3)
    chain(3, 3)
    put(1)
    finish(2)
    finish(3)
    put(2)

    for dy in range(1, NY):
        order_copy(dy).wait_send()
    for piece in pieces:
        sent = sends[PIECES[piece][0]].at[0 : (SLOTS - 1) * piece_rows[piece]]
        pltpu.make_async_copy(sent, sent, spread_send.at[piece]).wait()
        if RELAYS:
            pltpu.make_async_copy(relay[piece], relay[piece], relay_send.at[piece]).wait()
        core_copy(piece).wait_send()
        for step in range(STEPS):
            for way in (1, -1):
                z_copy(piece, step, way).wait_send()
        for part in range(X_PART):
            xd, there, _ = final_copies(piece, part)

            @pl.when(xd != x)
            def _():
                pltpu.make_async_remote_copy(**there).wait_send()


def shards(psi, left_ops, right_ops, pair_src, widths):
    size = psi.shape[1]
    targets = pair_src.shape[1]
    rows, lanes = size // SLOTS, size // CHUNKS
    bf, count = jnp.bfloat16, len(PIECES)
    tile = (TILE, lanes)
    scratch = [
        pltpu.VMEM(psi.shape, bf),
        pltpu.VMEM(left_ops.shape, bf),
        pltpu.VMEM(right_ops.shape, bf),
        pltpu.VMEM((8, targets), jnp.int32),
        pltpu.VMEM((NY, 8, targets), jnp.int32),
        pltpu.VMEM((SECTORS_HERE, GROUPS_HERE * (size - lanes), size), bf),
        pltpu.VMEM((TILE, size, size - lanes), bf),
        pltpu.VMEM((TILE * TILE, TILE * TILE), bf),
        pltpu.VMEM((targets, SOURCES), bf),
        *[pltpu.VMEM((size,) + tile, bf) for _ in range(CHUNKS)],
    ]
    for _, _, thirds in PIECES:
        here = rows * thirds // 3
        ring = pltpu.VMEM((STEPS, here) + tile, bf)
        scratch += [
            pltpu.VMEM((here, SOURCES, lanes), bf),
            pltpu.VMEM((2, max(RELAYS, 1), here // 2) + tile, bf),
            pltpu.VMEM((NZ, here) + tile, bf),
            pltpu.VMEM((NZ, here) + tile, bf),
            pltpu.VMEM((NZ, here) + tile, jnp.float32),
            ring, ring, ring, ring,
            pltpu.VMEM((X_PART, here // 2) + tile, bf),
            pltpu.VMEM((X_PART, here // 2) + tile, bf),
            pltpu.VMEM((X_PART * here * SECTORS_HERE, SECTORS_HERE * LANES), bf),
        ]
    dma = pltpu.SemaphoreType.DMA
    scratch += [
        dma((3, SECTORS_HERE)), dma((1,)), dma((NY,)), dma((count,)), dma((count,)),
        dma((count, 2)), dma((count,)), dma((count,)), dma((count,)),
        dma((count, STEPS)), dma((count, STEPS)), dma((count, STEPS)), dma((count, STEPS)),
        dma((count, X_PART)), dma((count,)),
    ]
    return pl.pallas_call(
        kernel,
        out_shape=jax.ShapeDtypeStruct((SECTORS_HERE, size, X_PART * rows), jnp.float32),
        in_specs=[
            pl.BlockSpec(memory_space=pltpu.VMEM),
            pl.BlockSpec(memory_space=pltpu.SMEM),
            pl.BlockSpec(memory_space=pl.ANY),
            pl.BlockSpec(memory_space=pl.ANY),
            pl.BlockSpec(memory_space=pl.ANY),
        ],
        out_specs=pl.BlockSpec(memory_space=pltpu.VMEM),
        scratch_shapes=scratch,
        compiler_params=pltpu.CompilerParams(
            collective_id=0, has_side_effects=True, vmem_limit_bytes=56 * 1024 * 1024
        ),
        cost_estimate=pl.CostEstimate(
            flops=64 * size**3, bytes_accessed=40 * size * size * 2, transcendentals=0
        ),
    )(pair_src, widths, psi, left_ops, right_ops)


def solution(mesh):
    return jax.shard_map(
        shards,
        mesh=mesh,
        in_specs=(
            P("sec", None, None),
            P("term", "sec", None, None),
            P("term", "sec", None, None),
            P("term", None),
            P(None, "sec"),
        ),
        out_specs=P("sec", None, "term"),
        check_vma=False,
    )
```

```python
import jax
import jax.numpy as jnp
from jax import lax
from jax.experimental import pallas as pl
from jax.experimental.pallas import tpu as pltpu
from jax.sharding import PartitionSpec as P

NX, NY, NZ, NC = 4, 4, 8, 2
CHUNKS = 3
PIECES = ((0, 0, 3), (1, 0, 3), (2, 0, 2), (2, 2, 1))
SLOTS = NX * NY
GROUPS_HERE = 2
SECTORS_HERE = 8
TILE = GROUPS_HERE * SECTORS_HERE
SOURCES = SLOTS * TILE
X_PART = NX // NC
STEPS = NZ // 2
MESH = pl.DeviceIdType.MESH
BUFFERS = 10


def moves():
    every = [(dx, dy) for dx in range(NX) for dy in range(NY) if (dx, dy) != (0, 0)]
    return sorted(every, key=lambda move: -min(move[0], NX - move[0]) - min(move[1], NY - move[1]))


def device(x, y, z, c):
    return (x * NZ + z, y * NC + c)


def ones_where(condition):
    return jnp.where(condition, 1.0, 0.0).astype(jnp.bfloat16)


def tile_at(index):
    return pl.ds(pl.multiple_of(index * TILE, TILE), TILE)


def kernel(pair_src, widths, psi, left, right, out, *rest):
    psi_v, left_v, right_v, orders_own, orders, parts, image, swap, pick, *rest = rest
    sends, rest = rest[:CHUNKS], rest[CHUNKS:]
    buffers = [rest[i * BUFFERS : (i + 1) * BUFFERS] for i in range(len(PIECES))]
    (
        load_sem, order_sem, order_send, spread_send, spread_recv, core_send, core_recv,
        up_send, up_recv, down_send, down_recv, final_send, final_recv,
    ) = rest[len(PIECES) * BUFFERS :]
    got, give, take, own, up_out, up_in, down_out, down_in, done, final = zip(*buffers)
    sec, term = lax.axis_index("sec"), lax.axis_index("term")
    x, z = lax.div(sec, NZ), lax.rem(sec, NZ)
    y, c = lax.div(term, NC), lax.rem(term, NC)
    size = psi_v.shape[-1]
    rows = size // SLOTS
    lanes = size // CHUNKS
    targets = pair_src.shape[1]
    pieces = range(len(PIECES))
    y_order = sorted(range(NY), key=lambda dy: -min(dy, NY - dy))
    first_row = [rows * at // 3 for _, at, _ in PIECES]
    piece_rows = [rows * count // 3 for _, _, count in PIECES]

    def shifted(value, by, count):
        return lax.rem(value + (by % count), count)

    barrier = pltpu.get_barrier_semaphore()
    others = [device(shifted(x, dx, NX), shifted(y, dy, NY), z, c) for dx, dy in moves()]
    others += [device(shifted(x, dx, NX), y, z, 1 - c) for dx in range(NX)]
    others += [device(x, y, shifted(z, 1, NZ), c), device(x, y, shifted(z, -1, NZ), c)]
    for other in others:
        pl.semaphore_signal(barrier, inc=1, device_id=other, device_id_type=MESH)

    def loads(k):
        return (
            pltpu.make_async_copy(psi.at[k], psi_v.at[k], load_sem.at[0, k]),
            pltpu.make_async_copy(left.at[:, k], left_v.at[:, k], load_sem.at[1, k]),
            pltpu.make_async_copy(right.at[:, k], right_v.at[:, k], load_sem.at[2, k]),
        )

    for which in ((0, 1), (2,)):
        for k in range(SECTORS_HERE):
            for copy in which:
                loads(k)[copy].start()

    row = lax.broadcasted_iota(jnp.int32, swap.shape, 0)
    column = lax.broadcasted_iota(jnp.int32, swap.shape, 1)
    swap[...] = ones_where(row == (column & (TILE - 1)) * TILE + lax.shift_right_logical(column, 4))
    orders_own[...] = jnp.concatenate([pair_src[...], jnp.zeros((6, targets), jnp.int32)], 0)

    def image_of(right_block, part):
        return lax.dot_general(
            right_block, part, (((1,), (1,)), ((), ())), preferred_element_type=jnp.float32
        ).astype(jnp.bfloat16)

    def turned(block):
        return jnp.dot(swap[...], block, preferred_element_type=jnp.float32).astype(jnp.bfloat16)

    def each_sector(body):
        def some(step, _):
            for inner in range(2):
                body(step * 2 + inner)
            return 0

        lax.fori_loop(0, SECTORS_HERE // 2, some, 0)

    def first_parts():
        def one(k):
            for copy in loads(k)[:2]:
                copy.wait()
            keep = (lax.broadcasted_iota(jnp.int32, (size, size), 0) < widths[0, k]) & (
                lax.broadcasted_iota(jnp.int32, (size, size), 1) < widths[1, k]
            )
            masked = jnp.where(keep, psi_v[k].astype(jnp.float32), 0.0).astype(jnp.bfloat16)
            psi_v[k] = masked
            here = left_v[:, k, 0:lanes, :].reshape(GROUPS_HERE * lanes, size)
            parts[k, 0 : GROUPS_HERE * lanes] = jnp.dot(
                here, masked, preferred_element_type=jnp.float32
            ).astype(jnp.bfloat16)

        each_sector(one)

    def first_images(rings, first):
        count = size // NY
        starts = [pl.multiple_of(shifted(y, dy, NY) * count, 2 * TILE) for dy in rings]

        def one(k):
            if first:
                loads(k)[2].wait()
            for group in range(GROUPS_HERE):
                chosen = jnp.concatenate([right_v[group, k, pl.ds(start, count), :] for start in starts], 0)
                image[group * SECTORS_HERE + k, 0 : count * len(starts), 0:lanes] = image_of(
                    chosen, parts[k, group * lanes : (group + 1) * lanes, :]
                )

        each_sector(one)
        for low in range(0, count * len(starts), 2 * TILE):
            both = turned(
                jnp.concatenate(
                    [
                        image[:, at : at + TILE, 0:lanes].reshape(TILE * TILE, lanes)
                        for at in (low, low + TILE)
                    ],
                    1,
                )
            )
            for part in range(2):
                at = starts[low // count] + low % count + part * TILE
                sends[0][pl.ds(at, TILE)] = both[:, part * lanes : (part + 1) * lanes].reshape(
                    TILE, TILE, lanes
                )

    later = size - lanes

    def later_parts():
        def one(k):
            here = left_v[:, k, lanes:, :].reshape(GROUPS_HERE * later, size)
            parts[k] = jnp.dot(here, psi_v[k], preferred_element_type=jnp.float32).astype(jnp.bfloat16)

        each_sector(one)

    def later_images():
        def one(k):
            for group in range(GROUPS_HERE):
                image[group * SECTORS_HERE + k] = image_of(
                    right_v[group, k], parts[k, group * later : (group + 1) * later, :]
                )

        each_sector(one)

        def some(step, _):
            for inner in range(4):
                at = pl.multiple_of((step * 4 + inner) * TILE, TILE)
                value = turned(image[:, pl.ds(at, TILE), :].reshape(TILE * TILE, later))
                for chunk in range(1, CHUNKS):
                    sends[chunk][pl.ds(at, TILE)] = value[
                        :, (chunk - 1) * lanes : chunk * lanes
                    ].reshape(TILE, TILE, lanes)
            return 0

        lax.fori_loop(0, size // (4 * TILE), some, 0)

    def halves(piece):
        count = piece_rows[piece] // 2
        return ((1, 0, count), (-1, count, count))

    def block_for(piece, x_to, y_to, low, count):
        start = (y_to * NX + x_to) * rows + first_row[piece] + low
        return sends[PIECES[piece][0]].at[pl.ds(start, count)]

    def place(piece, x_from, y_from, low, count):
        return got[piece].at[low : low + count, tile_at(y_from * NX + x_from)]

    def spread(piece, rings=range(NY)):
        count = piece_rows[piece]
        for dx, dy in moves():
            if dy in rings:
                xd, yd = shifted(x, dx, NX), shifted(y, dy, NY)
                pltpu.make_async_remote_copy(
                    src_ref=block_for(piece, xd, yd, 0, count),
                    dst_ref=place(piece, x, y, 0, count),
                    send_sem=spread_send.at[piece],
                    recv_sem=spread_recv.at[piece],
                    device_id=device(xd, yd, z, c),
                    device_id_type=MESH,
                ).start()
        if 0 in rings:
            pltpu.make_async_copy(
                block_for(piece, x, y, 0, count), place(piece, x, y, 0, count), spread_recv.at[piece]
            ).start()

    def order_copy(dy):
        return pltpu.make_async_remote_copy(
            src_ref=orders_own,
            dst_ref=orders.at[y],
            send_sem=order_send.at[dy],
            recv_sem=order_sem.at[0],
            device_id=device(x, shifted(y, dy, NY), z, c),
            device_id_type=MESH,
        )

    def make_pick():
        pltpu.make_async_copy(orders, orders, order_sem.at[0]).wait()
        line = lax.broadcasted_iota(jnp.int32, (SECTORS_HERE, targets), 0)
        blocks = []
        for yy in range(NY):
            for xx in range(NX):
                for group in range(GROUPS_HERE):
                    wanted = orders[yy, group : group + 1, :]
                    first = (xx * NZ + z) * SECTORS_HERE
                    blocks.append(jnp.where(wanted == line + first, 1.0, 0.0))
        table = jnp.concatenate(blocks, 0).T
        half = targets // NC
        for xh in range(NC):
            blocks = []
            for zz in range(NZ):
                for part in range(X_PART):
                    low = ((xh * X_PART + part) * NZ + zz) * SECTORS_HERE
                    blocks.append(table[low : low + SECTORS_HERE])
            start = pl.multiple_of((1 - c if xh == 0 else c) * half, half)
            pick[pl.ds(start, half), :] = jnp.concatenate(blocks, 0).astype(jnp.bfloat16)

    def gather(piece):
        pltpu.make_async_copy(got[piece], got[piece], spread_recv.at[piece]).wait()
        half = targets // NC

        def some(step, _):
            for inner in range(4):
                m = step * 8 + inner * 2
                both = jnp.concatenate([got[piece][m], got[piece][m + 1]], 1)
                value = jnp.dot(pick[...], both, preferred_element_type=jnp.float32)
                for part, to in ((0, give[piece]), (1, own[piece])):
                    for zz in range(NZ):
                        low = part * half + zz * TILE
                        for next_m in range(2):
                            to[zz, m + next_m] = value[
                                low : low + TILE, next_m * lanes : (next_m + 1) * lanes
                            ].astype(to.dtype)
            return 0

        lax.fori_loop(0, piece_rows[piece] // 8, some, 0)
        core_copy(piece).start()

    def core_copy(piece):
        return pltpu.make_async_remote_copy(
            src_ref=give[piece],
            dst_ref=take[piece],
            send_sem=core_send.at[piece],
            recv_sem=core_recv.at[piece],
            device_id=device(x, y, z, 1 - c),
            device_id_type=MESH,
        )

    def held(piece, zd, low, count):
        at = slice(low, low + count)
        return own[piece][zd, at] + take[piece][zd, at].astype(jnp.float32)

    def z_buffers(piece, way):
        return (up_out[piece], up_in[piece]) if way > 0 else (down_out[piece], down_in[piece])

    def z_copy(piece, step, way):
        source, target = z_buffers(piece, way)
        out_sem, in_sem = (up_send, up_recv) if way > 0 else (down_send, down_recv)
        at = (step,)
        if step == 0:
            _, low, count = halves(piece)[0 if way > 0 else 1]
            at = (step, slice(low, low + count))
        return pltpu.make_async_remote_copy(
            src_ref=source.at[at],
            dst_ref=target.at[at],
            send_sem=out_sem.at[piece, step],
            recv_sem=in_sem.at[piece, step],
            device_id=device(x, y, shifted(z, way, NZ), c),
            device_id_type=MESH,
        )

    def carried(step, way, sign):
        return step > 0 or way == sign

    def chain(piece, step):
        if step >= STEPS:
            return
        if step == 0:
            core_copy(piece).wait_recv()
        for way in (1, -1):
            source, target = z_buffers(piece, way)
            if step > 0:
                z_copy(piece, step - 1, way).wait_recv()
            zd = shifted(z, way * (STEPS - step), NZ)
            for sign, low, count in halves(piece):
                if carried(step, way, sign):
                    at = slice(low, low + count)
                    value = held(piece, zd, low, count)
                    if step > 0 and carried(step - 1, way, sign):
                        value = value + target[step - 1, at].astype(jnp.float32)
                    source[step, at] = value.astype(jnp.bfloat16)
            z_copy(piece, step, way).start()

    def final_copies(piece, part):
        xd = c * X_PART + part
        spot_there = final[piece].at[lax.rem(x, X_PART)]
        there = dict(
            src_ref=done[piece].at[part],
            dst_ref=spot_there,
            send_sem=final_send.at[piece, part],
            recv_sem=final_recv.at[piece],
            device_id=device(xd, y, z, lax.div(x, X_PART)),
            device_id_type=MESH,
        )
        here = (done[piece].at[part], spot_there, final_recv.at[piece])
        return xd, there, here

    def finish(piece):
        last = STEPS - 1
        for way in (1, -1):
            z_copy(piece, last, way).wait_recv()
        for sign, low, count in halves(piece):
            value = held(piece, z, low, count)
            for way in (1, -1):
                if carried(last, way, sign):
                    value = value + z_buffers(piece, way)[1][last, low : low + count].astype(jnp.float32)
            for part in range(X_PART):
                at = slice(part * SECTORS_HERE, (part + 1) * SECTORS_HERE)
                done[piece][part, low // 2 : (low + count) // 2] = (
                    value[:, at, :].reshape(count // 2, TILE, lanes).astype(jnp.bfloat16)
                )
        for part in range(X_PART):
            xd, there, here = final_copies(piece, part)

            @pl.when(xd != x)
            def _():
                pltpu.make_async_remote_copy(**there).start()

            @pl.when(xd == x)
            def _():
                pltpu.make_async_copy(*here).start()

    def put(piece):
        pltpu.make_async_copy(final[piece], final[piece], final_recv.at[piece]).wait()
        chunk, count = PIECES[piece][0], piece_rows[piece]
        total = X_PART * count * SECTORS_HERE
        row = lax.broadcasted_iota(jnp.int32, (total, total), 0)
        column = lax.broadcasted_iota(jnp.int32, (total, total), 1)
        sector = column & (SECTORS_HERE - 1)
        line = lax.shift_right_logical(column, 3)
        value = jnp.dot(
            ones_where(row == sector * (X_PART * count) + line),
            final[piece][...].reshape(total, lanes),
            preferred_element_type=jnp.float32,
        )
        for sector in range(SECTORS_HERE):
            for part in range(X_PART):
                low = part * rows + first_row[piece]
                start = (sector * X_PART + part) * count
                out[sector, low : low + count, chunk * lanes : (chunk + 1) * lanes] = value[
                    start : start + count
                ]

    first_parts()
    for part in range(2):
        rings = y_order[part * NY // 2 : (part + 1) * NY // 2]
        first_images(rings, part == 0)
        if part == 0:
            pl.semaphore_wait(barrier, len(others))
        spread(0, rings)
    for dy in range(1, NY):
        order_copy(dy).start()
    pltpu.make_async_copy(orders_own, orders.at[y], order_sem.at[0]).start()
    later_parts()
    later_images()
    spread(1)
    spread(2)
    spread(3)
    make_pick()
    gather(0)
    chain(0, 0)
    chain(0, 1)
    chain(0, 2)
    chain(0, 3)
    finish(0)
    gather(1)
    chain(1, 0)
    chain(1, 1)
    put(0)
    chain(1, 2)
    gather(2)
    chain(2, 0)
    chain(1, 3)
    gather(3)
    chain(2, 1)
    chain(3, 0)
    chain(2, 2)
    chain(3, 1)
    finish(1)
    chain(3, 2)
    chain(2, 3)
    chain(3, 3)
    put(1)
    finish(2)
    finish(3)
    put(2)
    put(3)

    for dy in range(1, NY):
        order_copy(dy).wait_send()
    for piece in pieces:
        sent = sends[PIECES[piece][0]].at[0 : (SLOTS - 1) * piece_rows[piece]]
        pltpu.make_async_copy(sent, sent, spread_send.at[piece]).wait()
        core_copy(piece).wait_send()
        for step in range(STEPS):
            for way in (1, -1):
                z_copy(piece, step, way).wait_send()
        for part in range(X_PART):
            xd, there, _ = final_copies(piece, part)

            @pl.when(xd != x)
            def _():
                pltpu.make_async_remote_copy(**there).wait_send()


def shards(psi, left_ops, right_ops, pair_src, widths):
    size = psi.shape[1]
    targets = pair_src.shape[1]
    rows, lanes = size // SLOTS, size // CHUNKS
    term = lax.axis_index("term")
    bf, count = jnp.bfloat16, len(PIECES)
    tile = (TILE, lanes)
    scratch = [
        pltpu.VMEM(psi.shape, bf),
        pltpu.VMEM(left_ops.shape, bf),
        pltpu.VMEM(right_ops.shape, bf),
        pltpu.VMEM((8, targets), jnp.int32),
        pltpu.VMEM((NY, 8, targets), jnp.int32),
        pltpu.VMEM((SECTORS_HERE, GROUPS_HERE * (size - lanes), size), bf),
        pltpu.VMEM((TILE, size, size - lanes), bf),
        pltpu.VMEM((TILE * TILE, TILE * TILE), bf),
        pltpu.VMEM((targets, SOURCES), bf),
        *[pltpu.VMEM((size,) + tile, bf) for _ in range(CHUNKS)],
    ]
    for _, _, thirds in PIECES:
        here = rows * thirds // 3
        ring = pltpu.VMEM((STEPS, here) + tile, bf)
        scratch += [
            pltpu.VMEM((here, SOURCES, lanes), bf),
            pltpu.VMEM((NZ, here) + tile, bf),
            pltpu.VMEM((NZ, here) + tile, bf),
            pltpu.VMEM((NZ, here) + tile, jnp.float32),
            ring, ring, ring, ring,
            pltpu.VMEM((X_PART, here // 2) + tile, bf),
            pltpu.VMEM((X_PART, here // 2) + tile, bf),
        ]
    dma = pltpu.SemaphoreType.DMA
    scratch += [
        dma((3, SECTORS_HERE)), dma((1,)), dma((NY,)), dma((count,)), dma((count,)),
        dma((count,)), dma((count,)),
        dma((count, STEPS)), dma((count, STEPS)), dma((count, STEPS)), dma((count, STEPS)),
        dma((count, X_PART)), dma((count,)),
    ]
    summed = pl.pallas_call(
        kernel,
        out_shape=jax.ShapeDtypeStruct((SECTORS_HERE, X_PART * rows, size), jnp.float32),
        in_specs=[
            pl.BlockSpec(memory_space=pltpu.VMEM),
            pl.BlockSpec(memory_space=pltpu.SMEM),
            pl.BlockSpec(memory_space=pl.ANY),
            pl.BlockSpec(memory_space=pl.ANY),
            pl.BlockSpec(memory_space=pl.ANY),
        ],
        out_specs=pl.BlockSpec(memory_space=pltpu.VMEM),
        scratch_shapes=scratch,
        compiler_params=pltpu.CompilerParams(
            collective_id=0, has_side_effects=True, vmem_limit_bytes=56 * 1024 * 1024
        ),
        cost_estimate=pl.CostEstimate(
            flops=64 * size**3, bytes_accessed=40 * size * size * 2, transcendentals=0
        ),
    )(pair_src, widths, psi, left_ops, right_ops)

    summed = jnp.swapaxes(summed, 1, 2)
    line = jnp.arange(size, dtype=jnp.int32)
    columns = term * (X_PART * rows) + jnp.arange(X_PART * rows, dtype=jnp.int32)
    keep = (line[None, :, None] < widths[0][:, None, None]) & (
        columns[None, None, :] < widths[1][:, None, None]
    )
    return jnp.where(keep, summed, jnp.zeros_like(summed))


def solution(mesh):
    return jax.shard_map(
        shards,
        mesh=mesh,
        in_specs=(
            P("sec", None, None),
            P("term", "sec", None, None),
            P("term", "sec", None, None),
            P("term", None),
            P(None, "sec"),
        ),
        out_specs=P("sec", None, "term"),
        check_vma=False,
    )
```

```python
import jax
import jax.numpy as jnp
from jax import lax
from jax.experimental import pallas as pl
from jax.experimental.pallas import tpu as pltpu
from jax.sharding import PartitionSpec as P

NX, NY, NZ, NC = 4, 4, 8, 2
CHUNKS = 3
PIECES = ((0, 0, 3), (1, 0, 3), (2, 0, 2), (2, 2, 1))
SLOTS = NX * NY
GROUPS_HERE = 2
SECTORS_HERE = 8
TILE = GROUPS_HERE * SECTORS_HERE
SOURCES = SLOTS * TILE
X_PART = NX // NC
STEPS = NZ // 2
MESH = pl.DeviceIdType.MESH
BUFFERS = 11


def places():
    found = []
    for dx in range(NX):
        for dy in range(NY):
            if (dx, dy) != (0, 0):
                found.append((dx, dy, NX > 2 and dx == NX // 2, NY > 2 and dy == NY // 2))
    return sorted(found, key=lambda at: -min(at[0], NX - at[0]) - min(at[1], NY - at[1]))


def relayed():
    found = []
    for dx, dy, far_x, far_y in places():
        if far_x or far_y:
            via = (1 if far_x else 0, 1 if far_y else 0)
            found.append(((dx, dy), via, (dx - via[0], dy - via[1])))
    return found


RELAYS = len(relayed())


def device(x, y, z, c):
    return (x * NZ + z, y * NC + c)


def ones_where(condition):
    return jnp.where(condition, 1.0, 0.0).astype(jnp.bfloat16)


def tile_at(index):
    return pl.ds(pl.multiple_of(index * TILE, TILE), TILE)


def kernel(pair_src, widths, psi, left, right, out, *rest):
    psi_v, left_v, right_v, orders_own, orders, parts, image, swap, pick, *rest = rest
    sends, rest = rest[:CHUNKS], rest[CHUNKS:]
    buffers = [rest[i * BUFFERS : (i + 1) * BUFFERS] for i in range(len(PIECES))]
    (
        load_sem, order_sem, order_send, spread_send, spread_recv, relay_recv, relay_send, core_send, core_recv,
        up_send, up_recv, down_send, down_recv, final_send, final_recv,
    ) = rest[len(PIECES) * BUFFERS :]
    got, relay, give, take, own, up_out, up_in, down_out, down_in, done, final = zip(*buffers)
    sec, term = lax.axis_index("sec"), lax.axis_index("term")
    x, z = lax.div(sec, NZ), lax.rem(sec, NZ)
    y, c = lax.div(term, NC), lax.rem(term, NC)
    size = psi_v.shape[-1]
    rows = size // SLOTS
    lanes = size // CHUNKS
    targets = pair_src.shape[1]
    pieces = range(len(PIECES))
    y_order = sorted(range(NY), key=lambda dy: -min(dy, NY - dy))
    first_row = [rows * at // 3 for _, at, _ in PIECES]
    piece_rows = [rows * count // 3 for _, _, count in PIECES]

    def shifted(value, by, count):
        return lax.rem(value + (by % count), count)

    barrier = pltpu.get_barrier_semaphore()
    others = [device(shifted(x, dx, NX), shifted(y, dy, NY), z, c) for dx, dy, _, _ in places()]
    others += [device(shifted(x, dx, NX), y, z, 1 - c) for dx in range(NX)]
    others += [device(x, y, shifted(z, 1, NZ), c), device(x, y, shifted(z, -1, NZ), c)]
    for other in others:
        pl.semaphore_signal(barrier, inc=1, device_id=other, device_id_type=MESH)

    def loads(k):
        return (
            pltpu.make_async_copy(psi.at[k], psi_v.at[k], load_sem.at[0, k]),
            pltpu.make_async_copy(left.at[:, k], left_v.at[:, k], load_sem.at[1, k]),
            pltpu.make_async_copy(right.at[:, k], right_v.at[:, k], load_sem.at[2, k]),
        )

    for which in ((0, 1), (2,)):
        for k in range(SECTORS_HERE):
            for copy in which:
                loads(k)[copy].start()

    row = lax.broadcasted_iota(jnp.int32, swap.shape, 0)
    column = lax.broadcasted_iota(jnp.int32, swap.shape, 1)
    swap[...] = ones_where(row == (column & (TILE - 1)) * TILE + lax.shift_right_logical(column, 4))
    orders_own[...] = jnp.concatenate([pair_src[...], jnp.zeros((6, targets), jnp.int32)], 0)

    def image_of(right_block, part):
        return lax.dot_general(
            right_block, part, (((1,), (1,)), ((), ())), preferred_element_type=jnp.float32
        ).astype(jnp.bfloat16)

    def turned(block):
        return jnp.dot(swap[...], block, preferred_element_type=jnp.float32).astype(jnp.bfloat16)

    def each_sector(body):
        def some(step, _):
            for inner in range(2):
                body(step * 2 + inner)
            return 0

        lax.fori_loop(0, SECTORS_HERE // 2, some, 0)

    def first_parts():
        def one(k):
            for copy in loads(k)[:2]:
                copy.wait()
            keep = (lax.broadcasted_iota(jnp.int32, (size, size), 0) < widths[0, k]) & (
                lax.broadcasted_iota(jnp.int32, (size, size), 1) < widths[1, k]
            )
            masked = jnp.where(keep, psi_v[k].astype(jnp.float32), 0.0).astype(jnp.bfloat16)
            psi_v[k] = masked
            here = left_v[:, k, 0:lanes, :].reshape(GROUPS_HERE * lanes, size)
            parts[k, 0 : GROUPS_HERE * lanes] = jnp.dot(
                here, masked, preferred_element_type=jnp.float32
            ).astype(jnp.bfloat16)

        each_sector(one)

    later = size - lanes

    def later_parts():
        def one(k):
            here = left_v[:, k, lanes:, :].reshape(GROUPS_HERE * later, size)
            parts[k] = jnp.dot(here, psi_v[k], preferred_element_type=jnp.float32).astype(jnp.bfloat16)

        each_sector(one)

    def images(rings, chunks, wait):
        count = size // NY
        width = lanes * len(chunks)
        starts = [pl.multiple_of(shifted(y, dy, NY) * count, 2 * TILE) for dy in rings]

        def one(k):
            if wait:
                loads(k)[2].wait()
            for group in range(GROUPS_HERE):
                chosen = jnp.concatenate([right_v[group, k, pl.ds(start, count), :] for start in starts], 0)
                image[group * SECTORS_HERE + k, 0 : count * len(starts), 0:width] = image_of(
                    chosen, parts[k, group * width : (group + 1) * width, :]
                )

        each_sector(one)
        step = 2 // len(chunks)
        for low in range(0, count * len(starts), step * TILE):
            blocks = [
                image[:, low + part * TILE : low + (part + 1) * TILE, 0:width].reshape(TILE * TILE, width)
                for part in range(step)
            ]
            value = turned(blocks[0] if step == 1 else jnp.concatenate(blocks, 1))
            for part in range(2):
                at = starts[low // count] + low % count + (part * TILE if step == 2 else 0)
                sends[chunks[0 if step == 2 else part]][pl.ds(at, TILE)] = value[
                    :, part * lanes : (part + 1) * lanes
                ].reshape(TILE, TILE, lanes)

    def halves(piece):
        count = piece_rows[piece] // 2
        return ((1, 0, count), (-1, count, count))

    def block_for(piece, x_to, y_to, low, count):
        start = (y_to * NX + x_to) * rows + first_row[piece] + low
        return sends[PIECES[piece][0]].at[pl.ds(start, count)]

    def place(piece, x_from, y_from, low, count):
        return got[piece].at[low : low + count, tile_at(y_from * NX + x_from)]

    def spread(piece, rings=range(NY)):
        count = piece_rows[piece]
        for j, ((dx, dy), (vx, vy), _) in enumerate(relayed()):
            if dy in rings:
                pltpu.make_async_remote_copy(
                    src_ref=block_for(
                        piece, shifted(x, dx, NX), shifted(y, dy, NY), count // 2, count // 2
                    ),
                    dst_ref=relay[piece].at[j],
                    send_sem=spread_send.at[piece],
                    recv_sem=relay_recv.at[piece],
                    device_id=device(shifted(x, vx, NX), shifted(y, vy, NY), z, c),
                    device_id_type=MESH,
                ).start()
        for dx, dy, far_x, far_y in places():
            if dy in rings:
                xd, yd = shifted(x, dx, NX), shifted(y, dy, NY)
                straight = count // 2 if far_x or far_y else count
                pltpu.make_async_remote_copy(
                    src_ref=block_for(piece, xd, yd, 0, straight),
                    dst_ref=place(piece, x, y, 0, straight),
                    send_sem=spread_send.at[piece],
                    recv_sem=spread_recv.at[piece],
                    device_id=device(xd, yd, z, c),
                    device_id_type=MESH,
                ).start()
        if 0 in rings:
            pltpu.make_async_copy(
                block_for(piece, x, y, 0, count), place(piece, x, y, 0, count), spread_recv.at[piece]
            ).start()

    def forward(piece):
        if RELAYS == 0:
            return
        count = piece_rows[piece] // 2
        pltpu.make_async_copy(relay[piece], relay[piece], relay_recv.at[piece]).wait()
        for j, (_, (vx, vy), (fx, fy)) in enumerate(relayed()):
            pltpu.make_async_remote_copy(
                src_ref=relay[piece].at[j],
                dst_ref=place(piece, shifted(x, -vx, NX), shifted(y, -vy, NY), count, count),
                send_sem=relay_send.at[piece],
                recv_sem=spread_recv.at[piece],
                device_id=device(shifted(x, fx, NX), shifted(y, fy, NY), z, c),
                device_id_type=MESH,
            ).start()

    def order_copy(dy):
        return pltpu.make_async_remote_copy(
            src_ref=orders_own,
            dst_ref=orders.at[y],
            send_sem=order_send.at[dy],
            recv_sem=order_sem.at[0],
            device_id=device(x, shifted(y, dy, NY), z, c),
            device_id_type=MESH,
        )

    def make_pick():
        pltpu.make_async_copy(orders, orders, order_sem.at[0]).wait()
        line = lax.broadcasted_iota(jnp.int32, (SECTORS_HERE, targets), 0)
        blocks = []
        for yy in range(NY):
            for xx in range(NX):
                for group in range(GROUPS_HERE):
                    wanted = orders[yy, group : group + 1, :]
                    first = (xx * NZ + z) * SECTORS_HERE
                    blocks.append(jnp.where(wanted == line + first, 1.0, 0.0))
        table = jnp.concatenate(blocks, 0).T
        half = targets // NC
        for xh in range(NC):
            blocks = []
            for zz in range(NZ):
                for part in range(X_PART):
                    low = ((xh * X_PART + part) * NZ + zz) * SECTORS_HERE
                    blocks.append(table[low : low + SECTORS_HERE])
            start = pl.multiple_of((1 - c if xh == 0 else c) * half, half)
            pick[pl.ds(start, half), :] = jnp.concatenate(blocks, 0).astype(jnp.bfloat16)

    def gather(piece):
        pltpu.make_async_copy(got[piece], got[piece], spread_recv.at[piece]).wait()
        half = targets // NC

        def some(step, _):
            for inner in range(4):
                m = step * 8 + inner * 2
                both = jnp.concatenate([got[piece][m], got[piece][m + 1]], 1)
                value = jnp.dot(pick[...], both, preferred_element_type=jnp.float32)
                for part, to in ((0, give[piece]), (1, own[piece])):
                    for zz in range(NZ):
                        low = part * half + zz * TILE
                        for next_m in range(2):
                            to[zz, m + next_m] = value[
                                low : low + TILE, next_m * lanes : (next_m + 1) * lanes
                            ].astype(to.dtype)
            return 0

        lax.fori_loop(0, piece_rows[piece] // 8, some, 0)
        core_copy(piece).start()

    def core_copy(piece):
        return pltpu.make_async_remote_copy(
            src_ref=give[piece],
            dst_ref=take[piece],
            send_sem=core_send.at[piece],
            recv_sem=core_recv.at[piece],
            device_id=device(x, y, z, 1 - c),
            device_id_type=MESH,
        )

    def held(piece, zd, low, count):
        at = slice(low, low + count)
        return own[piece][zd, at] + take[piece][zd, at].astype(jnp.float32)

    def z_buffers(piece, way):
        return (up_out[piece], up_in[piece]) if way > 0 else (down_out[piece], down_in[piece])

    def z_copy(piece, step, way):
        source, target = z_buffers(piece, way)
        out_sem, in_sem = (up_send, up_recv) if way > 0 else (down_send, down_recv)
        at = (step,)
        if step == 0:
            _, low, count = halves(piece)[0 if way > 0 else 1]
            at = (step, slice(low, low + count))
        return pltpu.make_async_remote_copy(
            src_ref=source.at[at],
            dst_ref=target.at[at],
            send_sem=out_sem.at[piece, step],
            recv_sem=in_sem.at[piece, step],
            device_id=device(x, y, shifted(z, way, NZ), c),
            device_id_type=MESH,
        )

    def carried(step, way, sign):
        return step > 0 or way == sign

    def chain(piece, step):
        if step >= STEPS:
            return
        if step == 0:
            core_copy(piece).wait_recv()
        for way in (1, -1):
            source, target = z_buffers(piece, way)
            if step > 0:
                z_copy(piece, step - 1, way).wait_recv()
            zd = shifted(z, way * (STEPS - step), NZ)
            for sign, low, count in halves(piece):
                if carried(step, way, sign):
                    at = slice(low, low + count)
                    value = held(piece, zd, low, count)
                    if step > 0 and carried(step - 1, way, sign):
                        value = value + target[step - 1, at].astype(jnp.float32)
                    source[step, at] = value.astype(jnp.bfloat16)
            z_copy(piece, step, way).start()

    def final_copies(piece, part):
        xd = c * X_PART + part
        spot_there = final[piece].at[lax.rem(x, X_PART)]
        there = dict(
            src_ref=done[piece].at[part],
            dst_ref=spot_there,
            send_sem=final_send.at[piece, part],
            recv_sem=final_recv.at[piece],
            device_id=device(xd, y, z, lax.div(x, X_PART)),
            device_id_type=MESH,
        )
        here = (done[piece].at[part], spot_there, final_recv.at[piece])
        return xd, there, here

    def finish(piece):
        last = STEPS - 1
        for way in (1, -1):
            z_copy(piece, last, way).wait_recv()
        for sign, low, count in halves(piece):
            value = held(piece, z, low, count)
            for way in (1, -1):
                if carried(last, way, sign):
                    value = value + z_buffers(piece, way)[1][last, low : low + count].astype(jnp.float32)
            for part in range(X_PART):
                at = slice(part * SECTORS_HERE, (part + 1) * SECTORS_HERE)
                done[piece][part, low // 2 : (low + count) // 2] = (
                    value[:, at, :].reshape(count // 2, TILE, lanes).astype(jnp.bfloat16)
                )
        for part in range(X_PART):
            xd, there, here = final_copies(piece, part)

            @pl.when(xd != x)
            def _():
                pltpu.make_async_remote_copy(**there).start()

            @pl.when(xd == x)
            def _():
                pltpu.make_async_copy(*here).start()

    def put(piece):
        pltpu.make_async_copy(final[piece], final[piece], final_recv.at[piece]).wait()
        chunk, count = PIECES[piece][0], piece_rows[piece]
        total = X_PART * count * SECTORS_HERE
        row = lax.broadcasted_iota(jnp.int32, (total, total), 0)
        column = lax.broadcasted_iota(jnp.int32, (total, total), 1)
        sector = column & (SECTORS_HERE - 1)
        line = lax.shift_right_logical(column, 3)
        value = jnp.dot(
            ones_where(row == sector * (X_PART * count) + line),
            final[piece][...].reshape(total, lanes),
            preferred_element_type=jnp.float32,
        )
        for sector in range(SECTORS_HERE):
            for part in range(X_PART):
                low = part * rows + first_row[piece]
                start = (sector * X_PART + part) * count
                out[sector, low : low + count, chunk * lanes : (chunk + 1) * lanes] = value[
                    start : start + count
                ]

    first_parts()
    ring_halves = (y_order[: NY // 2], y_order[NY // 2 :])
    for rings in ring_halves:
        images(rings, (0,), rings is ring_halves[0])
        if rings is ring_halves[0]:
            pl.semaphore_wait(barrier, len(others))
        spread(0, rings)
    for dy in range(1, NY):
        order_copy(dy).start()
    pltpu.make_async_copy(orders_own, orders.at[y], order_sem.at[0]).start()
    later_parts()
    forward(0)
    for rings in ring_halves:
        images(rings, (1, 2), False)
        spread(1, rings)
    make_pick()
    gather(0)
    forward(1)
    spread(2)
    chain(0, 0)
    chain(0, 1)
    spread(3)
    chain(0, 2)
    gather(1)
    chain(0, 3)
    forward(2)
    chain(1, 0)
    forward(3)
    finish(0)
    chain(1, 1)
    put(0)
    chain(1, 2)
    gather(2)
    chain(2, 0)
    chain(1, 3)
    gather(3)
    chain(2, 1)
    chain(3, 0)
    chain(2, 2)
    chain(3, 1)
    finish(1)
    chain(3, 2)
    chain(2, 3)
    chain(3, 3)
    put(1)
    finish(2)
    finish(3)
    put(2)
    put(3)

    for dy in range(1, NY):
        order_copy(dy).wait_send()
    for piece in pieces:
        sent = sends[PIECES[piece][0]].at[0 : (SLOTS - 1) * piece_rows[piece]]
        pltpu.make_async_copy(sent, sent, spread_send.at[piece]).wait()
        if RELAYS:
            pltpu.make_async_copy(relay[piece], relay[piece], relay_send.at[piece]).wait()
        core_copy(piece).wait_send()
        for step in range(STEPS):
            for way in (1, -1):
                z_copy(piece, step, way).wait_send()
        for part in range(X_PART):
            xd, there, _ = final_copies(piece, part)

            @pl.when(xd != x)
            def _():
                pltpu.make_async_remote_copy(**there).wait_send()


def shards(psi, left_ops, right_ops, pair_src, widths):
    size = psi.shape[1]
    targets = pair_src.shape[1]
    rows, lanes = size // SLOTS, size // CHUNKS
    term = lax.axis_index("term")
    bf, count = jnp.bfloat16, len(PIECES)
    tile = (TILE, lanes)
    scratch = [
        pltpu.VMEM(psi.shape, bf),
        pltpu.VMEM(left_ops.shape, bf),
        pltpu.VMEM(right_ops.shape, bf),
        pltpu.VMEM((8, targets), jnp.int32),
        pltpu.VMEM((NY, 8, targets), jnp.int32),
        pltpu.VMEM((SECTORS_HERE, GROUPS_HERE * (size - lanes), size), bf),
        pltpu.VMEM((TILE, size, size - lanes), bf),
        pltpu.VMEM((TILE * TILE, TILE * TILE), bf),
        pltpu.VMEM((targets, SOURCES), bf),
        *[pltpu.VMEM((size,) + tile, bf) for _ in range(CHUNKS)],
    ]
    for _, _, thirds in PIECES:
        here = rows * thirds // 3
        ring = pltpu.VMEM((STEPS, here) + tile, bf)
        scratch += [
            pltpu.VMEM((here, SOURCES, lanes), bf),
            pltpu.VMEM((max(RELAYS, 1), here // 2) + tile, bf),
            pltpu.VMEM((NZ, here) + tile, bf),
            pltpu.VMEM((NZ, here) + tile, bf),
            pltpu.VMEM((NZ, here) + tile, jnp.float32),
            ring, ring, ring, ring,
            pltpu.VMEM((X_PART, here // 2) + tile, bf),
            pltpu.VMEM((X_PART, here // 2) + tile, bf),
        ]
    dma = pltpu.SemaphoreType.DMA
    scratch += [
        dma((3, SECTORS_HERE)), dma((1,)), dma((NY,)), dma((count,)), dma((count,)),
        dma((count,)), dma((count,)), dma((count,)), dma((count,)),
        dma((count, STEPS)), dma((count, STEPS)), dma((count, STEPS)), dma((count, STEPS)),
        dma((count, X_PART)), dma((count,)),
    ]
    summed = pl.pallas_call(
        kernel,
        out_shape=jax.ShapeDtypeStruct((SECTORS_HERE, X_PART * rows, size), jnp.float32),
        in_specs=[
            pl.BlockSpec(memory_space=pltpu.VMEM),
            pl.BlockSpec(memory_space=pltpu.SMEM),
            pl.BlockSpec(memory_space=pl.ANY),
            pl.BlockSpec(memory_space=pl.ANY),
            pl.BlockSpec(memory_space=pl.ANY),
        ],
        out_specs=pl.BlockSpec(memory_space=pltpu.VMEM),
        scratch_shapes=scratch,
        compiler_params=pltpu.CompilerParams(
            collective_id=0, has_side_effects=True, vmem_limit_bytes=56 * 1024 * 1024
        ),
        cost_estimate=pl.CostEstimate(
            flops=64 * size**3, bytes_accessed=40 * size * size * 2, transcendentals=0
        ),
    )(pair_src, widths, psi, left_ops, right_ops)

    summed = jnp.swapaxes(summed, 1, 2)
    line = jnp.arange(size, dtype=jnp.int32)
    columns = term * (X_PART * rows) + jnp.arange(X_PART * rows, dtype=jnp.int32)
    keep = (line[None, :, None] < widths[0][:, None, None]) & (
        columns[None, None, :] < widths[1][:, None, None]
    )
    return jnp.where(keep, summed, jnp.zeros_like(summed))


def solution(mesh):
    return jax.shard_map(
        shards,
        mesh=mesh,
        in_specs=(
            P("sec", None, None),
            P("term", "sec", None, None),
            P("term", "sec", None, None),
            P("term", None),
            P(None, "sec"),
        ),
        out_specs=P("sec", None, "term"),
        check_vma=False,
    )
```

```python
import jax
import jax.numpy as jnp
from jax import lax
from jax.experimental import pallas as pl
from jax.experimental.pallas import tpu as pltpu
from jax.sharding import PartitionSpec as P

NX, NY, NZ, NC = 4, 4, 8, 2
CHUNKS = 3
PIECES = ((0, 0, 3), (1, 0, 3), (2, 0, 2), (2, 2, 1))
SLOTS = NX * NY
GROUPS_HERE = 2
SECTORS_HERE = 8
TILE = GROUPS_HERE * SECTORS_HERE
SOURCES = SLOTS * TILE
X_PART = NX // NC
STEPS = NZ // 2
MESH = pl.DeviceIdType.MESH
BUFFERS = 11


def routes(sign):
    direct, relayed = [], []
    for dx in range(NX):
        for dy in range(NY):
            far_x, far_y = NX > 2 and dx == NX // 2, NY > 2 and dy == NY // 2
            if far_x or far_y:
                via = (sign if far_x else 0, sign if far_y else 0)
                relayed.append(((dx, dy), via, (dx - via[0], dy - via[1])))
            elif (dx, dy) != (0, 0):
                direct.append((dx, dy))
    return direct, relayed


RELAYS = len(routes(1)[1])


def device(x, y, z, c):
    return (x * NZ + z, y * NC + c)


def ones_where(condition):
    return jnp.where(condition, 1.0, 0.0).astype(jnp.bfloat16)


def tile_at(index):
    return pl.ds(pl.multiple_of(index * TILE, TILE), TILE)


def kernel(pair_src, widths, psi, left, right, out, *rest):
    psi_v, left_v, right_v, orders_own, orders, parts, image, swap, pick, *rest = rest
    sends, rest = rest[:CHUNKS], rest[CHUNKS:]
    buffers = [rest[i * BUFFERS : (i + 1) * BUFFERS] for i in range(len(PIECES))]
    (
        load_sem, order_sem, order_send, spread_send, spread_recv, relay_recv, relay_send, core_send, core_recv,
        up_send, up_recv, down_send, down_recv, final_send, final_recv,
    ) = rest[len(PIECES) * BUFFERS :]
    got, relay, give, take, own, up_out, up_in, down_out, down_in, done, final = zip(*buffers)
    sec, term = lax.axis_index("sec"), lax.axis_index("term")
    x, z = lax.div(sec, NZ), lax.rem(sec, NZ)
    y, c = lax.div(term, NC), lax.rem(term, NC)
    size = psi_v.shape[-1]
    rows = size // SLOTS
    lanes = size // CHUNKS
    targets = pair_src.shape[1]
    pieces = range(len(PIECES))
    y_order = sorted(range(NY), key=lambda dy: -min(dy, NY - dy))
    first_row = [rows * at // 3 for _, at, _ in PIECES]
    piece_rows = [rows * count // 3 for _, _, count in PIECES]

    def shifted(value, by, count):
        return lax.rem(value + (by % count), count)

    barrier = pltpu.get_barrier_semaphore()
    others = [
        device(shifted(x, dx, NX), shifted(y, dy, NY), z, c)
        for dx in range(NX)
        for dy in range(NY)
        if (dx, dy) != (0, 0)
    ]
    others += [device(shifted(x, dx, NX), y, z, 1 - c) for dx in range(NX)]
    others += [device(x, y, shifted(z, 1, NZ), c), device(x, y, shifted(z, -1, NZ), c)]
    for other in others:
        pl.semaphore_signal(barrier, inc=1, device_id=other, device_id_type=MESH)

    def loads(k):
        return (
            pltpu.make_async_copy(psi.at[k], psi_v.at[k], load_sem.at[0, k]),
            pltpu.make_async_copy(left.at[:, k], left_v.at[:, k], load_sem.at[1, k]),
            pltpu.make_async_copy(right.at[:, k], right_v.at[:, k], load_sem.at[2, k]),
        )

    for which in ((0, 1), (2,)):
        for k in range(SECTORS_HERE):
            for copy in which:
                loads(k)[copy].start()

    row = lax.broadcasted_iota(jnp.int32, swap.shape, 0)
    column = lax.broadcasted_iota(jnp.int32, swap.shape, 1)
    swap[...] = ones_where(row == (column & (TILE - 1)) * TILE + lax.shift_right_logical(column, 4))
    orders_own[...] = jnp.concatenate([pair_src[...], jnp.zeros((6, targets), jnp.int32)], 0)

    def image_of(right_block, part):
        return lax.dot_general(
            right_block, part, (((1,), (1,)), ((), ())), preferred_element_type=jnp.float32
        ).astype(jnp.bfloat16)

    def turned(block):
        return jnp.dot(swap[...], block, preferred_element_type=jnp.float32).astype(jnp.bfloat16)

    def each_sector(body):
        def some(step, _):
            for inner in range(2):
                body(step * 2 + inner)
            return 0

        lax.fori_loop(0, SECTORS_HERE // 2, some, 0)

    def first_parts():
        def one(k):
            for copy in loads(k)[:2]:
                copy.wait()
            keep = (lax.broadcasted_iota(jnp.int32, (size, size), 0) < widths[0, k]) & (
                lax.broadcasted_iota(jnp.int32, (size, size), 1) < widths[1, k]
            )
            masked = jnp.where(keep, psi_v[k].astype(jnp.float32), 0.0).astype(jnp.bfloat16)
            psi_v[k] = masked
            here = left_v[:, k, 0:lanes, :].reshape(GROUPS_HERE * lanes, size)
            parts[k, 0 : GROUPS_HERE * lanes] = jnp.dot(
                here, masked, preferred_element_type=jnp.float32
            ).astype(jnp.bfloat16)

        each_sector(one)

    later = size - lanes

    def later_parts():
        def one(k):
            here = left_v[:, k, lanes:, :].reshape(GROUPS_HERE * later, size)
            parts[k] = jnp.dot(here, psi_v[k], preferred_element_type=jnp.float32).astype(jnp.bfloat16)

        each_sector(one)

    def images(chunk):
        def one(k):
            if chunk == 0:
                loads(k)[2].wait()
            for group in range(GROUPS_HERE):
                low = group * lanes if chunk == 0 else group * later + (chunk - 1) * lanes
                image[group * SECTORS_HERE + k] = image_of(
                    right_v[group, k], parts[k, low : low + lanes, :]
                )

        each_sector(one)

    def turn(chunk, rings):
        count = size // NY
        for dy in rings:
            start = shifted(y, dy, NY) * count
            for low in range(0, count, 2 * TILE):
                at = [pl.multiple_of(start + low + part * TILE, TILE) for part in range(2)]
                blocks = [image[:, pl.ds(here, TILE), :].reshape(TILE * TILE, lanes) for here in at]
                value = turned(jnp.concatenate(blocks, 1))
                for part in range(2):
                    sends[chunk][pl.ds(at[part], TILE)] = value[
                        :, part * lanes : (part + 1) * lanes
                    ].reshape(TILE, TILE, lanes)

    def halves(piece):
        count = piece_rows[piece] // 2
        return ((0, 1, 0, count), (1, -1, count, count))

    def block_for(piece, x_to, y_to, low, count):
        start = (y_to * NX + x_to) * rows + first_row[piece] + low
        return sends[PIECES[piece][0]].at[pl.ds(start, count)]

    def place(piece, x_from, y_from, low, count):
        return got[piece].at[low : low + count, tile_at(y_from * NX + x_from)]

    def spread(piece, rings=range(NY)):
        for half, sign, low, count in halves(piece):
            for j, ((dx, dy), (vx, vy), _) in enumerate(routes(sign)[1]):
                if dy in rings:
                    pltpu.make_async_remote_copy(
                        src_ref=block_for(piece, shifted(x, dx, NX), shifted(y, dy, NY), low, count),
                        dst_ref=relay[piece].at[half, j],
                        send_sem=spread_send.at[piece],
                        recv_sem=relay_recv.at[piece, half],
                        device_id=device(shifted(x, vx, NX), shifted(y, vy, NY), z, c),
                        device_id_type=MESH,
                    ).start()
        count = piece_rows[piece]
        for dx, dy in routes(1)[0]:
            if dy in rings:
                xd, yd = shifted(x, dx, NX), shifted(y, dy, NY)
                pltpu.make_async_remote_copy(
                    src_ref=block_for(piece, xd, yd, 0, count),
                    dst_ref=place(piece, x, y, 0, count),
                    send_sem=spread_send.at[piece],
                    recv_sem=spread_recv.at[piece],
                    device_id=device(xd, yd, z, c),
                    device_id_type=MESH,
                ).start()
        if 0 in rings:
            pltpu.make_async_copy(
                block_for(piece, x, y, 0, count), place(piece, x, y, 0, count), spread_recv.at[piece]
            ).start()

    def forward(piece):
        if RELAYS == 0:
            return
        for half, sign, low, count in halves(piece):
            arrived = relay[piece].at[half]
            pltpu.make_async_copy(arrived, arrived, relay_recv.at[piece, half]).wait()
            for j, (_, (vx, vy), (fx, fy)) in enumerate(routes(sign)[1]):
                pltpu.make_async_remote_copy(
                    src_ref=relay[piece].at[half, j],
                    dst_ref=place(piece, shifted(x, -vx, NX), shifted(y, -vy, NY), low, count),
                    send_sem=relay_send.at[piece],
                    recv_sem=spread_recv.at[piece],
                    device_id=device(shifted(x, fx, NX), shifted(y, fy, NY), z, c),
                    device_id_type=MESH,
                ).start()

    def order_copy(dy):
        return pltpu.make_async_remote_copy(
            src_ref=orders_own,
            dst_ref=orders.at[y],
            send_sem=order_send.at[dy],
            recv_sem=order_sem.at[0],
            device_id=device(x, shifted(y, dy, NY), z, c),
            device_id_type=MESH,
        )

    def make_pick():
        pltpu.make_async_copy(orders, orders, order_sem.at[0]).wait()
        line = lax.broadcasted_iota(jnp.int32, (SECTORS_HERE, targets), 0)
        blocks = []
        for yy in range(NY):
            for xx in range(NX):
                for group in range(GROUPS_HERE):
                    wanted = orders[yy, group : group + 1, :]
                    first = (xx * NZ + z) * SECTORS_HERE
                    blocks.append(jnp.where(wanted == line + first, 1.0, 0.0))
        table = jnp.concatenate(blocks, 0).T
        half = targets // NC
        for xh in range(NC):
            blocks = []
            for zz in range(NZ):
                for part in range(X_PART):
                    low = ((xh * X_PART + part) * NZ + zz) * SECTORS_HERE
                    blocks.append(table[low : low + SECTORS_HERE])
            start = pl.multiple_of((1 - c if xh == 0 else c) * half, half)
            pick[pl.ds(start, half), :] = jnp.concatenate(blocks, 0).astype(jnp.bfloat16)

    def gather(piece):
        pltpu.make_async_copy(got[piece], got[piece], spread_recv.at[piece]).wait()
        half = targets // NC

        def some(step, _):
            for inner in range(4):
                m = step * 8 + inner * 2
                both = jnp.concatenate([got[piece][m], got[piece][m + 1]], 1)
                value = jnp.dot(pick[...], both, preferred_element_type=jnp.float32)
                for part, to in ((0, give[piece]), (1, own[piece])):
                    for zz in range(NZ):
                        low = part * half + zz * TILE
                        for next_m in range(2):
                            to[zz, m + next_m] = value[
                                low : low + TILE, next_m * lanes : (next_m + 1) * lanes
                            ].astype(to.dtype)
            return 0

        lax.fori_loop(0, piece_rows[piece] // 8, some, 0)
        core_copy(piece).start()

    def core_copy(piece):
        return pltpu.make_async_remote_copy(
            src_ref=give[piece],
            dst_ref=take[piece],
            send_sem=core_send.at[piece],
            recv_sem=core_recv.at[piece],
            device_id=device(x, y, z, 1 - c),
            device_id_type=MESH,
        )

    def held(piece, zd, low, count):
        at = slice(low, low + count)
        return own[piece][zd, at] + take[piece][zd, at].astype(jnp.float32)

    def z_buffers(piece, way):
        return (up_out[piece], up_in[piece]) if way > 0 else (down_out[piece], down_in[piece])

    def z_copy(piece, step, way):
        source, target = z_buffers(piece, way)
        out_sem, in_sem = (up_send, up_recv) if way > 0 else (down_send, down_recv)
        at = (step,)
        if step == 0:
            _, _, low, count = halves(piece)[0 if way > 0 else 1]
            at = (step, slice(low, low + count))
        return pltpu.make_async_remote_copy(
            src_ref=source.at[at],
            dst_ref=target.at[at],
            send_sem=out_sem.at[piece, step],
            recv_sem=in_sem.at[piece, step],
            device_id=device(x, y, shifted(z, way, NZ), c),
            device_id_type=MESH,
        )

    def carried(step, way, sign):
        return step > 0 or way == sign

    def chain(piece, step):
        if step >= STEPS:
            return
        if step == 0:
            core_copy(piece).wait_recv()
        for way in (1, -1):
            source, target = z_buffers(piece, way)
            if step > 0:
                z_copy(piece, step - 1, way).wait_recv()
            zd = shifted(z, way * (STEPS - step), NZ)
            for _, sign, low, count in halves(piece):
                if carried(step, way, sign):
                    at = slice(low, low + count)
                    value = held(piece, zd, low, count)
                    if step > 0 and carried(step - 1, way, sign):
                        value = value + target[step - 1, at].astype(jnp.float32)
                    source[step, at] = value.astype(jnp.bfloat16)
            z_copy(piece, step, way).start()

    def final_copies(piece, part):
        xd = c * X_PART + part
        spot_there = final[piece].at[lax.rem(x, X_PART)]
        there = dict(
            src_ref=done[piece].at[part],
            dst_ref=spot_there,
            send_sem=final_send.at[piece, part],
            recv_sem=final_recv.at[piece],
            device_id=device(xd, y, z, lax.div(x, X_PART)),
            device_id_type=MESH,
        )
        here = (done[piece].at[part], spot_there, final_recv.at[piece])
        return xd, there, here

    def finish(piece):
        last = STEPS - 1
        for way in (1, -1):
            z_copy(piece, last, way).wait_recv()
        for _, sign, low, count in halves(piece):
            value = held(piece, z, low, count)
            for way in (1, -1):
                if carried(last, way, sign):
                    value = value + z_buffers(piece, way)[1][last, low : low + count].astype(jnp.float32)
            for part in range(X_PART):
                at = slice(part * SECTORS_HERE, (part + 1) * SECTORS_HERE)
                done[piece][part, low // 2 : (low + count) // 2] = (
                    value[:, at, :].reshape(count // 2, TILE, lanes).astype(jnp.bfloat16)
                )
        for part in range(X_PART):
            xd, there, here = final_copies(piece, part)

            @pl.when(xd != x)
            def _():
                pltpu.make_async_remote_copy(**there).start()

            @pl.when(xd == x)
            def _():
                pltpu.make_async_copy(*here).start()

    def put(piece):
        pltpu.make_async_copy(final[piece], final[piece], final_recv.at[piece]).wait()
        chunk, count = PIECES[piece][0], piece_rows[piece]
        total = X_PART * count * SECTORS_HERE
        row = lax.broadcasted_iota(jnp.int32, (total, total), 0)
        column = lax.broadcasted_iota(jnp.int32, (total, total), 1)
        sector = column & (SECTORS_HERE - 1)
        line = lax.shift_right_logical(column, 3)
        value = jnp.dot(
            ones_where(row == sector * (X_PART * count) + line),
            final[piece][...].reshape(total, lanes),
            preferred_element_type=jnp.float32,
        )
        for sector in range(SECTORS_HERE):
            for part in range(X_PART):
                low = part * rows + first_row[piece]
                start = (sector * X_PART + part) * count
                out[sector, low : low + count, chunk * lanes : (chunk + 1) * lanes] = value[
                    start : start + count
                ]

    ring_halves = (y_order[: NY // 2], y_order[NY // 2 :])
    first_parts()
    images(0)
    turn(0, ring_halves[0])
    pl.semaphore_wait(barrier, len(others))
    spread(0, ring_halves[0])
    turn(0, ring_halves[1])
    spread(0, ring_halves[1])
    for dy in range(1, NY):
        order_copy(dy).start()
    pltpu.make_async_copy(orders_own, orders.at[y], order_sem.at[0]).start()
    later_parts()
    forward(0)
    images(1)
    for rings in ring_halves:
        turn(1, rings)
        spread(1, rings)
    images(2)
    make_pick()
    gather(0)
    turn(2, range(NY))
    forward(1)
    spread(2)
    chain(0, 0)
    spread(3)
    chain(0, 1)
    chain(0, 2)
    gather(1)
    chain(0, 3)
    forward(2)
    chain(1, 0)
    forward(3)
    finish(0)
    chain(1, 1)
    put(0)
    chain(1, 2)
    gather(2)
    chain(2, 0)
    chain(1, 3)
    gather(3)
    chain(2, 1)
    chain(3, 0)
    chain(2, 2)
    chain(3, 1)
    finish(1)
    chain(3, 2)
    chain(2, 3)
    chain(3, 3)
    put(1)
    finish(2)
    finish(3)
    put(2)
    put(3)

    for dy in range(1, NY):
        order_copy(dy).wait_send()
    for piece in pieces:
        sent = sends[PIECES[piece][0]].at[0 : (SLOTS - 1) * piece_rows[piece]]
        pltpu.make_async_copy(sent, sent, spread_send.at[piece]).wait()
        if RELAYS:
            pltpu.make_async_copy(relay[piece], relay[piece], relay_send.at[piece]).wait()
        core_copy(piece).wait_send()
        for step in range(STEPS):
            for way in (1, -1):
                z_copy(piece, step, way).wait_send()
        for part in range(X_PART):
            xd, there, _ = final_copies(piece, part)

            @pl.when(xd != x)
            def _():
                pltpu.make_async_remote_copy(**there).wait_send()


def shards(psi, left_ops, right_ops, pair_src, widths):
    size = psi.shape[1]
    targets = pair_src.shape[1]
    rows, lanes = size // SLOTS, size // CHUNKS
    term = lax.axis_index("term")
    bf, count = jnp.bfloat16, len(PIECES)
    tile = (TILE, lanes)
    scratch = [
        pltpu.VMEM(psi.shape, bf),
        pltpu.VMEM(left_ops.shape, bf),
        pltpu.VMEM(right_ops.shape, bf),
        pltpu.VMEM((8, targets), jnp.int32),
        pltpu.VMEM((NY, 8, targets), jnp.int32),
        pltpu.VMEM((SECTORS_HERE, GROUPS_HERE * (size - lanes), size), bf),
        pltpu.VMEM((TILE, size, lanes), bf),
        pltpu.VMEM((TILE * TILE, TILE * TILE), bf),
        pltpu.VMEM((targets, SOURCES), bf),
        *[pltpu.VMEM((size,) + tile, bf) for _ in range(CHUNKS)],
    ]
    for _, _, thirds in PIECES:
        here = rows * thirds // 3
        ring = pltpu.VMEM((STEPS, here) + tile, bf)
        scratch += [
            pltpu.VMEM((here, SOURCES, lanes), bf),
            pltpu.VMEM((2, max(RELAYS, 1), here // 2) + tile, bf),
            pltpu.VMEM((NZ, here) + tile, bf),
            pltpu.VMEM((NZ, here) + tile, bf),
            pltpu.VMEM((NZ, here) + tile, jnp.float32),
            ring, ring, ring, ring,
            pltpu.VMEM((X_PART, here // 2) + tile, bf),
            pltpu.VMEM((X_PART, here // 2) + tile, bf),
        ]
    dma = pltpu.SemaphoreType.DMA
    scratch += [
        dma((3, SECTORS_HERE)), dma((1,)), dma((NY,)), dma((count,)), dma((count,)),
        dma((count, 2)), dma((count,)), dma((count,)), dma((count,)),
        dma((count, STEPS)), dma((count, STEPS)), dma((count, STEPS)), dma((count, STEPS)),
        dma((count, X_PART)), dma((count,)),
    ]
    summed = pl.pallas_call(
        kernel,
        out_shape=jax.ShapeDtypeStruct((SECTORS_HERE, X_PART * rows, size), jnp.float32),
        in_specs=[
            pl.BlockSpec(memory_space=pltpu.VMEM),
            pl.BlockSpec(memory_space=pltpu.SMEM),
            pl.BlockSpec(memory_space=pl.ANY),
            pl.BlockSpec(memory_space=pl.ANY),
            pl.BlockSpec(memory_space=pl.ANY),
        ],
        out_specs=pl.BlockSpec(memory_space=pltpu.VMEM),
        scratch_shapes=scratch,
        compiler_params=pltpu.CompilerParams(
            collective_id=0, has_side_effects=True, vmem_limit_bytes=56 * 1024 * 1024
        ),
        cost_estimate=pl.CostEstimate(
            flops=64 * size**3, bytes_accessed=40 * size * size * 2, transcendentals=0
        ),
    )(pair_src, widths, psi, left_ops, right_ops)

    summed = jnp.swapaxes(summed, 1, 2)
    line = jnp.arange(size, dtype=jnp.int32)
    columns = term * (X_PART * rows) + jnp.arange(X_PART * rows, dtype=jnp.int32)
    keep = (line[None, :, None] < widths[0][:, None, None]) & (
        columns[None, None, :] < widths[1][:, None, None]
    )
    return jnp.where(keep, summed, jnp.zeros_like(summed))


def solution(mesh):
    return jax.shard_map(
        shards,
        mesh=mesh,
        in_specs=(
            P("sec", None, None),
            P("term", "sec", None, None),
            P("term", "sec", None, None),
            P("term", None),
            P(None, "sec"),
        ),
        out_specs=P("sec", None, "term"),
        check_vma=False,
    )
```

```python
import jax
import jax.numpy as jnp
from jax import lax
from jax.experimental import pallas as pl
from jax.experimental.pallas import tpu as pltpu
from jax.sharding import PartitionSpec as P

NX, NY, NZ, NC = 4, 4, 8, 2
CHUNKS = 3
PIECES = ((0, 0, 3), (1, 0, 3), (2, 0, 2), (2, 2, 1))
SLOTS = NX * NY
GROUPS_HERE = 2
SECTORS_HERE = 8
TILE = GROUPS_HERE * SECTORS_HERE
SOURCES = SLOTS * TILE
X_PART = NX // NC
STEPS = NZ // 2
MESH = pl.DeviceIdType.MESH
LAST = len(PIECES) - 1
BUFFERS = 11


def routes(sign):
    direct, relayed = [], []
    for dx in range(NX):
        for dy in range(NY):
            far_x, far_y = NX > 2 and dx == NX // 2, NY > 2 and dy == NY // 2
            if far_x or far_y:
                via = (sign if far_x else 0, sign if far_y else 0)
                relayed.append(((dx, dy), via, (dx - via[0], dy - via[1])))
            elif (dx, dy) != (0, 0):
                direct.append((dx, dy))
    return direct, relayed


RELAYS = len(routes(1)[1])


def device(x, y, z, c):
    return (x * NZ + z, y * NC + c)


def ones_where(condition):
    return jnp.where(condition, 1.0, 0.0).astype(jnp.bfloat16)


def tile_at(index):
    return pl.ds(pl.multiple_of(index * TILE, TILE), TILE)


def kernel(pair_src, widths, psi, left, right, out, *rest):
    psi_v, left_v, right_v, orders_own, orders, parts, image, swap, pick, *rest = rest
    sends, rest = rest[:CHUNKS], rest[CHUNKS:]
    buffers = [rest[i * BUFFERS : (i + 1) * BUFFERS] for i in range(len(PIECES))]
    (
        load_sem, order_sem, order_send, spread_send, spread_recv, relay_recv, relay_send, core_send, core_recv,
        up_send, up_recv, down_send, down_recv, final_send, final_recv, straight_send, straight_recv,
        straight_out, straight_in,
    ) = rest[len(PIECES) * BUFFERS :]
    got, relay, give, take, own, up_out, up_in, down_out, down_in, done, final = zip(*buffers)
    sec, term = lax.axis_index("sec"), lax.axis_index("term")
    x, z = lax.div(sec, NZ), lax.rem(sec, NZ)
    y, c = lax.div(term, NC), lax.rem(term, NC)
    size = psi_v.shape[-1]
    rows = size // SLOTS
    lanes = size // CHUNKS
    targets = pair_src.shape[1]
    pieces = range(len(PIECES))
    y_order = sorted(range(NY), key=lambda dy: -min(dy, NY - dy))
    first_row = [rows * at // 3 for _, at, _ in PIECES]
    piece_rows = [rows * count // 3 for _, _, count in PIECES]

    def shifted(value, by, count):
        return lax.rem(value + (by % count), count)

    barrier = pltpu.get_barrier_semaphore()
    others = [
        device(shifted(x, dx, NX), shifted(y, dy, NY), z, c)
        for dx in range(NX)
        for dy in range(NY)
        if (dx, dy) != (0, 0)
    ]
    others += [device(shifted(x, dx, NX), y, z, 1 - c) for dx in range(NX)]
    others += [device(x, y, shifted(z, dz, NZ), c) for dz in range(1, NZ)]
    for other in others:
        pl.semaphore_signal(barrier, inc=1, device_id=other, device_id_type=MESH)

    def loads(k):
        return (
            pltpu.make_async_copy(psi.at[k], psi_v.at[k], load_sem.at[0, k]),
            pltpu.make_async_copy(
                left.at[:, k, 0:lanes], left_v.at[:, k, 0:lanes], load_sem.at[1, k]
            ),
            pltpu.make_async_copy(right.at[:, k], right_v.at[:, k], load_sem.at[2, k]),
            pltpu.make_async_copy(
                left.at[:, k, lanes:size], left_v.at[:, k, lanes:size], load_sem.at[3, k]
            ),
        )

    for which in ((0, 1), (2,), (3,)):
        for k in range(SECTORS_HERE):
            for copy in which:
                loads(k)[copy].start()

    row = lax.broadcasted_iota(jnp.int32, swap.shape, 0)
    column = lax.broadcasted_iota(jnp.int32, swap.shape, 1)
    swap[...] = ones_where(row == (column & (TILE - 1)) * TILE + lax.shift_right_logical(column, 4))
    orders_own[...] = jnp.concatenate([pair_src[...], jnp.zeros((6, targets), jnp.int32)], 0)

    def image_of(right_block, part):
        return lax.dot_general(
            right_block, part, (((1,), (1,)), ((), ())), preferred_element_type=jnp.float32
        ).astype(jnp.bfloat16)

    def turned(block):
        return jnp.dot(swap[...], block, preferred_element_type=jnp.float32).astype(jnp.bfloat16)

    def each_sector(body):
        def some(step, _):
            for inner in range(2):
                body(step * 2 + inner)
            return 0

        lax.fori_loop(0, SECTORS_HERE // 2, some, 0)

    def first_parts():
        def one(k):
            for copy in loads(k)[:2]:
                copy.wait()
            keep = (lax.broadcasted_iota(jnp.int32, (size, size), 0) < widths[0, k]) & (
                lax.broadcasted_iota(jnp.int32, (size, size), 1) < widths[1, k]
            )
            masked = jnp.where(keep, psi_v[k].astype(jnp.float32), 0.0).astype(jnp.bfloat16)
            psi_v[k] = masked
            here = left_v[:, k, 0:lanes, :].reshape(GROUPS_HERE * lanes, size)
            parts[k, 0 : GROUPS_HERE * lanes] = jnp.dot(
                here, masked, preferred_element_type=jnp.float32
            ).astype(jnp.bfloat16)

        each_sector(one)

    def first_images(rings, first):
        count = size // NY
        starts = [pl.multiple_of(shifted(y, dy, NY) * count, 2 * TILE) for dy in rings]

        def one(k):
            if first:
                loads(k)[2].wait()
            for group in range(GROUPS_HERE):
                chosen = jnp.concatenate([right_v[group, k, pl.ds(start, count), :] for start in starts], 0)
                image[group * SECTORS_HERE + k, 0 : count * len(starts), 0:lanes] = image_of(
                    chosen, parts[k, group * lanes : (group + 1) * lanes, :]
                )

        each_sector(one)
        for low in range(0, count * len(starts), 2 * TILE):
            both = turned(
                jnp.concatenate(
                    [
                        image[:, at : at + TILE, 0:lanes].reshape(TILE * TILE, lanes)
                        for at in (low, low + TILE)
                    ],
                    1,
                )
            )
            for part in range(2):
                at = starts[low // count] + low % count + part * TILE
                sends[0][pl.ds(at, TILE)] = both[:, part * lanes : (part + 1) * lanes].reshape(
                    TILE, TILE, lanes
                )

    later = size - lanes

    def later_parts():
        def one(k):
            loads(k)[3].wait()
            here = left_v[:, k, lanes:, :].reshape(GROUPS_HERE * later, size)
            parts[k] = jnp.dot(here, psi_v[k], preferred_element_type=jnp.float32).astype(jnp.bfloat16)

        each_sector(one)

    def later_images():
        def one(k):
            for group in range(GROUPS_HERE):
                image[group * SECTORS_HERE + k] = image_of(
                    right_v[group, k], parts[k, group * later : (group + 1) * later, :]
                )

        each_sector(one)

        def some(step, _):
            for inner in range(4):
                at = pl.multiple_of((step * 4 + inner) * TILE, TILE)
                value = turned(image[:, pl.ds(at, TILE), :].reshape(TILE * TILE, later))
                for chunk in range(1, CHUNKS):
                    sends[chunk][pl.ds(at, TILE)] = value[
                        :, (chunk - 1) * lanes : chunk * lanes
                    ].reshape(TILE, TILE, lanes)
            return 0

        lax.fori_loop(0, size // (4 * TILE), some, 0)

    def halves(piece):
        count = piece_rows[piece] // 2
        return ((0, 1, 0, count), (1, -1, count, count))

    def block_for(piece, x_to, y_to, low, count):
        start = (y_to * NX + x_to) * rows + first_row[piece] + low
        return sends[PIECES[piece][0]].at[pl.ds(start, count)]

    def place(piece, x_from, y_from, low, count):
        return got[piece].at[low : low + count, tile_at(y_from * NX + x_from)]

    def spread(piece, rings=range(NY)):
        for half, sign, low, count in halves(piece) if piece != LAST else ():
            for j, ((dx, dy), (vx, vy), _) in enumerate(routes(sign)[1]):
                if dy in rings:
                    pltpu.make_async_remote_copy(
                        src_ref=block_for(piece, shifted(x, dx, NX), shifted(y, dy, NY), low, count),
                        dst_ref=relay[piece].at[half, j],
                        send_sem=spread_send.at[piece],
                        recv_sem=relay_recv.at[piece, half],
                        device_id=device(shifted(x, vx, NX), shifted(y, vy, NY), z, c),
                        device_id_type=MESH,
                    ).start()
        count = piece_rows[piece]
        for dx, dy in routes(1)[0] + ([route[0] for route in routes(1)[1]] if piece == LAST else []):
            if dy in rings:
                xd, yd = shifted(x, dx, NX), shifted(y, dy, NY)
                pltpu.make_async_remote_copy(
                    src_ref=block_for(piece, xd, yd, 0, count),
                    dst_ref=place(piece, x, y, 0, count),
                    send_sem=spread_send.at[piece],
                    recv_sem=spread_recv.at[piece],
                    device_id=device(xd, yd, z, c),
                    device_id_type=MESH,
                ).start()
        if 0 in rings:
            pltpu.make_async_copy(
                block_for(piece, x, y, 0, count), place(piece, x, y, 0, count), spread_recv.at[piece]
            ).start()

    def forward(piece):
        if RELAYS == 0:
            return
        for half, sign, low, count in halves(piece):
            arrived = relay[piece].at[half]
            pltpu.make_async_copy(arrived, arrived, relay_recv.at[piece, half]).wait()
            for j, (_, (vx, vy), (fx, fy)) in enumerate(routes(sign)[1]):
                pltpu.make_async_remote_copy(
                    src_ref=relay[piece].at[half, j],
                    dst_ref=place(piece, shifted(x, -vx, NX), shifted(y, -vy, NY), low, count),
                    send_sem=relay_send.at[piece],
                    recv_sem=spread_recv.at[piece],
                    device_id=device(shifted(x, fx, NX), shifted(y, fy, NY), z, c),
                    device_id_type=MESH,
                ).start()

    def order_copy(dy):
        return pltpu.make_async_remote_copy(
            src_ref=orders_own,
            dst_ref=orders.at[y],
            send_sem=order_send.at[dy],
            recv_sem=order_sem.at[0],
            device_id=device(x, shifted(y, dy, NY), z, c),
            device_id_type=MESH,
        )

    def make_pick():
        pltpu.make_async_copy(orders, orders, order_sem.at[0]).wait()
        line = lax.broadcasted_iota(jnp.int32, (SECTORS_HERE, targets), 0)
        blocks = []
        for yy in range(NY):
            for xx in range(NX):
                for group in range(GROUPS_HERE):
                    wanted = orders[yy, group : group + 1, :]
                    first = (xx * NZ + z) * SECTORS_HERE
                    blocks.append(jnp.where(wanted == line + first, 1.0, 0.0))
        table = jnp.concatenate(blocks, 0).T
        half = targets // NC
        for xh in range(NC):
            blocks = []
            for zz in range(NZ):
                for part in range(X_PART):
                    low = ((xh * X_PART + part) * NZ + zz) * SECTORS_HERE
                    blocks.append(table[low : low + SECTORS_HERE])
            start = pl.multiple_of((1 - c if xh == 0 else c) * half, half)
            pick[pl.ds(start, half), :] = jnp.concatenate(blocks, 0).astype(jnp.bfloat16)

    def gather(piece):
        pltpu.make_async_copy(got[piece], got[piece], spread_recv.at[piece]).wait()
        half = targets // NC

        def some(step, _):
            for inner in range(4):
                m = step * 8 + inner * 2
                both = jnp.concatenate([got[piece][m], got[piece][m + 1]], 1)
                value = jnp.dot(pick[...], both, preferred_element_type=jnp.float32)
                for part, to in ((0, give[piece]), (1, own[piece])):
                    for zz in range(NZ):
                        low = part * half + zz * TILE
                        for next_m in range(2):
                            to[zz, m + next_m] = value[
                                low : low + TILE, next_m * lanes : (next_m + 1) * lanes
                            ].astype(to.dtype)
            return 0

        lax.fori_loop(0, piece_rows[piece] // 8, some, 0)
        core_copy(piece).start()

    def core_copy(piece):
        return pltpu.make_async_remote_copy(
            src_ref=give[piece],
            dst_ref=take[piece],
            send_sem=core_send.at[piece],
            recv_sem=core_recv.at[piece],
            device_id=device(x, y, z, 1 - c),
            device_id_type=MESH,
        )

    def held(piece, zd, low, count):
        at = slice(low, low + count)
        return own[piece][zd, at] + take[piece][zd, at].astype(jnp.float32)

    def z_buffers(piece, way):
        return (up_out[piece], up_in[piece]) if way > 0 else (down_out[piece], down_in[piece])

    def z_copy(piece, step, way):
        source, target = z_buffers(piece, way)
        out_sem, in_sem = (up_send, up_recv) if way > 0 else (down_send, down_recv)
        at = (step,)
        if step == 0:
            _, _, low, count = halves(piece)[0 if way > 0 else 1]
            at = (step, slice(low, low + count))
        return pltpu.make_async_remote_copy(
            src_ref=source.at[at],
            dst_ref=target.at[at],
            send_sem=out_sem.at[piece, step],
            recv_sem=in_sem.at[piece, step],
            device_id=device(x, y, shifted(z, way, NZ), c),
            device_id_type=MESH,
        )

    def straight_copy(dz):
        return pltpu.make_async_remote_copy(
            src_ref=straight_out.at[dz - 1],
            dst_ref=straight_in.at[dz - 1],
            send_sem=straight_send.at[dz - 1],
            recv_sem=straight_recv.at[0],
            device_id=device(x, y, shifted(z, dz, NZ), c),
            device_id_type=MESH,
        )

    def straight():
        core_copy(LAST).wait_recv()
        for dz in sorted(range(1, NZ), key=lambda dz: -min(dz, NZ - dz)):
            value = held(LAST, shifted(z, dz, NZ), 0, piece_rows[LAST])
            straight_out[dz - 1] = value.astype(jnp.bfloat16)
            straight_copy(dz).start()

    def carried(step, way, sign):
        return step > 0 or way == sign

    def chain(piece, step):
        if step >= STEPS:
            return
        if step == 0:
            core_copy(piece).wait_recv()
        for way in (1, -1):
            source, target = z_buffers(piece, way)
            if step > 0:
                z_copy(piece, step - 1, way).wait_recv()
            zd = shifted(z, way * (STEPS - step), NZ)
            for _, sign, low, count in halves(piece):
                if carried(step, way, sign):
                    at = slice(low, low + count)
                    value = held(piece, zd, low, count)
                    if step > 0 and carried(step - 1, way, sign):
                        value = value + target[step - 1, at].astype(jnp.float32)
                    source[step, at] = value.astype(jnp.bfloat16)
            z_copy(piece, step, way).start()

    def final_copies(piece, part):
        xd = c * X_PART + part
        spot_there = final[piece].at[lax.rem(x, X_PART)]
        there = dict(
            src_ref=done[piece].at[part],
            dst_ref=spot_there,
            send_sem=final_send.at[piece, part],
            recv_sem=final_recv.at[piece],
            device_id=device(xd, y, z, lax.div(x, X_PART)),
            device_id_type=MESH,
        )
        here = (done[piece].at[part], spot_there, final_recv.at[piece])
        return xd, there, here

    def finish(piece):
        last = STEPS - 1
        if piece == LAST:
            pltpu.make_async_copy(straight_in, straight_in, straight_recv.at[0]).wait()
        else:
            for way in (1, -1):
                z_copy(piece, last, way).wait_recv()
        for _, sign, low, count in halves(piece):
            value = held(piece, z, low, count)
            if piece == LAST:
                for dz in range(1, NZ):
                    value = value + straight_in[dz - 1, low : low + count].astype(jnp.float32)
            for way in (1, -1) if piece != LAST else ():
                if carried(last, way, sign):
                    value = value + z_buffers(piece, way)[1][last, low : low + count].astype(jnp.float32)
            for part in range(X_PART):
                at = slice(part * SECTORS_HERE, (part + 1) * SECTORS_HERE)
                done[piece][part, low // 2 : (low + count) // 2] = (
                    value[:, at, :].reshape(count // 2, TILE, lanes).astype(jnp.bfloat16)
                )
        for part in range(X_PART):
            xd, there, here = final_copies(piece, part)

            @pl.when(xd != x)
            def _():
                pltpu.make_async_remote_copy(**there).start()

            @pl.when(xd == x)
            def _():
                pltpu.make_async_copy(*here).start()

    def put(piece):
        pltpu.make_async_copy(final[piece], final[piece], final_recv.at[piece]).wait()
        chunk, count = PIECES[piece][0], piece_rows[piece]
        total = X_PART * count * SECTORS_HERE
        row = lax.broadcasted_iota(jnp.int32, (total, total), 0)
        column = lax.broadcasted_iota(jnp.int32, (total, total), 1)
        sector = column & (SECTORS_HERE - 1)
        line = lax.shift_right_logical(column, 3)
        value = jnp.dot(
            ones_where(row == sector * (X_PART * count) + line),
            final[piece][...].reshape(total, lanes),
            preferred_element_type=jnp.float32,
        )
        for sector in range(SECTORS_HERE):
            for part in range(X_PART):
                low = part * rows + first_row[piece]
                start = (sector * X_PART + part) * count
                m = term * (X_PART * rows) + low + lax.broadcasted_iota(jnp.int32, (count, lanes), 0)
                i = chunk * lanes + lax.broadcasted_iota(jnp.int32, (count, lanes), 1)
                keep = (i < widths[0, sector]) & (m < widths[1, sector])
                out[sector, low : low + count, chunk * lanes : (chunk + 1) * lanes] = jnp.where(
                    keep, value[start : start + count], 0.0
                )

    first_parts()
    for part in range(2):
        rings = y_order[part * NY // 2 : (part + 1) * NY // 2]
        first_images(rings, part == 0)
        if part == 0:
            pl.semaphore_wait(barrier, len(others))
        spread(0, rings)
    for dy in range(1, NY):
        order_copy(dy).start()
    pltpu.make_async_copy(orders_own, orders.at[y], order_sem.at[0]).start()
    later_parts()
    forward(0)
    later_images()
    spread(1)
    make_pick()
    gather(0)
    forward(1)
    spread(2)
    chain(0, 0)
    spread(3)
    chain(0, 1)
    chain(0, 2)
    gather(1)
    chain(0, 3)
    forward(2)
    chain(1, 0)
    finish(0)
    chain(1, 1)
    put(0)
    chain(1, 2)
    gather(2)
    chain(2, 0)
    chain(1, 3)
    gather(3)
    chain(2, 1)
    straight()
    finish(1)
    chain(2, 2)
    chain(2, 3)
    put(1)
    finish(3)
    finish(2)
    put(3)
    put(2)

    for dy in range(1, NY):
        order_copy(dy).wait_send()
    for dz in range(1, NZ):
        straight_copy(dz).wait_send()
    for piece in pieces:
        sent = sends[PIECES[piece][0]].at[0 : (SLOTS - 1) * piece_rows[piece]]
        pltpu.make_async_copy(sent, sent, spread_send.at[piece]).wait()
        if RELAYS and piece != LAST:
            pltpu.make_async_copy(relay[piece], relay[piece], relay_send.at[piece]).wait()
        core_copy(piece).wait_send()
        for step in range(STEPS) if piece != LAST else ():
            for way in (1, -1):
                z_copy(piece, step, way).wait_send()
        for part in range(X_PART):
            xd, there, _ = final_copies(piece, part)

            @pl.when(xd != x)
            def _():
                pltpu.make_async_remote_copy(**there).wait_send()


def shards(psi, left_ops, right_ops, pair_src, widths):
    size = psi.shape[1]
    targets = pair_src.shape[1]
    rows, lanes = size // SLOTS, size // CHUNKS
    bf, count = jnp.bfloat16, len(PIECES)
    tile = (TILE, lanes)
    scratch = [
        pltpu.VMEM(psi.shape, bf),
        pltpu.VMEM(left_ops.shape, bf),
        pltpu.VMEM(right_ops.shape, bf),
        pltpu.VMEM((8, targets), jnp.int32),
        pltpu.VMEM((NY, 8, targets), jnp.int32),
        pltpu.VMEM((SECTORS_HERE, GROUPS_HERE * (size - lanes), size), bf),
        pltpu.VMEM((TILE, size, size - lanes), bf),
        pltpu.VMEM((TILE * TILE, TILE * TILE), bf),
        pltpu.VMEM((targets, SOURCES), bf),
        *[pltpu.VMEM((size,) + tile, bf) for _ in range(CHUNKS)],
    ]
    for _, _, thirds in PIECES:
        here = rows * thirds // 3
        ring = pltpu.VMEM((STEPS, here) + tile, bf)
        scratch += [
            pltpu.VMEM((here, SOURCES, lanes), bf),
            pltpu.VMEM((2, max(RELAYS, 1), here // 2) + tile, bf),
            pltpu.VMEM((NZ, here) + tile, bf),
            pltpu.VMEM((NZ, here) + tile, bf),
            pltpu.VMEM((NZ, here) + tile, jnp.float32),
            ring, ring, ring, ring,
            pltpu.VMEM((X_PART, here // 2) + tile, bf),
            pltpu.VMEM((X_PART, here // 2) + tile, bf),
        ]
    dma = pltpu.SemaphoreType.DMA
    scratch += [
        dma((4, SECTORS_HERE)), dma((1,)), dma((NY,)), dma((count,)), dma((count,)),
        dma((count, 2)), dma((count,)), dma((count,)), dma((count,)),
        dma((count, STEPS)), dma((count, STEPS)), dma((count, STEPS)), dma((count, STEPS)),
        dma((count, X_PART)), dma((count,)), dma((NZ - 1,)), dma((1,)),
        *[pltpu.VMEM((NZ - 1, rows * PIECES[LAST][2] // 3) + tile, bf) for _ in range(2)],
    ]
    summed = pl.pallas_call(
        kernel,
        out_shape=jax.ShapeDtypeStruct((SECTORS_HERE, X_PART * rows, size), jnp.float32),
        in_specs=[
            pl.BlockSpec(memory_space=pltpu.VMEM),
            pl.BlockSpec(memory_space=pltpu.SMEM),
            pl.BlockSpec(memory_space=pl.ANY),
            pl.BlockSpec(memory_space=pl.ANY),
            pl.BlockSpec(memory_space=pl.ANY),
        ],
        out_specs=pl.BlockSpec(memory_space=pltpu.VMEM),
        scratch_shapes=scratch,
        compiler_params=pltpu.CompilerParams(
            collective_id=0, has_side_effects=True, vmem_limit_bytes=56 * 1024 * 1024
        ),
        cost_estimate=pl.CostEstimate(
            flops=64 * size**3, bytes_accessed=40 * size * size * 2, transcendentals=0
        ),
    )(pair_src, widths, psi, left_ops, right_ops)

    return jnp.swapaxes(summed, 1, 2)


def solution(mesh):
    return jax.shard_map(
        shards,
        mesh=mesh,
        in_specs=(
            P("sec", None, None),
            P("term", "sec", None, None),
            P("term", "sec", None, None),
            P("term", None),
            P(None, "sec"),
        ),
        out_specs=P("sec", None, "term"),
        check_vma=False,
    )
```

```python
import jax
import jax.numpy as jnp
from jax import lax
from jax.experimental import pallas as pl
from jax.experimental.pallas import tpu as pltpu
from jax.sharding import PartitionSpec as P

NX, NY, NZ, NC = 4, 4, 8, 2
CHUNKS = 3
PIECES = ((0, 0, 3), (1, 0, 3), (2, 0, 2), (2, 2, 1))
SLOTS = NX * NY
GROUPS_HERE = 2
SECTORS_HERE = 8
TILE = GROUPS_HERE * SECTORS_HERE
SOURCES = SLOTS * TILE
X_PART = NX // NC
STEPS = NZ // 2
MESH = pl.DeviceIdType.MESH
LAST = len(PIECES) - 1
BUFFERS = 11


def routes(sign):
    direct, relayed = [], []
    for dx in range(NX):
        for dy in range(NY):
            far_x, far_y = NX > 2 and dx == NX // 2, NY > 2 and dy == NY // 2
            if far_x or far_y:
                via = (sign if far_x else 0, sign if far_y else 0)
                relayed.append(((dx, dy), via, (dx - via[0], dy - via[1])))
            elif (dx, dy) != (0, 0):
                direct.append((dx, dy))
    return direct, relayed


RELAYS = len(routes(1)[1])


def device(x, y, z, c):
    return (x * NZ + z, y * NC + c)


def ones_where(condition):
    return jnp.where(condition, 1.0, 0.0).astype(jnp.bfloat16)


def tile_at(index):
    return pl.ds(pl.multiple_of(index * TILE, TILE), TILE)


def kernel(pair_src, widths, psi, left, right, out, *rest):
    psi_v, left_v, right_v, orders_own, orders, parts, image, swap, pick, *rest = rest
    sends, rest = rest[:CHUNKS], rest[CHUNKS:]
    buffers = [rest[i * BUFFERS : (i + 1) * BUFFERS] for i in range(len(PIECES))]
    (
        load_sem, order_sem, order_send, spread_send, spread_recv, relay_recv, relay_send, core_send, core_recv,
        up_send, up_recv, down_send, down_recv, final_send, final_recv,
    ) = rest[len(PIECES) * BUFFERS :]
    got, relay, give, take, own, up_out, up_in, down_out, down_in, done, final = zip(*buffers)
    sec, term = lax.axis_index("sec"), lax.axis_index("term")
    x, z = lax.div(sec, NZ), lax.rem(sec, NZ)
    y, c = lax.div(term, NC), lax.rem(term, NC)
    size = psi_v.shape[-1]
    rows = size // SLOTS
    lanes = size // CHUNKS
    targets = pair_src.shape[1]
    pieces = range(len(PIECES))
    y_order = sorted(range(NY), key=lambda dy: -min(dy, NY - dy))
    first_row = [rows * at // 3 for _, at, _ in PIECES]
    piece_rows = [rows * count // 3 for _, _, count in PIECES]

    def shifted(value, by, count):
        return lax.rem(value + (by % count), count)

    barrier = pltpu.get_barrier_semaphore()
    others = [
        device(shifted(x, dx, NX), shifted(y, dy, NY), z, c)
        for dx in range(NX)
        for dy in range(NY)
        if (dx, dy) != (0, 0)
    ]
    others += [device(shifted(x, dx, NX), y, z, 1 - c) for dx in range(NX)]
    others += [device(x, y, shifted(z, 1, NZ), c), device(x, y, shifted(z, -1, NZ), c)]
    for other in others:
        pl.semaphore_signal(barrier, inc=1, device_id=other, device_id_type=MESH)

    def loads(k):
        return (
            pltpu.make_async_copy(psi.at[k], psi_v.at[k], load_sem.at[0, k]),
            pltpu.make_async_copy(
                left.at[:, k, 0:lanes], left_v.at[:, k, 0:lanes], load_sem.at[1, k]
            ),
            pltpu.make_async_copy(right.at[:, k], right_v.at[:, k], load_sem.at[2, k]),
            pltpu.make_async_copy(
                left.at[:, k, lanes:size], left_v.at[:, k, lanes:size], load_sem.at[3, k]
            ),
        )

    for which in ((0, 1), (2,), (3,)):
        for k in range(SECTORS_HERE):
            for copy in which:
                loads(k)[copy].start()

    row = lax.broadcasted_iota(jnp.int32, swap.shape, 0)
    column = lax.broadcasted_iota(jnp.int32, swap.shape, 1)
    swap[...] = ones_where(row == (column & (TILE - 1)) * TILE + lax.shift_right_logical(column, 4))
    orders_own[...] = jnp.concatenate([pair_src[...], jnp.zeros((6, targets), jnp.int32)], 0)

    def image_of(right_block, part):
        return lax.dot_general(
            right_block, part, (((1,), (1,)), ((), ())), preferred_element_type=jnp.float32
        ).astype(jnp.bfloat16)

    def turned(block):
        return jnp.dot(swap[...], block, preferred_element_type=jnp.float32).astype(jnp.bfloat16)

    def each_sector(body):
        def some(step, _):
            for inner in range(2):
                body(step * 2 + inner)
            return 0

        lax.fori_loop(0, SECTORS_HERE // 2, some, 0)

    def first_parts():
        def one(k):
            for copy in loads(k)[:2]:
                copy.wait()
            keep = (lax.broadcasted_iota(jnp.int32, (size, size), 0) < widths[0, k]) & (
                lax.broadcasted_iota(jnp.int32, (size, size), 1) < widths[1, k]
            )
            masked = jnp.where(keep, psi_v[k].astype(jnp.float32), 0.0).astype(jnp.bfloat16)
            psi_v[k] = masked
            here = left_v[:, k, 0:lanes, :].reshape(GROUPS_HERE * lanes, size)
            parts[k, 0 : GROUPS_HERE * lanes] = jnp.dot(
                here, masked, preferred_element_type=jnp.float32
            ).astype(jnp.bfloat16)

        each_sector(one)

    def first_images(rings, first):
        count = size // NY
        starts = [pl.multiple_of(shifted(y, dy, NY) * count, 2 * TILE) for dy in rings]

        def one(k):
            if first:
                loads(k)[2].wait()
            for group in range(GROUPS_HERE):
                chosen = jnp.concatenate([right_v[group, k, pl.ds(start, count), :] for start in starts], 0)
                image[group * SECTORS_HERE + k, 0 : count * len(starts), 0:lanes] = image_of(
                    chosen, parts[k, group * lanes : (group + 1) * lanes, :]
                )

        each_sector(one)
        for low in range(0, count * len(starts), 2 * TILE):
            both = turned(
                jnp.concatenate(
                    [
                        image[:, at : at + TILE, 0:lanes].reshape(TILE * TILE, lanes)
                        for at in (low, low + TILE)
                    ],
                    1,
                )
            )
            for part in range(2):
                at = starts[low // count] + low % count + part * TILE
                sends[0][pl.ds(at, TILE)] = both[:, part * lanes : (part + 1) * lanes].reshape(
                    TILE, TILE, lanes
                )

    later = size - lanes

    def later_parts():
        def one(k):
            loads(k)[3].wait()
            here = left_v[:, k, lanes:, :].reshape(GROUPS_HERE * later, size)
            parts[k] = jnp.dot(here, psi_v[k], preferred_element_type=jnp.float32).astype(jnp.bfloat16)

        each_sector(one)

    def later_images():
        def one(k):
            for group in range(GROUPS_HERE):
                image[group * SECTORS_HERE + k] = image_of(
                    right_v[group, k], parts[k, group * later : (group + 1) * later, :]
                )

        each_sector(one)

        def some(step, _):
            for inner in range(4):
                at = pl.multiple_of((step * 4 + inner) * TILE, TILE)
                value = turned(image[:, pl.ds(at, TILE), :].reshape(TILE * TILE, later))
                for chunk in range(1, CHUNKS):
                    sends[chunk][pl.ds(at, TILE)] = value[
                        :, (chunk - 1) * lanes : chunk * lanes
                    ].reshape(TILE, TILE, lanes)
            return 0

        lax.fori_loop(0, size // (4 * TILE), some, 0)

    def halves(piece):
        count = piece_rows[piece] // 2
        return ((0, 1, 0, count), (1, -1, count, count))

    def block_for(piece, x_to, y_to, low, count):
        start = (y_to * NX + x_to) * rows + first_row[piece] + low
        return sends[PIECES[piece][0]].at[pl.ds(start, count)]

    def place(piece, x_from, y_from, low, count):
        return got[piece].at[low : low + count, tile_at(y_from * NX + x_from)]

    def spread(piece, rings=range(NY)):
        for half, sign, low, count in halves(piece) if piece != LAST else ():
            for j, ((dx, dy), (vx, vy), _) in enumerate(routes(sign)[1]):
                if dy in rings:
                    pltpu.make_async_remote_copy(
                        src_ref=block_for(piece, shifted(x, dx, NX), shifted(y, dy, NY), low, count),
                        dst_ref=relay[piece].at[half, j],
                        send_sem=spread_send.at[piece],
                        recv_sem=relay_recv.at[piece, half],
                        device_id=device(shifted(x, vx, NX), shifted(y, vy, NY), z, c),
                        device_id_type=MESH,
                    ).start()
        count = piece_rows[piece]
        for dx, dy in ([route[0] for route in routes(1)[1]] if piece == LAST else []) + routes(1)[0]:
            if dy in rings:
                xd, yd = shifted(x, dx, NX), shifted(y, dy, NY)
                pltpu.make_async_remote_copy(
                    src_ref=block_for(piece, xd, yd, 0, count),
                    dst_ref=place(piece, x, y, 0, count),
                    send_sem=spread_send.at[piece],
                    recv_sem=spread_recv.at[piece],
                    device_id=device(xd, yd, z, c),
                    device_id_type=MESH,
                ).start()
        if 0 in rings:
            pltpu.make_async_copy(
                block_for(piece, x, y, 0, count), place(piece, x, y, 0, count), spread_recv.at[piece]
            ).start()

    def forward(piece):
        if RELAYS == 0:
            return
        for half, sign, low, count in halves(piece):
            arrived = relay[piece].at[half]
            pltpu.make_async_copy(arrived, arrived, relay_recv.at[piece, half]).wait()
            for j, (_, (vx, vy), (fx, fy)) in enumerate(routes(sign)[1]):
                pltpu.make_async_remote_copy(
                    src_ref=relay[piece].at[half, j],
                    dst_ref=place(piece, shifted(x, -vx, NX), shifted(y, -vy, NY), low, count),
                    send_sem=relay_send.at[piece],
                    recv_sem=spread_recv.at[piece],
                    device_id=device(shifted(x, fx, NX), shifted(y, fy, NY), z, c),
                    device_id_type=MESH,
                ).start()

    def order_copy(dy):
        return pltpu.make_async_remote_copy(
            src_ref=orders_own,
            dst_ref=orders.at[y],
            send_sem=order_send.at[dy],
            recv_sem=order_sem.at[0],
            device_id=device(x, shifted(y, dy, NY), z, c),
            device_id_type=MESH,
        )

    def make_pick():
        pltpu.make_async_copy(orders, orders, order_sem.at[0]).wait()
        line = lax.broadcasted_iota(jnp.int32, (SECTORS_HERE, targets), 0)
        blocks = []
        for yy in range(NY):
            for xx in range(NX):
                for group in range(GROUPS_HERE):
                    wanted = orders[yy, group : group + 1, :]
                    first = (xx * NZ + z) * SECTORS_HERE
                    blocks.append(jnp.where(wanted == line + first, 1.0, 0.0))
        table = jnp.concatenate(blocks, 0).T
        half = targets // NC
        for xh in range(NC):
            blocks = []
            for zz in range(NZ):
                for part in range(X_PART):
                    low = ((xh * X_PART + part) * NZ + zz) * SECTORS_HERE
                    blocks.append(table[low : low + SECTORS_HERE])
            start = pl.multiple_of((1 - c if xh == 0 else c) * half, half)
            pick[pl.ds(start, half), :] = jnp.concatenate(blocks, 0).astype(jnp.bfloat16)

    def gather(piece):
        pltpu.make_async_copy(got[piece], got[piece], spread_recv.at[piece]).wait()
        half = targets // NC

        def some(step, _):
            for inner in range(4):
                m = step * 8 + inner * 2
                both = jnp.concatenate([got[piece][m], got[piece][m + 1]], 1)
                value = jnp.dot(pick[...], both, preferred_element_type=jnp.float32)
                for part, to in ((0, give[piece]), (1, own[piece])):
                    for zz in range(NZ):
                        low = part * half + zz * TILE
                        for next_m in range(2):
                            to[zz, m + next_m] = value[
                                low : low + TILE, next_m * lanes : (next_m + 1) * lanes
                            ].astype(to.dtype)
            return 0

        lax.fori_loop(0, piece_rows[piece] // 8, some, 0)
        core_copy(piece).start()

    def core_copy(piece):
        return pltpu.make_async_remote_copy(
            src_ref=give[piece],
            dst_ref=take[piece],
            send_sem=core_send.at[piece],
            recv_sem=core_recv.at[piece],
            device_id=device(x, y, z, 1 - c),
            device_id_type=MESH,
        )

    def held(piece, zd, low, count):
        at = slice(low, low + count)
        return own[piece][zd, at] + take[piece][zd, at].astype(jnp.float32)

    def z_buffers(piece, way):
        return (up_out[piece], up_in[piece]) if way > 0 else (down_out[piece], down_in[piece])

    def z_copy(piece, step, way):
        source, target = z_buffers(piece, way)
        out_sem, in_sem = (up_send, up_recv) if way > 0 else (down_send, down_recv)
        at = (step,)
        if step == 0:
            _, _, low, count = halves(piece)[0 if way > 0 else 1]
            at = (step, slice(low, low + count))
        return pltpu.make_async_remote_copy(
            src_ref=source.at[at],
            dst_ref=target.at[at],
            send_sem=out_sem.at[piece, step],
            recv_sem=in_sem.at[piece, step],
            device_id=device(x, y, shifted(z, way, NZ), c),
            device_id_type=MESH,
        )

    def carried(step, way, sign):
        return step > 0 or way == sign

    def chain(piece, step):
        if step >= STEPS:
            return
        if step == 0:
            core_copy(piece).wait_recv()
        for way in (1, -1):
            source, target = z_buffers(piece, way)
            if step > 0:
                z_copy(piece, step - 1, way).wait_recv()
            zd = shifted(z, way * (STEPS - step), NZ)
            for _, sign, low, count in halves(piece):
                if carried(step, way, sign):
                    at = slice(low, low + count)
                    value = held(piece, zd, low, count)
                    if step > 0 and carried(step - 1, way, sign):
                        value = value + target[step - 1, at].astype(jnp.float32)
                    source[step, at] = value.astype(jnp.bfloat16)
            z_copy(piece, step, way).start()

    def final_copies(piece, part):
        xd = c * X_PART + part
        spot_there = final[piece].at[lax.rem(x, X_PART)]
        there = dict(
            src_ref=done[piece].at[part],
            dst_ref=spot_there,
            send_sem=final_send.at[piece, part],
            recv_sem=final_recv.at[piece],
            device_id=device(xd, y, z, lax.div(x, X_PART)),
            device_id_type=MESH,
        )
        here = (done[piece].at[part], spot_there, final_recv.at[piece])
        return xd, there, here

    def finish(piece):
        last = STEPS - 1
        for way in (1, -1):
            z_copy(piece, last, way).wait_recv()
        for _, sign, low, count in halves(piece):
            value = held(piece, z, low, count)
            for way in (1, -1):
                if carried(last, way, sign):
                    value = value + z_buffers(piece, way)[1][last, low : low + count].astype(jnp.float32)
            for part in range(X_PART):
                at = slice(part * SECTORS_HERE, (part + 1) * SECTORS_HERE)
                done[piece][part, low // 2 : (low + count) // 2] = (
                    value[:, at, :].reshape(count // 2, TILE, lanes).astype(jnp.bfloat16)
                )
        for part in range(X_PART):
            xd, there, here = final_copies(piece, part)

            @pl.when(xd != x)
            def _():
                pltpu.make_async_remote_copy(**there).start()

            @pl.when(xd == x)
            def _():
                pltpu.make_async_copy(*here).start()

    def put(piece):
        pltpu.make_async_copy(final[piece], final[piece], final_recv.at[piece]).wait()
        chunk, count = PIECES[piece][0], piece_rows[piece]
        total = X_PART * count * SECTORS_HERE
        row = lax.broadcasted_iota(jnp.int32, (total, total), 0)
        column = lax.broadcasted_iota(jnp.int32, (total, total), 1)
        sector = column & (SECTORS_HERE - 1)
        line = lax.shift_right_logical(column, 3)
        value = jnp.dot(
            ones_where(row == sector * (X_PART * count) + line),
            final[piece][...].reshape(total, lanes),
            preferred_element_type=jnp.float32,
        )
        for sector in range(SECTORS_HERE):
            for part in range(X_PART):
                low = part * rows + first_row[piece]
                start = (sector * X_PART + part) * count
                m = term * (X_PART * rows) + low + lax.broadcasted_iota(jnp.int32, (count, lanes), 0)
                i = chunk * lanes + lax.broadcasted_iota(jnp.int32, (count, lanes), 1)
                keep = (i < widths[0, sector]) & (m < widths[1, sector])
                out[sector, low : low + count, chunk * lanes : (chunk + 1) * lanes] = jnp.where(
                    keep, value[start : start + count], 0.0
                )

    first_parts()
    for part in range(2):
        rings = y_order[part * NY // 2 : (part + 1) * NY // 2]
        first_images(rings, part == 0)
        if part == 0:
            pl.semaphore_wait(barrier, len(others))
        spread(0, rings)
    for dy in range(1, NY):
        order_copy(dy).start()
    pltpu.make_async_copy(orders_own, orders.at[y], order_sem.at[0]).start()
    later_parts()
    forward(0)
    later_images()
    spread(1)
    make_pick()
    gather(0)
    forward(1)
    spread(2)
    chain(0, 0)
    spread(3)
    chain(0, 1)
    chain(0, 2)
    gather(1)
    chain(0, 3)
    forward(2)
    chain(1, 0)
    finish(0)
    chain(1, 1)
    put(0)
    chain(1, 2)
    gather(2)
    chain(1, 3)
    chain(2, 0)
    gather(3)
    finish(1)
    chain(3, 0)
    chain(2, 1)
    chain(3, 1)
    put(1)
    chain(2, 2)
    chain(3, 2)
    chain(2, 3)
    chain(3, 3)
    finish(2)
    finish(3)
    put(2)
    put(3)

    for dy in range(1, NY):
        order_copy(dy).wait_send()
    for piece in pieces:
        sent = sends[PIECES[piece][0]].at[0 : (SLOTS - 1) * piece_rows[piece]]
        pltpu.make_async_copy(sent, sent, spread_send.at[piece]).wait()
        if RELAYS and piece != LAST:
            pltpu.make_async_copy(relay[piece], relay[piece], relay_send.at[piece]).wait()
        core_copy(piece).wait_send()
        for step in range(STEPS):
            for way in (1, -1):
                z_copy(piece, step, way).wait_send()
        for part in range(X_PART):
            xd, there, _ = final_copies(piece, part)

            @pl.when(xd != x)
            def _():
                pltpu.make_async_remote_copy(**there).wait_send()


def shards(psi, left_ops, right_ops, pair_src, widths):
    size = psi.shape[1]
    targets = pair_src.shape[1]
    rows, lanes = size // SLOTS, size // CHUNKS
    bf, count = jnp.bfloat16, len(PIECES)
    tile = (TILE, lanes)
    scratch = [
        pltpu.VMEM(psi.shape, bf),
        pltpu.VMEM(left_ops.shape, bf),
        pltpu.VMEM(right_ops.shape, bf),
        pltpu.VMEM((8, targets), jnp.int32),
        pltpu.VMEM((NY, 8, targets), jnp.int32),
        pltpu.VMEM((SECTORS_HERE, GROUPS_HERE * (size - lanes), size), bf),
        pltpu.VMEM((TILE, size, size - lanes), bf),
        pltpu.VMEM((TILE * TILE, TILE * TILE), bf),
        pltpu.VMEM((targets, SOURCES), bf),
        *[pltpu.VMEM((size,) + tile, bf) for _ in range(CHUNKS)],
    ]
    for _, _, thirds in PIECES:
        here = rows * thirds // 3
        ring = pltpu.VMEM((STEPS, here) + tile, bf)
        scratch += [
            pltpu.VMEM((here, SOURCES, lanes), bf),
            pltpu.VMEM((2, max(RELAYS, 1), here // 2) + tile, bf),
            pltpu.VMEM((NZ, here) + tile, bf),
            pltpu.VMEM((NZ, here) + tile, bf),
            pltpu.VMEM((NZ, here) + tile, jnp.float32),
            ring, ring, ring, ring,
            pltpu.VMEM((X_PART, here // 2) + tile, bf),
            pltpu.VMEM((X_PART, here // 2) + tile, bf),
        ]
    dma = pltpu.SemaphoreType.DMA
    scratch += [
        dma((4, SECTORS_HERE)), dma((1,)), dma((NY,)), dma((count,)), dma((count,)),
        dma((count, 2)), dma((count,)), dma((count,)), dma((count,)),
        dma((count, STEPS)), dma((count, STEPS)), dma((count, STEPS)), dma((count, STEPS)),
        dma((count, X_PART)), dma((count,)),
    ]
    summed = pl.pallas_call(
        kernel,
        out_shape=jax.ShapeDtypeStruct((SECTORS_HERE, X_PART * rows, size), jnp.float32),
        in_specs=[
            pl.BlockSpec(memory_space=pltpu.VMEM),
            pl.BlockSpec(memory_space=pltpu.SMEM),
            pl.BlockSpec(memory_space=pl.ANY),
            pl.BlockSpec(memory_space=pl.ANY),
            pl.BlockSpec(memory_space=pl.ANY),
        ],
        out_specs=pl.BlockSpec(memory_space=pltpu.VMEM),
        scratch_shapes=scratch,
        compiler_params=pltpu.CompilerParams(
            collective_id=0, has_side_effects=True, vmem_limit_bytes=56 * 1024 * 1024
        ),
        cost_estimate=pl.CostEstimate(
            flops=64 * size**3, bytes_accessed=40 * size * size * 2, transcendentals=0
        ),
    )(pair_src, widths, psi, left_ops, right_ops)

    return jnp.swapaxes(summed, 1, 2)


def solution(mesh):
    return jax.shard_map(
        shards,
        mesh=mesh,
        in_specs=(
            P("sec", None, None),
            P("term", "sec", None, None),
            P("term", "sec", None, None),
            P("term", None),
            P(None, "sec"),
        ),
        out_specs=P("sec", None, "term"),
        check_vma=False,
    )
```

```python
import jax
import jax.numpy as jnp
from jax import lax
from jax.experimental import pallas as pl
from jax.experimental.pallas import tpu as pltpu
from jax.sharding import PartitionSpec as P

NX, NY, NZ, NC = 4, 4, 8, 2
CHUNKS = 3
PIECES = ((0, 0, 3), (1, 0, 3), (2, 0, 2), (2, 2, 1))
SLOTS = NX * NY
GROUPS_HERE = 2
SECTORS_HERE = 8
TILE = GROUPS_HERE * SECTORS_HERE
SOURCES = SLOTS * TILE
X_PART = NX // NC
STEPS = NZ // 2
MESH = pl.DeviceIdType.MESH
BUFFERS = 11


def routes(sign):
    direct, relayed = [], []
    for dx in range(NX):
        for dy in range(NY):
            far_x, far_y = NX > 2 and dx == NX // 2, NY > 2 and dy == NY // 2
            if far_x or far_y:
                via = (sign if far_x else 0, sign if far_y else 0)
                relayed.append(((dx, dy), via, (dx - via[0], dy - via[1])))
            elif (dx, dy) != (0, 0):
                direct.append((dx, dy))
    return direct, relayed


RELAYS = len(routes(1)[1])


def device(x, y, z, c):
    return (x * NZ + z, y * NC + c)


def ones_where(condition):
    return jnp.where(condition, 1.0, 0.0).astype(jnp.bfloat16)


def tile_at(index):
    return pl.ds(pl.multiple_of(index * TILE, TILE), TILE)


def kernel(pair_src, widths, psi, left, right, out, *rest):
    psi_v, left_v, right_v, orders_own, orders, parts, image, swap, pick, *rest = rest
    sends, rest = rest[:CHUNKS], rest[CHUNKS:]
    buffers = [rest[i * BUFFERS : (i + 1) * BUFFERS] for i in range(len(PIECES))]
    (
        load_sem, order_sem, order_send, spread_send, spread_recv, relay_recv, relay_send, core_send, core_recv,
        up_send, up_recv, down_send, down_recv, final_send, final_recv,
    ) = rest[len(PIECES) * BUFFERS :]
    got, relay, give, take, own, up_out, up_in, down_out, down_in, done, final = zip(*buffers)
    sec, term = lax.axis_index("sec"), lax.axis_index("term")
    x, z = lax.div(sec, NZ), lax.rem(sec, NZ)
    y, c = lax.div(term, NC), lax.rem(term, NC)
    size = psi_v.shape[-1]
    rows = size // SLOTS
    lanes = size // CHUNKS
    targets = pair_src.shape[1]
    pieces = range(len(PIECES))
    y_order = sorted(range(NY), key=lambda dy: -min(dy, NY - dy))
    first_row = [rows * at // 3 for _, at, _ in PIECES]
    piece_rows = [rows * count // 3 for _, _, count in PIECES]

    def shifted(value, by, count):
        return lax.rem(value + (by % count), count)

    barrier = pltpu.get_barrier_semaphore()
    others = [
        device(shifted(x, dx, NX), shifted(y, dy, NY), z, c)
        for dx in range(NX)
        for dy in range(NY)
        if (dx, dy) != (0, 0)
    ]
    others += [device(shifted(x, dx, NX), y, z, 1 - c) for dx in range(NX)]
    others += [device(x, y, shifted(z, 1, NZ), c), device(x, y, shifted(z, -1, NZ), c)]
    for other in others:
        pl.semaphore_signal(barrier, inc=1, device_id=other, device_id_type=MESH)

    def loads(k):
        return (
            pltpu.make_async_copy(psi.at[k], psi_v.at[k], load_sem.at[0, k]),
            pltpu.make_async_copy(
                left.at[:, k, 0:lanes], left_v.at[:, k, 0:lanes], load_sem.at[1, k]
            ),
            pltpu.make_async_copy(right.at[:, k], right_v.at[:, k], load_sem.at[2, k]),
            pltpu.make_async_copy(
                left.at[:, k, lanes:size], left_v.at[:, k, lanes:size], load_sem.at[3, k]
            ),
        )

    for which in ((0, 1), (2,), (3,)):
        for k in range(SECTORS_HERE):
            for copy in which:
                loads(k)[copy].start()

    row = lax.broadcasted_iota(jnp.int32, swap.shape, 0)
    column = lax.broadcasted_iota(jnp.int32, swap.shape, 1)
    swap[...] = ones_where(row == (column & (TILE - 1)) * TILE + lax.shift_right_logical(column, 4))
    orders_own[...] = jnp.concatenate([pair_src[...], jnp.zeros((6, targets), jnp.int32)], 0)

    def image_of(right_block, part):
        return lax.dot_general(
            right_block, part, (((1,), (1,)), ((), ())), preferred_element_type=jnp.float32
        ).astype(jnp.bfloat16)

    def turned(block):
        return jnp.dot(swap[...], block, preferred_element_type=jnp.float32).astype(jnp.bfloat16)

    def each_sector(body):
        def some(step, _):
            for inner in range(2):
                body(step * 2 + inner)
            return 0

        lax.fori_loop(0, SECTORS_HERE // 2, some, 0)

    def first_parts():
        def one(k):
            for copy in loads(k)[:2]:
                copy.wait()
            keep = (lax.broadcasted_iota(jnp.int32, (size, size), 0) < widths[0, k]) & (
                lax.broadcasted_iota(jnp.int32, (size, size), 1) < widths[1, k]
            )
            masked = jnp.where(keep, psi_v[k].astype(jnp.float32), 0.0).astype(jnp.bfloat16)
            psi_v[k] = masked
            here = left_v[:, k, 0:lanes, :].reshape(GROUPS_HERE * lanes, size)
            parts[k, 0 : GROUPS_HERE * lanes] = jnp.dot(
                here, masked, preferred_element_type=jnp.float32
            ).astype(jnp.bfloat16)

        each_sector(one)

    def first_images(rings, first):
        count = size // NY
        starts = [pl.multiple_of(shifted(y, dy, NY) * count, 2 * TILE) for dy in rings]

        def one(k):
            if first:
                loads(k)[2].wait()
            for group in range(GROUPS_HERE):
                chosen = jnp.concatenate([right_v[group, k, pl.ds(start, count), :] for start in starts], 0)
                image[group * SECTORS_HERE + k, 0 : count * len(starts), 0:lanes] = image_of(
                    chosen, parts[k, group * lanes : (group + 1) * lanes, :]
                )

        each_sector(one)
        for low in range(0, count * len(starts), 2 * TILE):
            both = turned(
                jnp.concatenate(
                    [
                        image[:, at : at + TILE, 0:lanes].reshape(TILE * TILE, lanes)
                        for at in (low, low + TILE)
                    ],
                    1,
                )
            )
            for part in range(2):
                at = starts[low // count] + low % count + part * TILE
                sends[0][pl.ds(at, TILE)] = both[:, part * lanes : (part + 1) * lanes].reshape(
                    TILE, TILE, lanes
                )

    later = size - lanes

    def later_parts():
        def one(k):
            loads(k)[3].wait()
            here = left_v[:, k, lanes:, :].reshape(GROUPS_HERE * later, size)
            parts[k] = jnp.dot(here, psi_v[k], preferred_element_type=jnp.float32).astype(jnp.bfloat16)

        each_sector(one)

    def later_images():
        def one(k):
            for group in range(GROUPS_HERE):
                image[group * SECTORS_HERE + k] = image_of(
                    right_v[group, k], parts[k, group * later : (group + 1) * later, :]
                )

        each_sector(one)

        def some(step, _):
            for inner in range(4):
                at = pl.multiple_of((step * 4 + inner) * TILE, TILE)
                value = turned(image[:, pl.ds(at, TILE), :].reshape(TILE * TILE, later))
                for chunk in range(1, CHUNKS):
                    sends[chunk][pl.ds(at, TILE)] = value[
                        :, (chunk - 1) * lanes : chunk * lanes
                    ].reshape(TILE, TILE, lanes)
            return 0

        lax.fori_loop(0, size // (4 * TILE), some, 0)

    def halves(piece):
        count = piece_rows[piece] // 2
        return ((0, 1, 0, count), (1, -1, count, count))

    def block_for(piece, x_to, y_to, low, count):
        start = (y_to * NX + x_to) * rows + first_row[piece] + low
        return sends[PIECES[piece][0]].at[pl.ds(start, count)]

    def place(piece, x_from, y_from, low, count):
        return got[piece].at[low : low + count, tile_at(y_from * NX + x_from)]

    def spread(piece, rings=range(NY)):
        for half, sign, low, count in halves(piece):
            for j, ((dx, dy), (vx, vy), _) in enumerate(routes(sign)[1]):
                if dy in rings:
                    pltpu.make_async_remote_copy(
                        src_ref=block_for(piece, shifted(x, dx, NX), shifted(y, dy, NY), low, count),
                        dst_ref=relay[piece].at[half, j],
                        send_sem=spread_send.at[piece],
                        recv_sem=relay_recv.at[piece, half],
                        device_id=device(shifted(x, vx, NX), shifted(y, vy, NY), z, c),
                        device_id_type=MESH,
                    ).start()
        count = piece_rows[piece]
        for dx, dy in routes(1)[0]:
            if dy in rings:
                xd, yd = shifted(x, dx, NX), shifted(y, dy, NY)
                pltpu.make_async_remote_copy(
                    src_ref=block_for(piece, xd, yd, 0, count),
                    dst_ref=place(piece, x, y, 0, count),
                    send_sem=spread_send.at[piece],
                    recv_sem=spread_recv.at[piece],
                    device_id=device(xd, yd, z, c),
                    device_id_type=MESH,
                ).start()
        if 0 in rings:
            pltpu.make_async_copy(
                block_for(piece, x, y, 0, count), place(piece, x, y, 0, count), spread_recv.at[piece]
            ).start()

    def forward(piece):
        if RELAYS == 0:
            return
        for half, sign, low, count in halves(piece):
            arrived = relay[piece].at[half]
            pltpu.make_async_copy(arrived, arrived, relay_recv.at[piece, half]).wait()
            for j, (_, (vx, vy), (fx, fy)) in enumerate(routes(sign)[1]):
                pltpu.make_async_remote_copy(
                    src_ref=relay[piece].at[half, j],
                    dst_ref=place(piece, shifted(x, -vx, NX), shifted(y, -vy, NY), low, count),
                    send_sem=relay_send.at[piece],
                    recv_sem=spread_recv.at[piece],
                    device_id=device(shifted(x, fx, NX), shifted(y, fy, NY), z, c),
                    device_id_type=MESH,
                ).start()

    def order_copy(dy):
        return pltpu.make_async_remote_copy(
            src_ref=orders_own,
            dst_ref=orders.at[y],
            send_sem=order_send.at[dy],
            recv_sem=order_sem.at[0],
            device_id=device(x, shifted(y, dy, NY), z, c),
            device_id_type=MESH,
        )

    def make_pick():
        pltpu.make_async_copy(orders, orders, order_sem.at[0]).wait()
        line = lax.broadcasted_iota(jnp.int32, (SECTORS_HERE, targets), 0)
        blocks = []
        for yy in range(NY):
            for xx in range(NX):
                for group in range(GROUPS_HERE):
                    wanted = orders[yy, group : group + 1, :]
                    first = (xx * NZ + z) * SECTORS_HERE
                    blocks.append(jnp.where(wanted == line + first, 1.0, 0.0))
        table = jnp.concatenate(blocks, 0).T
        half = targets // NC
        for xh in range(NC):
            blocks = []
            for zz in range(NZ):
                for part in range(X_PART):
                    low = ((xh * X_PART + part) * NZ + zz) * SECTORS_HERE
                    blocks.append(table[low : low + SECTORS_HERE])
            start = pl.multiple_of((1 - c if xh == 0 else c) * half, half)
            pick[pl.ds(start, half), :] = jnp.concatenate(blocks, 0).astype(jnp.bfloat16)

    def gather(piece):
        pltpu.make_async_copy(got[piece], got[piece], spread_recv.at[piece]).wait()
        half = targets // NC

        def some(step, _):
            for inner in range(4):
                m = step * 8 + inner * 2
                both = jnp.concatenate([got[piece][m], got[piece][m + 1]], 1)
                value = jnp.dot(pick[...], both, preferred_element_type=jnp.float32)
                for part, to in ((0, give[piece]), (1, own[piece])):
                    for zz in range(NZ):
                        low = part * half + zz * TILE
                        for next_m in range(2):
                            to[zz, m + next_m] = value[
                                low : low + TILE, next_m * lanes : (next_m + 1) * lanes
                            ].astype(to.dtype)
            return 0

        lax.fori_loop(0, piece_rows[piece] // 8, some, 0)
        core_copy(piece).start()

    def core_copy(piece):
        return pltpu.make_async_remote_copy(
            src_ref=give[piece],
            dst_ref=take[piece],
            send_sem=core_send.at[piece],
            recv_sem=core_recv.at[piece],
            device_id=device(x, y, z, 1 - c),
            device_id_type=MESH,
        )

    def held(piece, zd, low, count):
        at = slice(low, low + count)
        return own[piece][zd, at] + take[piece][zd, at].astype(jnp.float32)

    def z_buffers(piece, way):
        return (up_out[piece], up_in[piece]) if way > 0 else (down_out[piece], down_in[piece])

    def z_copy(piece, step, way):
        source, target = z_buffers(piece, way)
        out_sem, in_sem = (up_send, up_recv) if way > 0 else (down_send, down_recv)
        at = (step,)
        if step == 0:
            _, _, low, count = halves(piece)[0 if way > 0 else 1]
            at = (step, slice(low, low + count))
        return pltpu.make_async_remote_copy(
            src_ref=source.at[at],
            dst_ref=target.at[at],
            send_sem=out_sem.at[piece, step],
            recv_sem=in_sem.at[piece, step],
            device_id=device(x, y, shifted(z, way, NZ), c),
            device_id_type=MESH,
        )

    def carried(step, way, sign):
        return step > 0 or way == sign

    def chain(piece, step):
        if step >= STEPS:
            return
        if step == 0:
            core_copy(piece).wait_recv()
        for way in (1, -1):
            source, target = z_buffers(piece, way)
            if step > 0:
                z_copy(piece, step - 1, way).wait_recv()
            zd = shifted(z, way * (STEPS - step), NZ)
            for _, sign, low, count in halves(piece):
                if carried(step, way, sign):
                    at = slice(low, low + count)
                    value = held(piece, zd, low, count)
                    if step > 0 and carried(step - 1, way, sign):
                        value = value + target[step - 1, at].astype(jnp.float32)
                    source[step, at] = value.astype(jnp.bfloat16)
            z_copy(piece, step, way).start()

    def final_copies(piece, part):
        xd = c * X_PART + part
        spot_there = final[piece].at[lax.rem(x, X_PART)]
        there = dict(
            src_ref=done[piece].at[part],
            dst_ref=spot_there,
            send_sem=final_send.at[piece, part],
            recv_sem=final_recv.at[piece],
            device_id=device(xd, y, z, lax.div(x, X_PART)),
            device_id_type=MESH,
        )
        here = (done[piece].at[part], spot_there, final_recv.at[piece])
        return xd, there, here

    def finish(piece):
        last = STEPS - 1
        for way in (1, -1):
            z_copy(piece, last, way).wait_recv()
        for _, sign, low, count in halves(piece):
            value = held(piece, z, low, count)
            for way in (1, -1):
                if carried(last, way, sign):
                    value = value + z_buffers(piece, way)[1][last, low : low + count].astype(jnp.float32)
            for part in range(X_PART):
                at = slice(part * SECTORS_HERE, (part + 1) * SECTORS_HERE)
                done[piece][part, low // 2 : (low + count) // 2] = (
                    value[:, at, :].reshape(count // 2, TILE, lanes).astype(jnp.bfloat16)
                )
        for part in range(X_PART):
            xd, there, here = final_copies(piece, part)

            @pl.when(xd != x)
            def _():
                pltpu.make_async_remote_copy(**there).start()

            @pl.when(xd == x)
            def _():
                pltpu.make_async_copy(*here).start()

    def put(piece):
        pltpu.make_async_copy(final[piece], final[piece], final_recv.at[piece]).wait()
        chunk, count = PIECES[piece][0], piece_rows[piece]
        total = X_PART * count * SECTORS_HERE
        row = lax.broadcasted_iota(jnp.int32, (total, total), 0)
        column = lax.broadcasted_iota(jnp.int32, (total, total), 1)
        sector = column & (SECTORS_HERE - 1)
        line = lax.shift_right_logical(column, 3)
        value = jnp.dot(
            ones_where(row == sector * (X_PART * count) + line),
            final[piece][...].reshape(total, lanes),
            preferred_element_type=jnp.float32,
        )
        for sector in range(SECTORS_HERE):
            for part in range(X_PART):
                low = part * rows + first_row[piece]
                start = (sector * X_PART + part) * count
                m = term * (X_PART * rows) + low + lax.broadcasted_iota(jnp.int32, (count, lanes), 0)
                i = chunk * lanes + lax.broadcasted_iota(jnp.int32, (count, lanes), 1)
                keep = (i < widths[0, sector]) & (m < widths[1, sector])
                out[sector, low : low + count, chunk * lanes : (chunk + 1) * lanes] = jnp.where(
                    keep, value[start : start + count], 0.0
                )

    first_parts()
    first_images(y_order[:1], True)
    pl.semaphore_wait(barrier, len(others))
    spread(0, y_order[:1])
    first_images(y_order[1:], False)
    spread(0, y_order[1:])
    for dy in range(1, NY):
        order_copy(dy).start()
    pltpu.make_async_copy(orders_own, orders.at[y], order_sem.at[0]).start()
    later_parts()
    forward(0)
    later_images()
    spread(1)
    make_pick()
    gather(0)
    forward(1)
    spread(2)
    chain(0, 0)
    spread(3)
    chain(0, 1)
    chain(0, 2)
    gather(1)
    chain(0, 3)
    forward(2)
    chain(1, 0)
    finish(0)
    chain(1, 1)
    forward(3)
    put(0)
    chain(1, 2)
    gather(2)
    chain(1, 3)
    chain(2, 0)
    gather(3)
    finish(1)
    chain(3, 0)
    chain(2, 1)
    chain(3, 1)
    put(1)
    chain(2, 2)
    chain(3, 2)
    chain(2, 3)
    chain(3, 3)
    finish(2)
    finish(3)
    put(2)
    put(3)

    for dy in range(1, NY):
        order_copy(dy).wait_send()
    for piece in pieces:
        sent = sends[PIECES[piece][0]].at[0 : (SLOTS - 1) * piece_rows[piece]]
        pltpu.make_async_copy(sent, sent, spread_send.at[piece]).wait()
        if RELAYS:
            pltpu.make_async_copy(relay[piece], relay[piece], relay_send.at[piece]).wait()
        core_copy(piece).wait_send()
        for step in range(STEPS):
            for way in (1, -1):
                z_copy(piece, step, way).wait_send()
        for part in range(X_PART):
            xd, there, _ = final_copies(piece, part)

            @pl.when(xd != x)
            def _():
                pltpu.make_async_remote_copy(**there).wait_send()


def shards(psi, left_ops, right_ops, pair_src, widths):
    size = psi.shape[1]
    targets = pair_src.shape[1]
    rows, lanes = size // SLOTS, size // CHUNKS
    bf, count = jnp.bfloat16, len(PIECES)
    tile = (TILE, lanes)
    scratch = [
        pltpu.VMEM(psi.shape, bf),
        pltpu.VMEM(left_ops.shape, bf),
        pltpu.VMEM(right_ops.shape, bf),
        pltpu.VMEM((8, targets), jnp.int32),
        pltpu.VMEM((NY, 8, targets), jnp.int32),
        pltpu.VMEM((SECTORS_HERE, GROUPS_HERE * (size - lanes), size), bf),
        pltpu.VMEM((TILE, size, size - lanes), bf),
        pltpu.VMEM((TILE * TILE, TILE * TILE), bf),
        pltpu.VMEM((targets, SOURCES), bf),
        *[pltpu.VMEM((size,) + tile, bf) for _ in range(CHUNKS)],
    ]
    for _, _, thirds in PIECES:
        here = rows * thirds // 3
        ring = pltpu.VMEM((STEPS, here) + tile, bf)
        scratch += [
            pltpu.VMEM((here, SOURCES, lanes), bf),
            pltpu.VMEM((2, max(RELAYS, 1), here // 2) + tile, bf),
            pltpu.VMEM((NZ, here) + tile, bf),
            pltpu.VMEM((NZ, here) + tile, bf),
            pltpu.VMEM((NZ, here) + tile, jnp.float32),
            ring, ring, ring, ring,
            pltpu.VMEM((X_PART, here // 2) + tile, bf),
            pltpu.VMEM((X_PART, here // 2) + tile, bf),
        ]
    dma = pltpu.SemaphoreType.DMA
    scratch += [
        dma((4, SECTORS_HERE)), dma((1,)), dma((NY,)), dma((count,)), dma((count,)),
        dma((count, 2)), dma((count,)), dma((count,)), dma((count,)),
        dma((count, STEPS)), dma((count, STEPS)), dma((count, STEPS)), dma((count, STEPS)),
        dma((count, X_PART)), dma((count,)),
    ]
    summed = pl.pallas_call(
        kernel,
        out_shape=jax.ShapeDtypeStruct((SECTORS_HERE, X_PART * rows, size), jnp.float32),
        in_specs=[
            pl.BlockSpec(memory_space=pltpu.VMEM),
            pl.BlockSpec(memory_space=pltpu.SMEM),
            pl.BlockSpec(memory_space=pl.ANY),
            pl.BlockSpec(memory_space=pl.ANY),
            pl.BlockSpec(memory_space=pl.ANY),
        ],
        out_specs=pl.BlockSpec(memory_space=pltpu.VMEM),
        scratch_shapes=scratch,
        compiler_params=pltpu.CompilerParams(
            collective_id=0, has_side_effects=True, vmem_limit_bytes=56 * 1024 * 1024
        ),
        cost_estimate=pl.CostEstimate(
            flops=64 * size**3, bytes_accessed=40 * size * size * 2, transcendentals=0
        ),
    )(pair_src, widths, psi, left_ops, right_ops)

    return jnp.swapaxes(summed, 1, 2)


def solution(mesh):
    return jax.shard_map(
        shards,
        mesh=mesh,
        in_specs=(
            P("sec", None, None),
            P("term", "sec", None, None),
            P("term", "sec", None, None),
            P("term", None),
            P(None, "sec"),
        ),
        out_specs=P("sec", None, "term"),
        check_vma=False,
    )
```

```python
import jax
import jax.numpy as jnp
from jax import lax
from jax.experimental import pallas as pl
from jax.experimental.pallas import tpu as pltpu
from jax.sharding import PartitionSpec as P

NX, NY, NZ, NC = 4, 4, 8, 2
CHUNKS = 3
PIECES = ((0, 0, 3), (1, 0, 3), (2, 0, 2), (2, 2, 1))
SLOTS = NX * NY
GROUPS_HERE = 2
SECTORS_HERE = 8
TILE = GROUPS_HERE * SECTORS_HERE
SOURCES = SLOTS * TILE
X_PART = NX // NC
STEPS = NZ // 2
MESH = pl.DeviceIdType.MESH
BUFFERS = 11


def routes(sign):
    direct, relayed = [], []
    for dx in range(NX):
        for dy in range(NY):
            far_x, far_y = NX > 2 and dx == NX // 2, NY > 2 and dy == NY // 2
            if far_x or far_y:
                via = (sign if far_x else 0, sign if far_y else 0)
                relayed.append(((dx, dy), via, (dx - via[0], dy - via[1])))
            elif (dx, dy) != (0, 0):
                direct.append((dx, dy))
    return direct, relayed


RELAYS = len(routes(1)[1])


def device(x, y, z, c):
    return (x * NZ + z, y * NC + c)


def ones_where(condition):
    return jnp.where(condition, 1.0, 0.0).astype(jnp.bfloat16)


def tile_at(index):
    return pl.ds(pl.multiple_of(index * TILE, TILE), TILE)


def kernel(pair_src, widths, psi, left, right, out, *rest):
    psi_v, left_v, right_v, orders_own, orders, parts, image, swap, pick, *rest = rest
    sends, rest = rest[:CHUNKS], rest[CHUNKS:]
    buffers = [rest[i * BUFFERS : (i + 1) * BUFFERS] for i in range(len(PIECES))]
    (
        load_sem, order_sem, order_send, spread_send, spread_recv, relay_recv, relay_send, core_send, core_recv,
        up_send, up_recv, down_send, down_recv, final_send, final_recv,
    ) = rest[len(PIECES) * BUFFERS :]
    got, relay, give, take, own, up_out, up_in, down_out, down_in, done, final = zip(*buffers)
    sec, term = lax.axis_index("sec"), lax.axis_index("term")
    x, z = lax.div(sec, NZ), lax.rem(sec, NZ)
    y, c = lax.div(term, NC), lax.rem(term, NC)
    size = psi_v.shape[-1]
    rows = size // SLOTS
    lanes = size // CHUNKS
    targets = pair_src.shape[1]
    pieces = range(len(PIECES))
    y_order = sorted(range(NY), key=lambda dy: -min(dy, NY - dy))
    first_row = [rows * at // 3 for _, at, _ in PIECES]
    piece_rows = [rows * count // 3 for _, _, count in PIECES]

    def shifted(value, by, count):
        return lax.rem(value + (by % count), count)

    barrier = pltpu.get_barrier_semaphore()
    others = [
        device(shifted(x, dx, NX), shifted(y, dy, NY), z, c)
        for dx in range(NX)
        for dy in range(NY)
        if (dx, dy) != (0, 0)
    ]
    others += [device(shifted(x, dx, NX), y, z, 1 - c) for dx in range(NX)]
    others += [device(x, y, shifted(z, 1, NZ), c), device(x, y, shifted(z, -1, NZ), c)]
    for other in others:
        pl.semaphore_signal(barrier, inc=1, device_id=other, device_id_type=MESH)

    def loads(k):
        return (
            pltpu.make_async_copy(psi.at[k], psi_v.at[k], load_sem.at[0, k]),
            pltpu.make_async_copy(
                left.at[:, k, 0:lanes], left_v.at[:, k, 0:lanes], load_sem.at[1, k]
            ),
            pltpu.make_async_copy(right.at[:, k], right_v.at[:, k], load_sem.at[2, k]),
            pltpu.make_async_copy(
                left.at[:, k, lanes:size], left_v.at[:, k, lanes:size], load_sem.at[3, k]
            ),
        )

    for which in ((0, 1), (2,), (3,)):
        for k in range(SECTORS_HERE):
            for copy in which:
                loads(k)[copy].start()

    row = lax.broadcasted_iota(jnp.int32, swap.shape, 0)
    column = lax.broadcasted_iota(jnp.int32, swap.shape, 1)
    swap[...] = ones_where(row == (column & (TILE - 1)) * TILE + lax.shift_right_logical(column, 4))
    orders_own[...] = jnp.concatenate([pair_src[...], jnp.zeros((6, targets), jnp.int32)], 0)

    def image_of(right_block, part):
        return lax.dot_general(
            right_block, part, (((1,), (1,)), ((), ())), preferred_element_type=jnp.float32
        ).astype(jnp.bfloat16)

    def turned(block):
        return jnp.dot(swap[...], block, preferred_element_type=jnp.float32).astype(jnp.bfloat16)

    def each_sector(body):
        def some(step, _):
            for inner in range(2):
                body(step * 2 + inner)
            return 0

        lax.fori_loop(0, SECTORS_HERE // 2, some, 0)

    def first_parts():
        def one(k):
            for copy in loads(k)[:2]:
                copy.wait()
            keep = (lax.broadcasted_iota(jnp.int32, (size, size), 0) < widths[0, k]) & (
                lax.broadcasted_iota(jnp.int32, (size, size), 1) < widths[1, k]
            )
            masked = jnp.where(keep, psi_v[k].astype(jnp.float32), 0.0).astype(jnp.bfloat16)
            psi_v[k] = masked
            here = left_v[:, k, 0:lanes, :].reshape(GROUPS_HERE * lanes, size)
            parts[k, 0 : GROUPS_HERE * lanes] = jnp.dot(
                here, masked, preferred_element_type=jnp.float32
            ).astype(jnp.bfloat16)

        each_sector(one)

    def first_images(rings, first):
        count = size // NY
        starts = [pl.multiple_of(shifted(y, dy, NY) * count, 2 * TILE) for dy in rings]

        def one(k):
            if first:
                loads(k)[2].wait()
            for group in range(GROUPS_HERE):
                chosen = jnp.concatenate([right_v[group, k, pl.ds(start, count), :] for start in starts], 0)
                image[group * SECTORS_HERE + k, 0 : count * len(starts), 0:lanes] = image_of(
                    chosen, parts[k, group * lanes : (group + 1) * lanes, :]
                )

        each_sector(one)
        for low in range(0, count * len(starts), 2 * TILE):
            both = turned(
                jnp.concatenate(
                    [
                        image[:, at : at + TILE, 0:lanes].reshape(TILE * TILE, lanes)
                        for at in (low, low + TILE)
                    ],
                    1,
                )
            )
            for part in range(2):
                at = starts[low // count] + low % count + part * TILE
                sends[0][pl.ds(at, TILE)] = both[:, part * lanes : (part + 1) * lanes].reshape(
                    TILE, TILE, lanes
                )

    later = size - lanes

    def later_parts():
        def one(k):
            loads(k)[3].wait()
            here = left_v[:, k, lanes:, :].reshape(GROUPS_HERE * later, size)
            parts[k] = jnp.dot(here, psi_v[k], preferred_element_type=jnp.float32).astype(jnp.bfloat16)

        each_sector(one)

    def later_images():
        def one(k):
            for group in range(GROUPS_HERE):
                image[group * SECTORS_HERE + k] = image_of(
                    right_v[group, k], parts[k, group * later : (group + 1) * later, :]
                )

        each_sector(one)

    def later_turn(dy):
        count = size // NY
        start = shifted(y, dy, NY) * count

        def some(step, _):
            for inner in range(3):
                at = pl.multiple_of(start + (step * 3 + inner) * TILE, TILE)
                value = turned(image[:, pl.ds(at, TILE), :].reshape(TILE * TILE, later))
                for chunk in range(1, CHUNKS):
                    sends[chunk][pl.ds(at, TILE)] = value[
                        :, (chunk - 1) * lanes : chunk * lanes
                    ].reshape(TILE, TILE, lanes)
            return 0

        lax.fori_loop(0, count // (3 * TILE), some, 0)

    def halves(piece):
        count = piece_rows[piece] // 2
        return ((0, 1, 0, count), (1, -1, count, count))

    def block_for(piece, x_to, y_to, low, count):
        start = (y_to * NX + x_to) * rows + first_row[piece] + low
        return sends[PIECES[piece][0]].at[pl.ds(start, count)]

    def place(piece, x_from, y_from, low, count):
        return got[piece].at[low : low + count, tile_at(y_from * NX + x_from)]

    def spread(piece, rings=range(NY)):
        for half, sign, low, count in halves(piece):
            for j, ((dx, dy), (vx, vy), _) in enumerate(routes(sign)[1]):
                if dy in rings:
                    pltpu.make_async_remote_copy(
                        src_ref=block_for(piece, shifted(x, dx, NX), shifted(y, dy, NY), low, count),
                        dst_ref=relay[piece].at[half, j],
                        send_sem=spread_send.at[piece],
                        recv_sem=relay_recv.at[piece, half],
                        device_id=device(shifted(x, vx, NX), shifted(y, vy, NY), z, c),
                        device_id_type=MESH,
                    ).start()
        count = piece_rows[piece]
        for dx, dy in routes(1)[0]:
            if dy in rings:
                xd, yd = shifted(x, dx, NX), shifted(y, dy, NY)
                pltpu.make_async_remote_copy(
                    src_ref=block_for(piece, xd, yd, 0, count),
                    dst_ref=place(piece, x, y, 0, count),
                    send_sem=spread_send.at[piece],
                    recv_sem=spread_recv.at[piece],
                    device_id=device(xd, yd, z, c),
                    device_id_type=MESH,
                ).start()
        if 0 in rings:
            pltpu.make_async_copy(
                block_for(piece, x, y, 0, count), place(piece, x, y, 0, count), spread_recv.at[piece]
            ).start()

    def forward(piece):
        if RELAYS == 0:
            return
        for half, sign, low, count in halves(piece):
            arrived = relay[piece].at[half]
            pltpu.make_async_copy(arrived, arrived, relay_recv.at[piece, half]).wait()
            for j, (_, (vx, vy), (fx, fy)) in enumerate(routes(sign)[1]):
                pltpu.make_async_remote_copy(
                    src_ref=relay[piece].at[half, j],
                    dst_ref=place(piece, shifted(x, -vx, NX), shifted(y, -vy, NY), low, count),
                    send_sem=relay_send.at[piece],
                    recv_sem=spread_recv.at[piece],
                    device_id=device(shifted(x, fx, NX), shifted(y, fy, NY), z, c),
                    device_id_type=MESH,
                ).start()

    def order_copy(dy):
        return pltpu.make_async_remote_copy(
            src_ref=orders_own,
            dst_ref=orders.at[y],
            send_sem=order_send.at[dy],
            recv_sem=order_sem.at[0],
            device_id=device(x, shifted(y, dy, NY), z, c),
            device_id_type=MESH,
        )

    def make_pick():
        pltpu.make_async_copy(orders, orders, order_sem.at[0]).wait()
        line = lax.broadcasted_iota(jnp.int32, (SECTORS_HERE, targets), 0)
        blocks = []
        for yy in range(NY):
            for xx in range(NX):
                for group in range(GROUPS_HERE):
                    wanted = orders[yy, group : group + 1, :]
                    first = (xx * NZ + z) * SECTORS_HERE
                    blocks.append(jnp.where(wanted == line + first, 1.0, 0.0))
        table = jnp.concatenate(blocks, 0).T
        half = targets // NC
        for xh in range(NC):
            blocks = []
            for zz in range(NZ):
                for part in range(X_PART):
                    low = ((xh * X_PART + part) * NZ + zz) * SECTORS_HERE
                    blocks.append(table[low : low + SECTORS_HERE])
            start = pl.multiple_of((1 - c if xh == 0 else c) * half, half)
            pick[pl.ds(start, half), :] = jnp.concatenate(blocks, 0).astype(jnp.bfloat16)

    def gather(piece):
        pltpu.make_async_copy(got[piece], got[piece], spread_recv.at[piece]).wait()
        half = targets // NC

        def some(step, _):
            for inner in range(4):
                m = step * 8 + inner * 2
                both = jnp.concatenate([got[piece][m], got[piece][m + 1]], 1)
                value = jnp.dot(pick[...], both, preferred_element_type=jnp.float32)
                for part, to in ((0, give[piece]), (1, own[piece])):
                    for zz in range(NZ):
                        low = part * half + zz * TILE
                        for next_m in range(2):
                            to[zz, m + next_m] = value[
                                low : low + TILE, next_m * lanes : (next_m + 1) * lanes
                            ].astype(to.dtype)
            return 0

        lax.fori_loop(0, piece_rows[piece] // 8, some, 0)
        core_copy(piece).start()

    def core_copy(piece):
        return pltpu.make_async_remote_copy(
            src_ref=give[piece],
            dst_ref=take[piece],
            send_sem=core_send.at[piece],
            recv_sem=core_recv.at[piece],
            device_id=device(x, y, z, 1 - c),
            device_id_type=MESH,
        )

    def held(piece, zd, low, count):
        at = slice(low, low + count)
        return own[piece][zd, at] + take[piece][zd, at].astype(jnp.float32)

    def z_buffers(piece, way):
        return (up_out[piece], up_in[piece]) if way > 0 else (down_out[piece], down_in[piece])

    def z_copy(piece, step, way):
        source, target = z_buffers(piece, way)
        out_sem, in_sem = (up_send, up_recv) if way > 0 else (down_send, down_recv)
        at = (step,)
        if step == 0:
            _, _, low, count = halves(piece)[0 if way > 0 else 1]
            at = (step, slice(low, low + count))
        return pltpu.make_async_remote_copy(
            src_ref=source.at[at],
            dst_ref=target.at[at],
            send_sem=out_sem.at[piece, step],
            recv_sem=in_sem.at[piece, step],
            device_id=device(x, y, shifted(z, way, NZ), c),
            device_id_type=MESH,
        )

    def carried(step, way, sign):
        return step > 0 or way == sign

    def chain(piece, step):
        if step >= STEPS:
            return
        if step == 0:
            core_copy(piece).wait_recv()
        for way in (1, -1):
            source, target = z_buffers(piece, way)
            if step > 0:
                z_copy(piece, step - 1, way).wait_recv()
            zd = shifted(z, way * (STEPS - step), NZ)
            for _, sign, low, count in halves(piece):
                if carried(step, way, sign):
                    at = slice(low, low + count)
                    value = held(piece, zd, low, count)
                    if step > 0 and carried(step - 1, way, sign):
                        value = value + target[step - 1, at].astype(jnp.float32)
                    source[step, at] = value.astype(jnp.bfloat16)
            z_copy(piece, step, way).start()

    def final_copies(piece, part):
        xd = c * X_PART + part
        spot_there = final[piece].at[lax.rem(x, X_PART)]
        there = dict(
            src_ref=done[piece].at[part],
            dst_ref=spot_there,
            send_sem=final_send.at[piece, part],
            recv_sem=final_recv.at[piece],
            device_id=device(xd, y, z, lax.div(x, X_PART)),
            device_id_type=MESH,
        )
        here = (done[piece].at[part], spot_there, final_recv.at[piece])
        return xd, there, here

    def finish(piece):
        last = STEPS - 1
        for way in (1, -1):
            z_copy(piece, last, way).wait_recv()
        for _, sign, low, count in halves(piece):
            value = held(piece, z, low, count)
            for way in (1, -1):
                if carried(last, way, sign):
                    value = value + z_buffers(piece, way)[1][last, low : low + count].astype(jnp.float32)
            for part in range(X_PART):
                at = slice(part * SECTORS_HERE, (part + 1) * SECTORS_HERE)
                done[piece][part, low // 2 : (low + count) // 2] = (
                    value[:, at, :].reshape(count // 2, TILE, lanes).astype(jnp.bfloat16)
                )
        for part in range(X_PART):
            xd, there, here = final_copies(piece, part)

            @pl.when(xd != x)
            def _():
                pltpu.make_async_remote_copy(**there).start()

            @pl.when(xd == x)
            def _():
                pltpu.make_async_copy(*here).start()

    def put(piece):
        pltpu.make_async_copy(final[piece], final[piece], final_recv.at[piece]).wait()
        chunk, count = PIECES[piece][0], piece_rows[piece]
        total = X_PART * count * SECTORS_HERE
        row = lax.broadcasted_iota(jnp.int32, (total, total), 0)
        column = lax.broadcasted_iota(jnp.int32, (total, total), 1)
        sector = column & (SECTORS_HERE - 1)
        line = lax.shift_right_logical(column, 3)
        value = jnp.dot(
            ones_where(row == sector * (X_PART * count) + line),
            final[piece][...].reshape(total, lanes),
            preferred_element_type=jnp.float32,
        )
        for sector in range(SECTORS_HERE):
            for part in range(X_PART):
                low = part * rows + first_row[piece]
                start = (sector * X_PART + part) * count
                m = term * (X_PART * rows) + low + lax.broadcasted_iota(jnp.int32, (count, lanes), 0)
                i = chunk * lanes + lax.broadcasted_iota(jnp.int32, (count, lanes), 1)
                keep = (i < widths[0, sector]) & (m < widths[1, sector])
                out[sector, low : low + count, chunk * lanes : (chunk + 1) * lanes] = jnp.where(
                    keep, value[start : start + count], 0.0
                )

    first_parts()
    first_images(y_order[:1], True)
    pl.semaphore_wait(barrier, len(others))
    spread(0, y_order[:1])
    first_images(y_order[1:], False)
    spread(0, y_order[1:])
    for dy in range(1, NY):
        order_copy(dy).start()
    pltpu.make_async_copy(orders_own, orders.at[y], order_sem.at[0]).start()
    later_parts()
    forward(0)
    later_images()
    for part in range(2):
        rings = y_order[part * NY // 2 : (part + 1) * NY // 2]
        for dy in rings:
            later_turn(dy)
        spread(1, rings)
    make_pick()
    gather(0)
    forward(1)
    spread(2)
    chain(0, 0)
    spread(3)
    chain(0, 1)
    chain(0, 2)
    gather(1)
    chain(0, 3)
    forward(2)
    chain(1, 0)
    finish(0)
    chain(1, 1)
    forward(3)
    put(0)
    chain(1, 2)
    gather(2)
    chain(1, 3)
    chain(2, 0)
    gather(3)
    finish(1)
    chain(3, 0)
    chain(2, 1)
    chain(3, 1)
    put(1)
    chain(2, 2)
    chain(3, 2)
    chain(2, 3)
    chain(3, 3)
    finish(2)
    finish(3)
    put(2)
    put(3)

    for dy in range(1, NY):
        order_copy(dy).wait_send()
    for piece in pieces:
        sent = sends[PIECES[piece][0]].at[0 : (SLOTS - 1) * piece_rows[piece]]
        pltpu.make_async_copy(sent, sent, spread_send.at[piece]).wait()
        if RELAYS:
            pltpu.make_async_copy(relay[piece], relay[piece], relay_send.at[piece]).wait()
        core_copy(piece).wait_send()
        for step in range(STEPS):
            for way in (1, -1):
                z_copy(piece, step, way).wait_send()
        for part in range(X_PART):
            xd, there, _ = final_copies(piece, part)

            @pl.when(xd != x)
            def _():
                pltpu.make_async_remote_copy(**there).wait_send()


def shards(psi, left_ops, right_ops, pair_src, widths):
    size = psi.shape[1]
    targets = pair_src.shape[1]
    rows, lanes = size // SLOTS, size // CHUNKS
    bf, count = jnp.bfloat16, len(PIECES)
    tile = (TILE, lanes)
    scratch = [
        pltpu.VMEM(psi.shape, bf),
        pltpu.VMEM(left_ops.shape, bf),
        pltpu.VMEM(right_ops.shape, bf),
        pltpu.VMEM((8, targets), jnp.int32),
        pltpu.VMEM((NY, 8, targets), jnp.int32),
        pltpu.VMEM((SECTORS_HERE, GROUPS_HERE * (size - lanes), size), bf),
        pltpu.VMEM((TILE, size, size - lanes), bf),
        pltpu.VMEM((TILE * TILE, TILE * TILE), bf),
        pltpu.VMEM((targets, SOURCES), bf),
        *[pltpu.VMEM((size,) + tile, bf) for _ in range(CHUNKS)],
    ]
    for _, _, thirds in PIECES:
        here = rows * thirds // 3
        ring = pltpu.VMEM((STEPS, here) + tile, bf)
        scratch += [
            pltpu.VMEM((here, SOURCES, lanes), bf),
            pltpu.VMEM((2, max(RELAYS, 1), here // 2) + tile, bf),
            pltpu.VMEM((NZ, here) + tile, bf),
            pltpu.VMEM((NZ, here) + tile, bf),
            pltpu.VMEM((NZ, here) + tile, jnp.float32),
            ring, ring, ring, ring,
            pltpu.VMEM((X_PART, here // 2) + tile, bf),
            pltpu.VMEM((X_PART, here // 2) + tile, bf),
        ]
    dma = pltpu.SemaphoreType.DMA
    scratch += [
        dma((4, SECTORS_HERE)), dma((1,)), dma((NY,)), dma((count,)), dma((count,)),
        dma((count, 2)), dma((count,)), dma((count,)), dma((count,)),
        dma((count, STEPS)), dma((count, STEPS)), dma((count, STEPS)), dma((count, STEPS)),
        dma((count, X_PART)), dma((count,)),
    ]
    summed = pl.pallas_call(
        kernel,
        out_shape=jax.ShapeDtypeStruct((SECTORS_HERE, X_PART * rows, size), jnp.float32),
        in_specs=[
            pl.BlockSpec(memory_space=pltpu.VMEM),
            pl.BlockSpec(memory_space=pltpu.SMEM),
            pl.BlockSpec(memory_space=pl.ANY),
            pl.BlockSpec(memory_space=pl.ANY),
            pl.BlockSpec(memory_space=pl.ANY),
        ],
        out_specs=pl.BlockSpec(memory_space=pltpu.VMEM),
        scratch_shapes=scratch,
        compiler_params=pltpu.CompilerParams(
            collective_id=0, has_side_effects=True, vmem_limit_bytes=56 * 1024 * 1024
        ),
        cost_estimate=pl.CostEstimate(
            flops=64 * size**3, bytes_accessed=40 * size * size * 2, transcendentals=0
        ),
    )(pair_src, widths, psi, left_ops, right_ops)

    return jnp.swapaxes(summed, 1, 2)


def solution(mesh):
    return jax.shard_map(
        shards,
        mesh=mesh,
        in_specs=(
            P("sec", None, None),
            P("term", "sec", None, None),
            P("term", "sec", None, None),
            P("term", None),
            P(None, "sec"),
        ),
        out_specs=P("sec", None, "term"),
        check_vma=False,
    )
```

```python
import jax
import jax.numpy as jnp
from jax import lax
from jax.experimental import pallas as pl
from jax.experimental.pallas import tpu as pltpu
from jax.sharding import PartitionSpec as P

NX, NY, NZ, NC = 4, 4, 8, 2
CHUNKS = 3
PIECES = ((0, 0, 3), (1, 0, 3), (2, 0, 2), (2, 2, 1))
SLOTS = NX * NY
GROUPS_HERE = 2
SECTORS_HERE = 8
TILE = GROUPS_HERE * SECTORS_HERE
SOURCES = SLOTS * TILE
X_PART = NX // NC
STEPS = NZ // 2
MESH = pl.DeviceIdType.MESH
BUFFERS = 11


def routes(sign):
    direct, relayed = [], []
    for dx in range(NX):
        for dy in range(NY):
            far_x, far_y = NX > 2 and dx == NX // 2, NY > 2 and dy == NY // 2
            if far_x or far_y:
                via = (sign if far_x else 0, sign if far_y else 0)
                relayed.append(((dx, dy), via, (dx - via[0], dy - via[1])))
            elif (dx, dy) != (0, 0):
                direct.append((dx, dy))
    return direct, relayed


RELAYS = len(routes(1)[1])


def device(x, y, z, c):
    return (x * NZ + z, y * NC + c)


def ones_where(condition):
    return jnp.where(condition, 1.0, 0.0).astype(jnp.bfloat16)


def tile_at(index):
    return pl.ds(pl.multiple_of(index * TILE, TILE), TILE)


def kernel(pair_src, widths, psi, left, right, out, *rest):
    psi_v, left_v, right_v, orders_own, orders, parts, image, swap, pick, *rest = rest
    sends, rest = rest[:CHUNKS], rest[CHUNKS:]
    buffers = [rest[i * BUFFERS : (i + 1) * BUFFERS] for i in range(len(PIECES))]
    (
        load_sem, order_sem, order_send, spread_send, spread_recv, relay_recv, relay_send, core_send, core_recv,
        up_send, up_recv, down_send, down_recv, final_send, final_recv,
    ) = rest[len(PIECES) * BUFFERS :]
    got, relay, give, take, own, up_out, up_in, down_out, down_in, done, final = zip(*buffers)
    sec, term = lax.axis_index("sec"), lax.axis_index("term")
    x, z = lax.div(sec, NZ), lax.rem(sec, NZ)
    y, c = lax.div(term, NC), lax.rem(term, NC)
    size = psi_v.shape[-1]
    rows = size // SLOTS
    lanes = size // CHUNKS
    targets = pair_src.shape[1]
    pieces = range(len(PIECES))
    y_order = sorted(range(NY), key=lambda dy: -min(dy, NY - dy))
    first_row = [rows * at // 3 for _, at, _ in PIECES]
    piece_rows = [rows * count // 3 for _, _, count in PIECES]

    def shifted(value, by, count):
        return lax.rem(value + (by % count), count)

    barrier = pltpu.get_barrier_semaphore()
    others = [
        device(shifted(x, dx, NX), shifted(y, dy, NY), z, c)
        for dx in range(NX)
        for dy in range(NY)
        if (dx, dy) != (0, 0)
    ]
    others += [device(shifted(x, dx, NX), y, z, 1 - c) for dx in range(NX)]
    others += [device(x, y, shifted(z, 1, NZ), c), device(x, y, shifted(z, -1, NZ), c)]
    for other in others:
        pl.semaphore_signal(barrier, inc=1, device_id=other, device_id_type=MESH)

    def loads(k):
        return (
            pltpu.make_async_copy(psi.at[k], psi_v.at[k], load_sem.at[0, k]),
            pltpu.make_async_copy(
                left.at[:, k, 0:lanes], left_v.at[:, k, 0:lanes], load_sem.at[1, k]
            ),
            pltpu.make_async_copy(right.at[:, k], right_v.at[:, k], load_sem.at[2, k]),
            pltpu.make_async_copy(
                left.at[:, k, lanes:size], left_v.at[:, k, lanes:size], load_sem.at[3, k]
            ),
        )

    for which in ((0, 1), (2,), (3,)):
        for k in range(SECTORS_HERE):
            for copy in which:
                loads(k)[copy].start()

    row = lax.broadcasted_iota(jnp.int32, swap.shape, 0)
    column = lax.broadcasted_iota(jnp.int32, swap.shape, 1)
    swap[...] = ones_where(row == (column & (TILE - 1)) * TILE + lax.shift_right_logical(column, 4))
    orders_own[...] = jnp.concatenate([pair_src[...], jnp.zeros((6, targets), jnp.int32)], 0)

    def image_of(right_block, part):
        return lax.dot_general(
            right_block, part, (((1,), (1,)), ((), ())), preferred_element_type=jnp.float32
        ).astype(jnp.bfloat16)

    def turned(block):
        return jnp.dot(swap[...], block, preferred_element_type=jnp.float32).astype(jnp.bfloat16)

    def each_sector(body):
        def some(step, _):
            for inner in range(2):
                body(step * 2 + inner)
            return 0

        lax.fori_loop(0, SECTORS_HERE // 2, some, 0)

    def first_parts():
        def one(k):
            for copy in loads(k)[:2]:
                copy.wait()
            keep = (lax.broadcasted_iota(jnp.int32, (size, size), 0) < widths[0, k]) & (
                lax.broadcasted_iota(jnp.int32, (size, size), 1) < widths[1, k]
            )
            masked = jnp.where(keep, psi_v[k].astype(jnp.float32), 0.0).astype(jnp.bfloat16)
            psi_v[k] = masked
            here = left_v[:, k, 0:lanes, :].reshape(GROUPS_HERE * lanes, size)
            parts[k, 0 : GROUPS_HERE * lanes] = jnp.dot(
                here, masked, preferred_element_type=jnp.float32
            ).astype(jnp.bfloat16)

        each_sector(one)

    def first_images(rings, first):
        count = size // NY
        starts = [pl.multiple_of(shifted(y, dy, NY) * count, 2 * TILE) for dy in rings]

        def one(k):
            if first:
                loads(k)[2].wait()
            for group in range(GROUPS_HERE):
                chosen = jnp.concatenate([right_v[group, k, pl.ds(start, count), :] for start in starts], 0)
                image[group * SECTORS_HERE + k, 0 : count * len(starts), 0:lanes] = image_of(
                    chosen, parts[k, group * lanes : (group + 1) * lanes, :]
                )

        each_sector(one)
        for low in range(0, count * len(starts), 2 * TILE):
            both = turned(
                jnp.concatenate(
                    [
                        image[:, at : at + TILE, 0:lanes].reshape(TILE * TILE, lanes)
                        for at in (low, low + TILE)
                    ],
                    1,
                )
            )
            for part in range(2):
                at = starts[low // count] + low % count + part * TILE
                sends[0][pl.ds(at, TILE)] = both[:, part * lanes : (part + 1) * lanes].reshape(
                    TILE, TILE, lanes
                )

    later = size - lanes

    def later_parts():
        def one(k):
            loads(k)[3].wait()
            here = left_v[:, k, lanes:, :].reshape(GROUPS_HERE * later, size)
            parts[k] = jnp.dot(here, psi_v[k], preferred_element_type=jnp.float32).astype(jnp.bfloat16)

        each_sector(one)

    def later_images():
        def one(k):
            for group in range(GROUPS_HERE):
                image[group * SECTORS_HERE + k] = image_of(
                    right_v[group, k], parts[k, group * later : (group + 1) * later, :]
                )

        each_sector(one)

        def some(step, _):
            for inner in range(4):
                at = pl.multiple_of((step * 4 + inner) * TILE, TILE)
                value = turned(image[:, pl.ds(at, TILE), :].reshape(TILE * TILE, later))
                for chunk in range(1, CHUNKS):
                    sends[chunk][pl.ds(at, TILE)] = value[
                        :, (chunk - 1) * lanes : chunk * lanes
                    ].reshape(TILE, TILE, lanes)
            return 0

        lax.fori_loop(0, size // (4 * TILE), some, 0)

    def halves(piece):
        count = piece_rows[piece] // 2
        return ((0, 1, 0, count), (1, -1, count, count))

    def block_for(piece, x_to, y_to, low, count):
        start = (y_to * NX + x_to) * rows + first_row[piece] + low
        return sends[PIECES[piece][0]].at[pl.ds(start, count)]

    def place(piece, x_from, y_from, low, count):
        return got[piece].at[low : low + count, tile_at(y_from * NX + x_from)]

    def spread(piece, rings=range(NY)):
        for j in range(RELAYS):
            for half, sign, low, count in halves(piece):
                (dx, dy), (vx, vy), _ = routes(sign)[1][j]
                if dy in rings:
                    pltpu.make_async_remote_copy(
                        src_ref=block_for(piece, shifted(x, dx, NX), shifted(y, dy, NY), low, count),
                        dst_ref=relay[piece].at[half, j],
                        send_sem=spread_send.at[piece],
                        recv_sem=relay_recv.at[piece, half],
                        device_id=device(shifted(x, vx, NX), shifted(y, vy, NY), z, c),
                        device_id_type=MESH,
                    ).start()
        count = piece_rows[piece]
        for dx, dy in routes(1)[0]:
            if dy in rings:
                xd, yd = shifted(x, dx, NX), shifted(y, dy, NY)
                pltpu.make_async_remote_copy(
                    src_ref=block_for(piece, xd, yd, 0, count),
                    dst_ref=place(piece, x, y, 0, count),
                    send_sem=spread_send.at[piece],
                    recv_sem=spread_recv.at[piece],
                    device_id=device(xd, yd, z, c),
                    device_id_type=MESH,
                ).start()
        if 0 in rings:
            pltpu.make_async_copy(
                block_for(piece, x, y, 0, count), place(piece, x, y, 0, count), spread_recv.at[piece]
            ).start()

    def forward(piece):
        if RELAYS == 0:
            return
        for half in range(2):
            arrived = relay[piece].at[half]
            pltpu.make_async_copy(arrived, arrived, relay_recv.at[piece, half]).wait()
        for j in range(RELAYS):
            for half, sign, low, count in halves(piece):
                _, (vx, vy), (fx, fy) = routes(sign)[1][j]
                pltpu.make_async_remote_copy(
                    src_ref=relay[piece].at[half, j],
                    dst_ref=place(piece, shifted(x, -vx, NX), shifted(y, -vy, NY), low, count),
                    send_sem=relay_send.at[piece],
                    recv_sem=spread_recv.at[piece],
                    device_id=device(shifted(x, fx, NX), shifted(y, fy, NY), z, c),
                    device_id_type=MESH,
                ).start()

    def order_copy(dy):
        return pltpu.make_async_remote_copy(
            src_ref=orders_own,
            dst_ref=orders.at[y],
            send_sem=order_send.at[dy],
            recv_sem=order_sem.at[0],
            device_id=device(x, shifted(y, dy, NY), z, c),
            device_id_type=MESH,
        )

    def make_pick():
        pltpu.make_async_copy(orders, orders, order_sem.at[0]).wait()
        line = lax.broadcasted_iota(jnp.int32, (SECTORS_HERE, targets), 0)
        blocks = []
        for yy in range(NY):
            for xx in range(NX):
                for group in range(GROUPS_HERE):
                    wanted = orders[yy, group : group + 1, :]
                    first = (xx * NZ + z) * SECTORS_HERE
                    blocks.append(jnp.where(wanted == line + first, 1.0, 0.0))
        table = jnp.concatenate(blocks, 0).T
        half = targets // NC
        for xh in range(NC):
            blocks = []
            for zz in range(NZ):
                for part in range(X_PART):
                    low = ((xh * X_PART + part) * NZ + zz) * SECTORS_HERE
                    blocks.append(table[low : low + SECTORS_HERE])
            start = pl.multiple_of((1 - c if xh == 0 else c) * half, half)
            pick[pl.ds(start, half), :] = jnp.concatenate(blocks, 0).astype(jnp.bfloat16)

    def gather(piece):
        pltpu.make_async_copy(got[piece], got[piece], spread_recv.at[piece]).wait()
        half = targets // NC

        def some(step, _):
            for inner in range(4):
                m = step * 8 + inner * 2
                both = jnp.concatenate([got[piece][m], got[piece][m + 1]], 1)
                value = jnp.dot(pick[...], both, preferred_element_type=jnp.float32)
                for part, to in ((0, give[piece]), (1, own[piece])):
                    for zz in range(NZ):
                        low = part * half + zz * TILE
                        for next_m in range(2):
                            to[zz, m + next_m] = value[
                                low : low + TILE, next_m * lanes : (next_m + 1) * lanes
                            ].astype(to.dtype)
            return 0

        lax.fori_loop(0, piece_rows[piece] // 8, some, 0)
        core_copy(piece).start()

    def core_copy(piece):
        return pltpu.make_async_remote_copy(
            src_ref=give[piece],
            dst_ref=take[piece],
            send_sem=core_send.at[piece],
            recv_sem=core_recv.at[piece],
            device_id=device(x, y, z, 1 - c),
            device_id_type=MESH,
        )

    def held(piece, zd, low, count):
        at = slice(low, low + count)
        return own[piece][zd, at] + take[piece][zd, at].astype(jnp.float32)

    def z_buffers(piece, way):
        return (up_out[piece], up_in[piece]) if way > 0 else (down_out[piece], down_in[piece])

    def z_copy(piece, step, way):
        source, target = z_buffers(piece, way)
        out_sem, in_sem = (up_send, up_recv) if way > 0 else (down_send, down_recv)
        at = (step,)
        if step == 0:
            _, _, low, count = halves(piece)[0 if way > 0 else 1]
            at = (step, slice(low, low + count))
        return pltpu.make_async_remote_copy(
            src_ref=source.at[at],
            dst_ref=target.at[at],
            send_sem=out_sem.at[piece, step],
            recv_sem=in_sem.at[piece, step],
            device_id=device(x, y, shifted(z, way, NZ), c),
            device_id_type=MESH,
        )

    def carried(step, way, sign):
        return step > 0 or way == sign

    def chain(piece, step):
        if step >= STEPS:
            return
        if step == 0:
            core_copy(piece).wait_recv()
        for way in (1, -1):
            source, target = z_buffers(piece, way)
            if step > 0:
                z_copy(piece, step - 1, way).wait_recv()
            zd = shifted(z, way * (STEPS - step), NZ)
            for _, sign, low, count in halves(piece):
                if carried(step, way, sign):
                    at = slice(low, low + count)
                    value = held(piece, zd, low, count)
                    if step > 0 and carried(step - 1, way, sign):
                        value = value + target[step - 1, at].astype(jnp.float32)
                    source[step, at] = value.astype(jnp.bfloat16)
            z_copy(piece, step, way).start()

    def final_copies(piece, part):
        xd = c * X_PART + part
        spot_there = final[piece].at[lax.rem(x, X_PART)]
        there = dict(
            src_ref=done[piece].at[part],
            dst_ref=spot_there,
            send_sem=final_send.at[piece, part],
            recv_sem=final_recv.at[piece],
            device_id=device(xd, y, z, lax.div(x, X_PART)),
            device_id_type=MESH,
        )
        here = (done[piece].at[part], spot_there, final_recv.at[piece])
        return xd, there, here

    def finish(piece):
        last = STEPS - 1
        for way in (1, -1):
            z_copy(piece, last, way).wait_recv()
        for _, sign, low, count in halves(piece):
            value = held(piece, z, low, count)
            for way in (1, -1):
                if carried(last, way, sign):
                    value = value + z_buffers(piece, way)[1][last, low : low + count].astype(jnp.float32)
            for part in range(X_PART):
                at = slice(part * SECTORS_HERE, (part + 1) * SECTORS_HERE)
                done[piece][part, low // 2 : (low + count) // 2] = (
                    value[:, at, :].reshape(count // 2, TILE, lanes).astype(jnp.bfloat16)
                )
        for part in range(X_PART):
            xd, there, here = final_copies(piece, part)

            @pl.when(xd != x)
            def _():
                pltpu.make_async_remote_copy(**there).start()

            @pl.when(xd == x)
            def _():
                pltpu.make_async_copy(*here).start()

    def put(piece):
        pltpu.make_async_copy(final[piece], final[piece], final_recv.at[piece]).wait()
        chunk, count = PIECES[piece][0], piece_rows[piece]
        total = X_PART * count * SECTORS_HERE
        row = lax.broadcasted_iota(jnp.int32, (total, total), 0)
        column = lax.broadcasted_iota(jnp.int32, (total, total), 1)
        sector = column & (SECTORS_HERE - 1)
        line = lax.shift_right_logical(column, 3)
        value = jnp.dot(
            ones_where(row == sector * (X_PART * count) + line),
            final[piece][...].reshape(total, lanes),
            preferred_element_type=jnp.float32,
        )
        for sector in range(SECTORS_HERE):
            for part in range(X_PART):
                low = part * rows + first_row[piece]
                start = (sector * X_PART + part) * count
                m = term * (X_PART * rows) + low + lax.broadcasted_iota(jnp.int32, (count, lanes), 0)
                i = chunk * lanes + lax.broadcasted_iota(jnp.int32, (count, lanes), 1)
                keep = (i < widths[0, sector]) & (m < widths[1, sector])
                out[sector, low : low + count, chunk * lanes : (chunk + 1) * lanes] = jnp.where(
                    keep, value[start : start + count], 0.0
                )

    first_parts()
    first_images(y_order[:1], True)
    pl.semaphore_wait(barrier, len(others))
    spread(0, y_order[:1])
    first_images(y_order[1:], False)
    spread(0, y_order[1:])
    for dy in range(1, NY):
        order_copy(dy).start()
    pltpu.make_async_copy(orders_own, orders.at[y], order_sem.at[0]).start()
    later_parts()
    forward(0)
    later_images()
    spread(1)
    make_pick()
    gather(0)
    forward(1)
    spread(2)
    chain(0, 0)
    spread(3)
    chain(0, 1)
    chain(0, 2)
    gather(1)
    chain(0, 3)
    forward(2)
    chain(1, 0)
    finish(0)
    chain(1, 1)
    forward(3)
    put(0)
    chain(1, 2)
    gather(2)
    chain(1, 3)
    chain(2, 0)
    gather(3)
    finish(1)
    chain(3, 0)
    chain(2, 1)
    chain(3, 1)
    put(1)
    chain(2, 2)
    chain(3, 2)
    chain(2, 3)
    chain(3, 3)
    finish(2)
    finish(3)
    put(2)
    put(3)

    for dy in range(1, NY):
        order_copy(dy).wait_send()
    for piece in pieces:
        sent = sends[PIECES[piece][0]].at[0 : (SLOTS - 1) * piece_rows[piece]]
        pltpu.make_async_copy(sent, sent, spread_send.at[piece]).wait()
        if RELAYS:
            pltpu.make_async_copy(relay[piece], relay[piece], relay_send.at[piece]).wait()
        core_copy(piece).wait_send()
        for step in range(STEPS):
            for way in (1, -1):
                z_copy(piece, step, way).wait_send()
        for part in range(X_PART):
            xd, there, _ = final_copies(piece, part)

            @pl.when(xd != x)
            def _():
                pltpu.make_async_remote_copy(**there).wait_send()


def shards(psi, left_ops, right_ops, pair_src, widths):
    size = psi.shape[1]
    targets = pair_src.shape[1]
    rows, lanes = size // SLOTS, size // CHUNKS
    bf, count = jnp.bfloat16, len(PIECES)
    tile = (TILE, lanes)
    scratch = [
        pltpu.VMEM(psi.shape, bf),
        pltpu.VMEM(left_ops.shape, bf),
        pltpu.VMEM(right_ops.shape, bf),
        pltpu.VMEM((8, targets), jnp.int32),
        pltpu.VMEM((NY, 8, targets), jnp.int32),
        pltpu.VMEM((SECTORS_HERE, GROUPS_HERE * (size - lanes), size), bf),
        pltpu.VMEM((TILE, size, size - lanes), bf),
        pltpu.VMEM((TILE * TILE, TILE * TILE), bf),
        pltpu.VMEM((targets, SOURCES), bf),
        *[pltpu.VMEM((size,) + tile, bf) for _ in range(CHUNKS)],
    ]
    for _, _, thirds in PIECES:
        here = rows * thirds // 3
        ring = pltpu.VMEM((STEPS, here) + tile, bf)
        scratch += [
            pltpu.VMEM((here, SOURCES, lanes), bf),
            pltpu.VMEM((2, max(RELAYS, 1), here // 2) + tile, bf),
            pltpu.VMEM((NZ, here) + tile, bf),
            pltpu.VMEM((NZ, here) + tile, bf),
            pltpu.VMEM((NZ, here) + tile, jnp.float32),
            ring, ring, ring, ring,
            pltpu.VMEM((X_PART, here // 2) + tile, bf),
            pltpu.VMEM((X_PART, here // 2) + tile, bf),
        ]
    dma = pltpu.SemaphoreType.DMA
    scratch += [
        dma((4, SECTORS_HERE)), dma((1,)), dma((NY,)), dma((count,)), dma((count,)),
        dma((count, 2)), dma((count,)), dma((count,)), dma((count,)),
        dma((count, STEPS)), dma((count, STEPS)), dma((count, STEPS)), dma((count, STEPS)),
        dma((count, X_PART)), dma((count,)),
    ]
    summed = pl.pallas_call(
        kernel,
        out_shape=jax.ShapeDtypeStruct((SECTORS_HERE, X_PART * rows, size), jnp.float32),
        in_specs=[
            pl.BlockSpec(memory_space=pltpu.VMEM),
            pl.BlockSpec(memory_space=pltpu.SMEM),
            pl.BlockSpec(memory_space=pl.ANY),
            pl.BlockSpec(memory_space=pl.ANY),
            pl.BlockSpec(memory_space=pl.ANY),
        ],
        out_specs=pl.BlockSpec(memory_space=pltpu.VMEM),
        scratch_shapes=scratch,
        compiler_params=pltpu.CompilerParams(
            collective_id=0, has_side_effects=True, vmem_limit_bytes=56 * 1024 * 1024
        ),
        cost_estimate=pl.CostEstimate(
            flops=64 * size**3, bytes_accessed=40 * size * size * 2, transcendentals=0
        ),
    )(pair_src, widths, psi, left_ops, right_ops)

    return jnp.swapaxes(summed, 1, 2)


def solution(mesh):
    return jax.shard_map(
        shards,
        mesh=mesh,
        in_specs=(
            P("sec", None, None),
            P("term", "sec", None, None),
            P("term", "sec", None, None),
            P("term", None),
            P(None, "sec"),
        ),
        out_specs=P("sec", None, "term"),
        check_vma=False,
    )
```
